32 devices in a mesh: fsdp: 4 (over z), ctx: 4 (over y, core), tp: 2 (over x).
Axes of the slice: x: 2, y: 2, z: 4, core: 2. Of those that a mesh axis runs over, the one named last changes fastest.
Arguments:
- tokens: bfloat16 [4, 2048, 2048], P('fsdp', ('ctx', 'tp')), may hold values from -6 to 6
- positions: int32 [2048], replicated, may hold values from 0 to 2047, as said below
- cotangent: bfloat16 [4, 2048, 2048], P('fsdp', ('ctx', 'tp')), may hold values from -6 to 6
- norm_gain: bfloat16 [2048], replicated, may hold values from 0.5 to 1.5
- norm_bias: bfloat16 [2048], replicated, may hold values from -1.75 to 1.75
- qkv_weight: bfloat16 [2048, 3, 2048], P(('fsdp', 'ctx'), None, 'tp'), may hold values from -0.125 to 0.125
- qkv_bias: bfloat16 [3, 2048], P(None, 'tp'), may hold values from -1.75 to 1.75
- out_weight: bfloat16 [2048, 2048], P('tp', ('fsdp', 'ctx')), may hold values from -3 to 3
- out_bias: bfloat16 [2048], replicated, may hold values from -1.75 to 1.75
- up_weight: bfloat16 [2048, 8192], P(('fsdp', 'ctx'), 'tp'), may hold values from -0.125 to 0.125
- up_bias: bfloat16 [8192], P('tp'), may hold values from -1.75 to 1.75
- down_weight: bfloat16 [8192, 2048], P('tp', ('fsdp', 'ctx')), may hold values from -0.0625 to 0.0625
- down_bias: bfloat16 [2048], replicated, may hold values from -1.75 to 1.75
Outputs:
- layer_output: bfloat16 [4, 2048, 2048], P('fsdp', ('ctx', 'tp'))
- tokens_grad: float32 [4, 2048, 2048], P('fsdp', ('ctx', 'tp'))
- norm_gain_grad: float32 [2048], replicated
- norm_bias_grad: float32 [2048], replicated
- qkv_weight_grad: float32 [2048, 3, 2048], P(('fsdp', 'ctx'), None, 'tp')
- qkv_bias_grad: float32 [3, 2048], P(None, 'tp')
- out_weight_grad: float32 [2048, 2048], P('tp', ('fsdp', 'ctx'))
- out_bias_grad: float32 [2048], replicated
- up_weight_grad: float32 [2048, 8192], P(('fsdp', 'ctx'), 'tp')
- up_bias_grad: float32 [8192], P('tp')
- down_weight_grad: float32 [8192, 2048], P('tp', ('fsdp', 'ctx'))
- down_bias_grad: float32 [2048], replicated
The draws below stay inside these ranges and needn't reach their ends.
Inputs may be any that keep to these rules, and one draw needn't show every extreme that they name: The sequence is cut into 8 groups of 256 consecutive positions; each block of 512 stored rows holds group k and group 2 * 4 - 1 - k, each in ascending order; which k lies in which block and the two groups' order vary with the seed; every position appears once.
All inputs are finite; a program needn't handle non-finite values.
Results may differ from the reference program's by a relative error of at most 0.014.
Values may be sent and summed in bfloat16 or wider, within the bound.
No kernel may reach another device: no remote copies, remote signals or barrier semaphores. Data moves between devices by JAX's collectives and lax.ppermute only.
A program may use at most 256 MiB of HBM per device.

```python
import jax
import jax.numpy as jnp
from jax import lax

D = 2048
HEADS = 32
HEAD_DIM = 64
ROT = 32
FF = 8192
SEQ_LEN = 2048
SEQS = 4
GROUP = 256


def draw_positions(key, part):
    key = jax.random.fold_in(key, 7)
    pair_count = SEQ_LEN // (2 * GROUP)
    order = jax.random.permutation(jax.random.fold_in(key, 1), pair_count)
    flips = jax.random.randint(jax.random.fold_in(key, 2), (pair_count,), 0, 2)
    slots = jnp.arange(2 * pair_count)
    holder = slots // 2
    which_side = (slots % 2 + flips[holder]) % 2
    group_index = jnp.where(which_side == 0, order[holder], 2 * pair_count - 1 - order[holder])
    placed = group_index[:, None] * GROUP + jnp.arange(GROUP)[None, :]
    return placed.reshape(SEQ_LEN).astype(jnp.int32)


def block_scale(stream_key, dims, split, least, high):
    def one(axis_at, parts):
        steps = jax.random.uniform(jax.random.fold_in(jax.random.fold_in(stream_key, 6), axis_at), (parts,), jnp.float32, least / len(split), high / len(split))
        return jnp.repeat(jnp.exp(steps), dims[axis_at] // parts).reshape((-1,) + (1,) * (len(dims) - axis_at - 1))

    gain = one(*split[0])
    for cut in split[1:]:
        gain = gain * one(*cut)
    return gain


def gaussian(rng, dims, scale, bound, cuts=(), kind=jnp.bfloat16):
    level = block_scale(rng, dims, cuts, -0.22, 0.18) if cuts else 1.0
    entries = jax.random.normal(rng, dims, jnp.float32) * scale * level
    return jnp.minimum(jnp.maximum(entries, -bound), bound).astype(kind)


def setup_inputs(seed: int = 0) -> dict:
    arg_keys = jax.random.split(jax.random.key(seed), 14)
    tokens = gaussian(arg_keys[0], (SEQS, SEQ_LEN, D), 1.0, 6.0, ((0, 4), (1, 8)))
    positions = draw_positions(jax.random.fold_in(arg_keys[13], 71), 0)
    cotangent = gaussian(arg_keys[2], (SEQS, SEQ_LEN, D), 1.0, 6.0, ((0, 4), (1, 8)))
    norm_gain = jnp.clip(1.0 + 0.1 * jax.random.normal(arg_keys[3], (D,), jnp.float32), 0.5, 1.5).astype(jnp.bfloat16)
    norm_bias = gaussian(arg_keys[4], (D,), 0.3, 1.75)
    qkv_weight = gaussian(arg_keys[5], (D, 3, HEADS * HEAD_DIM), D ** -0.5, 0.125, ((0, 16), (2, 2)))
    qkv_bias = gaussian(arg_keys[6], (3, HEADS * HEAD_DIM), 0.3, 1.75, ((1, 2),))
    out_weight = gaussian(arg_keys[7], (HEADS * HEAD_DIM, D), (max(1, HEADS * HEAD_DIM * 4 // SEQ_LEN)) ** -0.5, 3.0, ((0, 2), (1, 16)))
    out_bias = gaussian(arg_keys[8], (D,), 0.3, 1.75)
    up_weight = gaussian(arg_keys[9], (D, FF), D ** -0.5, 0.125, ((0, 16), (1, 2)))
    up_bias = gaussian(arg_keys[10], (FF,), 0.3, 1.75, ((0, 2),))
    down_weight = gaussian(arg_keys[11], (FF, D), FF ** -0.5, 0.0625, ((0, 2), (1, 16)))
    down_bias = gaussian(arg_keys[12], (D,), 0.3, 1.75)
    return {"tokens": tokens, "positions": positions, "cotangent": cotangent, "norm_gain": norm_gain, "norm_bias": norm_bias, "qkv_weight": qkv_weight, "qkv_bias": qkv_bias, "out_weight": out_weight, "out_bias": out_bias, "up_weight": up_weight, "up_bias": up_bias, "down_weight": down_weight, "down_bias": down_bias}


@jax.custom_vjp
def low(v):
    return lax.optimization_barrier(v.astype(jnp.bfloat16)).astype(jnp.float32)

@jax.custom_vjp
def low_back(v):
    return v

def low_keep(v):
    return (low(v), None)

def low_pass(kept, grad):
    return (grad,)

def back_keep(v):
    return (v, None)

def back_low(kept, grad):
    return (low(grad),)
low.defvjp(low_keep, low_pass)
low_back.defvjp(back_keep, back_low)
HIGHEST = lax.Precision.HIGHEST
EPSILON = 1e-05
MASKED = -1e+30

def turning(places):
    halfway = ROT // 2
    frequencies = 10000.0 ** (-(jnp.arange(halfway, dtype=jnp.float32) * 2.0 / ROT))
    angle_table = places.astype(jnp.float32)[:, None] * frequencies[None, :]
    return (jnp.cos(angle_table)[:, None, :], jnp.sin(angle_table)[:, None, :])

def rotate(values, cosine_table, sine_table):
    halfway = ROT // 2
    first_half = values[..., :halfway]
    second_half = values[..., halfway:ROT]
    return jnp.concatenate([first_half * cosine_table - second_half * sine_table, second_half * cosine_table + first_half * sine_table, values[..., ROT:]], axis=-1)

def attention(queries, keys_all, values_all, places):
    block_rows = min(512, SEQ_LEN)
    query_blocks = queries.reshape(SEQ_LEN // block_rows, block_rows, HEADS, HEAD_DIM)
    place_blocks = places.reshape(SEQ_LEN // block_rows, block_rows)

    def one_block(block_pair):
        query_block, query_places = block_pair
        scores = low_back(jnp.einsum('qhd,khd->hqk', query_block, keys_all, precision=HIGHEST) * HEAD_DIM ** (-0.5))
        causal = (query_places[:, None] >= places[None, :])[None]
        scores = jnp.where(causal, scores, MASKED)
        row_max = lax.optimization_barrier(jnp.max(scores, axis=-1, keepdims=True))
        log_total = row_max + jnp.log(lax.optimization_barrier(jnp.sum(jnp.exp(scores - row_max), axis=-1, keepdims=True)))
        probabilities = low(jnp.where(causal, jnp.exp(scores - log_total), 0.0))
        return jnp.einsum('hqk,khd->qhd', probabilities, values_all, precision=HIGHEST)
    outputs = lax.map(jax.checkpoint(one_block), (query_blocks, place_blocks))
    return outputs.reshape(SEQ_LEN, HEADS, HEAD_DIM)

def block_forward(params, inputs, places):
    norm_gain, norm_bias, qkv_weight, qkv_bias, out_weight, out_bias, up_weight, up_bias, down_weight, down_bias = params
    head_width = HEADS * HEAD_DIM
    row_mean = lax.optimization_barrier(jnp.mean(inputs, axis=-1, keepdims=True))
    centered = inputs - row_mean
    variance = lax.optimization_barrier(jnp.mean(centered * centered, axis=-1, keepdims=True))
    normed = low(centered * lax.rsqrt(variance + EPSILON) * norm_gain + norm_bias)
    mixed_qkv = low_back(jnp.dot(normed, qkv_weight.reshape(D, 3 * head_width), precision=HIGHEST) + qkv_bias.reshape(3 * head_width))
    mixed_qkv = mixed_qkv.reshape(SEQ_LEN, 3, HEADS, HEAD_DIM)
    cosine_table, sine_table = turning(places)
    queries = low(rotate(mixed_qkv[:, 0], cosine_table, sine_table))
    keys_all = low(rotate(mixed_qkv[:, 1], cosine_table, sine_table))
    values_all = low(mixed_qkv[:, 2])
    attended = low(low_back(attention(queries, keys_all, values_all, places).reshape(SEQ_LEN, head_width)))
    hidden = low_back(jnp.dot(normed, up_weight, precision=HIGHEST) + up_bias)
    activated = low(jax.nn.gelu(hidden, approximate=True))
    return inputs + jnp.dot(attended, out_weight, precision=HIGHEST) + out_bias + jnp.dot(activated, down_weight, precision=HIGHEST) + down_bias

def reference(tokens, positions, cotangent, norm_gain, norm_bias, qkv_weight, qkv_bias, out_weight, out_bias, up_weight, up_bias, down_weight, down_bias):
    params = tuple((weight_item.astype(jnp.float32) for weight_item in (norm_gain, norm_bias, qkv_weight, qkv_bias, out_weight, out_bias, up_weight, up_bias, down_weight, down_bias)))
    inputs = tokens.astype(jnp.float32)
    cot_rows = cotangent.astype(jnp.float32)

    def per_sequence(totals, sequence_pair):
        input_rows, grad_rows = sequence_pair
        output_rows, pullback = jax.vjp(lambda weights_in, rows_in: block_forward(weights_in, rows_in, positions), params, input_rows)
        weight_grads, input_grads = pullback(grad_rows)
        totals = jax.tree.map(lambda left, right: left + right, totals, weight_grads)
        return (totals, (output_rows.astype(jnp.bfloat16), input_grads))
    zeros_start = tuple((jnp.zeros_like(weight_item) for weight_item in params))
    totals, (layer_output, tokens_grad) = lax.scan(per_sequence, zeros_start, (inputs, cot_rows))
    return (layer_output, tokens_grad, totals[0], totals[1], totals[2], totals[3], totals[4], totals[5], totals[6], totals[7], totals[8], totals[9])
```

```python
import functools

import jax
import jax.numpy as jnp
from jax import lax
from jax.experimental import pallas as pl
from jax.experimental.pallas import tpu as pltpu
from jax.sharding import PartitionSpec as P

D = 2048
HEAD_DIM = 64
ROT = 32
GROUP = 256
PAIR = 2 * HEAD_DIM

EPSILON = 1e-05
MASKED = -1e30
GELU_SLOPE = 0.7978845608028654
GELU_CUBE = 0.044715

NT = (((1,), (1,)), ((), ()))
NN = (((1,), (0,)), ((), ()))


def dot(left, right, dims=NN):
    return lax.dot_general(left, right, dims, preferred_element_type=jnp.float32)


def turning(places):
    halfway = ROT // 2
    frequencies = 10000.0 ** (-(jnp.arange(halfway, dtype=jnp.float32) * 2.0 / ROT))
    angles = places.astype(jnp.float32)[:, None] * frequencies[None, :]
    cosine, sine = jnp.cos(angles), jnp.sin(angles)
    rest = jnp.ones((places.shape[0], HEAD_DIM - ROT), jnp.float32)
    cosine_table = jnp.concatenate([cosine, cosine, rest] * 2, axis=1)
    sine_table = jnp.concatenate([-sine, sine, 0.0 * rest] * 2, axis=1)
    return cosine_table, sine_table


def turn(values, cosine, sine):
    halfway = ROT // 2
    lane = lax.broadcasted_iota(jnp.int32, values.shape, 1) % HEAD_DIM
    partner = jnp.where(
        lane < halfway,
        pltpu.roll(values, PAIR - halfway, 1),
        pltpu.roll(values, halfway, 1),
    )
    return values * cosine + partner * sine


def attention_kernel(
    order,
    query_in,
    key_in,
    value_in,
    grad_in,
    cosine_all,
    sine_all,
    attended_out,
    query_out,
    key_out,
    value_out,
    keys,
    values,
    keys_turned,
    values_turned,
    key_total,
    value_total,
    strip,
):
    groups = pl.num_programs(1)
    group = pl.program_id(1)
    scale = HEAD_DIM ** (-0.5)

    def rows(index):
        return pl.ds(pl.multiple_of(index * GROUP, GROUP), GROUP)

    @pl.when(group == 0)
    def _():
        def sort(place, carry):
            source, target = rows(order[place]), rows(place)
            key = turn(key_in[source, :], cosine_all[source, :], sine_all[source, :])
            value = value_in[source, :]
            keys[target, :] = key.astype(jnp.bfloat16)
            values[target, :] = value.astype(jnp.bfloat16)
            keys_turned[place] = key.T.astype(jnp.bfloat16)
            values_turned[place] = value.T.astype(jnp.bfloat16)
            key_total[target, :] = jnp.zeros((GROUP, PAIR), jnp.float32)
            value_total[target, :] = jnp.zeros((GROUP, PAIR), jnp.float32)
            return carry

        lax.fori_loop(0, groups, sort, 0)

    own = rows(order[group])
    cosine, sine = cosine_all[own, :], sine_all[own, :]
    query = turn(query_in[...], cosine, sine).astype(jnp.bfloat16)
    query = (query.astype(jnp.float32) * scale).astype(jnp.bfloat16)
    grad = grad_in[...]
    first = lax.broadcasted_iota(jnp.int32, (GROUP, PAIR), 1) < HEAD_DIM
    nothing = jnp.zeros((GROUP, PAIR), jnp.bfloat16)
    query_pair = jnp.concatenate(
        [jnp.where(first, query, nothing), jnp.where(first, nothing, query)], axis=0
    )
    grad_pair = jnp.concatenate(
        [jnp.where(first, grad, nothing), jnp.where(first, nothing, grad)], axis=0
    )
    wide = 2 * GROUP

    def fold(tile):
        return tile.reshape(GROUP // 8, 8, wide)

    def score(place):
        return dot(keys[rows(place), :], query_pair, NT)

    def scores(place, most):
        tile = score(place)
        strip[place] = tile
        return jnp.maximum(most, jnp.max(fold(tile), axis=0))

    most = lax.fori_loop(0, group, scores, jnp.full((8, wide), MASKED, jnp.float32))
    key_row = lax.broadcasted_iota(jnp.int32, (GROUP, wide), 0)
    query_lane = lax.broadcasted_iota(jnp.int32, (GROUP, wide), 1) % GROUP
    tile = jnp.where(key_row <= query_lane, score(group), MASKED)
    strip[group] = tile
    most = jnp.max(jnp.maximum(most, jnp.max(fold(tile), axis=0)), axis=0, keepdims=True)

    def weigh(place, carry):
        total, upper, lower = carry
        tile = jnp.exp(strip[place] - most)
        strip[place] = tile
        low = tile.astype(jnp.bfloat16)
        upper = upper + dot(values_turned[place, :HEAD_DIM, :], low[:, :GROUP])
        lower = lower + dot(values_turned[place, HEAD_DIM:, :], low[:, GROUP:])
        return total + jnp.sum(fold(tile), axis=0), upper, lower

    blank = jnp.zeros((HEAD_DIM, GROUP), jnp.float32)
    total, upper, lower = lax.fori_loop(
        0, group + 1, weigh, (jnp.zeros((8, wide), jnp.float32), blank, blank)
    )
    share = 1.0 / jnp.sum(total, axis=0, keepdims=True)
    upper = upper * share[:, :GROUP]
    lower = lower * share[:, GROUP:]
    attended_out[...] = jnp.concatenate([upper, lower], axis=0).T.astype(jnp.bfloat16)
    grad_turned = grad.astype(jnp.float32).T
    delta = jnp.concatenate(
        [
            jnp.sum(upper * grad_turned[:HEAD_DIM], axis=0, keepdims=True),
            jnp.sum(lower * grad_turned[HEAD_DIM:], axis=0, keepdims=True),
        ],
        axis=1,
    )

    def back(place, carry):
        upper, lower = carry
        here = rows(place)
        part = strip[place] * share
        value_total[here, :] += dot(part.astype(jnp.bfloat16), grad_pair)
        part = part * (dot(values[here, :], grad_pair, NT) - delta)
        low = part.astype(jnp.bfloat16)
        key_total[here, :] += dot(low, query_pair)
        upper = upper + dot(keys_turned[place, :HEAD_DIM, :], low[:, :GROUP])
        lower = lower + dot(keys_turned[place, HEAD_DIM:, :], low[:, GROUP:])
        return upper, lower

    upper, lower = lax.fori_loop(0, group + 1, back, (blank, blank))
    query_grad = jnp.concatenate([upper, lower], axis=0).T * scale
    query_out[...] = turn(query_grad, cosine, -sine).astype(jnp.bfloat16)

    @pl.when(group == groups - 1)
    def _():
        def unsort(place, carry):
            source, target = rows(place), rows(order[place])
            key_grad = turn(key_total[source, :], cosine_all[target, :], -sine_all[target, :])
            key_out[target, :] = key_grad.astype(jnp.bfloat16)
            value_out[target, :] = value_total[source, :].astype(jnp.bfloat16)
            return carry

        lax.fori_loop(0, groups, unsort, 0)


def attention(order, mixed, out_grads, cosine_table, sine_table):
    length = mixed.shape[0]
    width = out_grads.shape[1]
    pairs = width // PAIR
    groups = length // GROUP
    mixed = mixed.reshape(length, 3 * width)

    def block(which):
        return pl.BlockSpec((GROUP, PAIR), lambda pair, group, order: (order[group], which * pairs + pair))

    def column(which):
        return pl.BlockSpec((length, PAIR), lambda pair, group, order: (0, which * pairs + pair))

    table = pl.BlockSpec((length, PAIR), lambda pair, group, order: (0, 0))
    shape = jax.ShapeDtypeStruct((length, width), jnp.bfloat16)
    tiles = groups * (groups + 1) // 2 * pairs * 2 * GROUP * GROUP
    return pl.pallas_call(
        attention_kernel,
        grid_spec=pltpu.PrefetchScalarGridSpec(
            num_scalar_prefetch=1,
            grid=(pairs, groups),
            in_specs=[block(0), column(1), column(2), block(0), table, table],
            out_specs=[block(0), block(0), column(0), column(0)],
            scratch_shapes=[
                pltpu.VMEM((length, PAIR), jnp.bfloat16),
                pltpu.VMEM((length, PAIR), jnp.bfloat16),
                pltpu.VMEM((groups, PAIR, GROUP), jnp.bfloat16),
                pltpu.VMEM((groups, PAIR, GROUP), jnp.bfloat16),
                pltpu.VMEM((length, PAIR), jnp.float32),
                pltpu.VMEM((length, PAIR), jnp.float32),
                pltpu.VMEM((groups, GROUP, 2 * GROUP), jnp.float32),
            ],
        ),
        out_shape=[shape] * 4,
        compiler_params=pltpu.CompilerParams(
            dimension_semantics=("arbitrary", "arbitrary"), vmem_limit_bytes=40 * 1024 * 1024
        ),
        cost_estimate=pl.CostEstimate(
            flops=tiles * 6 * 2 * 256, bytes_accessed=length * width * 22, transcendentals=tiles
        ),
    )(order, mixed, mixed, mixed, out_grads, cosine_table, sine_table)


def swap(values, axis, bit):
    size = lax.axis_size(axis)
    return lax.ppermute(values, axis, [(place, place ^ bit) for place in range(size)])


def total(values, axes):
    for axis in axes:
        bit = 1
        while bit < lax.axis_size(axis):
            values = values + swap(values, axis, bit)
            bit *= 2
    return values


def paired():
    return lax.axis_size("ctx") == 4 and lax.axis_size("tp") == 2


def gather_rows(own):
    if not paired():
        return lax.all_gather(own, ("ctx", "tp"), axis=0, tiled=True)
    half = own.shape[0] // 2
    across = swap(own, "tp", 1)
    along = swap(own, "ctx", 2)
    corner = jnp.concatenate([swap(across[:half], "ctx", 2), swap(along[half:], "tp", 1)], axis=0)
    near = [own, across, along, corner]
    return jnp.concatenate(near + [swap(part, "ctx", 1) for part in near], axis=0)


def scatter_rows(parts):
    if not paired():
        return lax.psum_scatter(parts, ("ctx", "tp"), scatter_dimension=0, tiled=True).astype(
            jnp.float32
        )
    size = parts.shape[0] // 8
    half = size // 2

    def add(left, right):
        return left.astype(jnp.float32) + right.astype(jnp.float32)

    def block(index):
        return parts[index * size : (index + 1) * size]

    own, across, along, corner = [
        add(block(index), swap(block(4 + index), "ctx", 1)) for index in range(4)
    ]
    corner = corner.astype(jnp.bfloat16)
    from_across = swap(corner[:half], "tp", 1)
    from_along = swap(corner[half:], "ctx", 2)
    along = jnp.concatenate([add(along[:half], from_across), along[half:]], axis=0)
    across = jnp.concatenate([across[:half], add(across[half:], from_along)], axis=0)
    return add(
        add(own, swap(across.astype(jnp.bfloat16), "tp", 1)),
        swap(along.astype(jnp.bfloat16), "ctx", 2),
    )


def local_places(positions):
    if not paired():
        return positions
    devices = jnp.array([2 * along + near for near in (0, 1) for along in (0, 1) for _ in (0, 1)])
    blocks = (lax.axis_index("ctx") ^ devices) * 2 + (
        lax.axis_index("tp") ^ jnp.array([0, 1] * 4)
    )
    return positions.reshape(8, -1)[blocks].reshape(-1)


def spread(own):
    size, place = lax.axis_size("fsdp"), lax.axis_index("fsdp")
    result = jnp.zeros((size,) + own.shape, own.dtype)
    result = lax.dynamic_update_index_in_dim(result, own, place, 0)
    upward = downward = own
    for step in range(1, size):
        upward = lax.ppermute(upward, "fsdp", [(j, j + 1) for j in range(step - 1, size - 1)])
        downward = lax.ppermute(downward, "fsdp", [(j, j - 1) for j in range(1, size - step + 1)])
        for there, source, block in (
            (place >= step, place - step, upward),
            (place < size - step, place + step, downward),
        ):
            result = lax.dynamic_update_index_in_dim(
                result, jnp.where(there, block, own), jnp.where(there, source, place), 0
            )
    return result


def collapse(parts):
    size, place = lax.axis_size("fsdp"), lax.axis_index("fsdp")

    def block(index):
        return lax.dynamic_index_in_dim(parts, jnp.clip(index, 0, size - 1), 0, keepdims=False)

    def add(left, right):
        return left if right is None else left.astype(jnp.float32) + right.astype(jnp.float32)

    upward = downward = None
    for step in range(1, size):
        send = add(block(size - step + place), upward).astype(jnp.bfloat16)
        upward = lax.ppermute(send, "fsdp", [(j, j + 1) for j in range(step)])
        send = add(block(place + step - size), downward).astype(jnp.bfloat16)
        downward = lax.ppermute(send, "fsdp", [(j, j - 1) for j in range(size - step, size)])
    return add(add(block(place), upward), downward)


def gather_weight(shard):
    width = shard.shape[2] // lax.axis_size("ctx")
    mine = lax.all_to_all(shard, "ctx", 2, 0, tiled=True)
    return spread(mine.reshape(mine.shape[0], -1)).reshape(-1, shard.shape[1] * width)


def scatter_grad(grad, parts):
    size = lax.axis_size("fsdp")
    mine = collapse(grad.reshape(size, -1, grad.shape[1])).astype(jnp.bfloat16)
    mine = mine.reshape(mine.shape[0], parts, -1)
    return lax.all_to_all(mine, "ctx", 0, 2, tiled=True).astype(jnp.float32)


def on_device(
    tokens,
    positions,
    cotangent,
    norm_gain,
    norm_bias,
    qkv_weight,
    qkv_bias,
    out_weight,
    out_bias,
    up_weight,
    up_bias,
    down_weight,
    down_bias,
):
    parts = lax.axis_size("ctx")
    part = lax.axis_index("ctx")
    width = qkv_weight.shape[2] // parts
    units = up_weight.shape[1] // parts

    inputs = tokens[0].astype(jnp.float32)
    row_mean = jnp.mean(inputs, axis=-1, keepdims=True)
    centered = inputs - row_mean
    inverse = lax.rsqrt(jnp.mean(centered * centered, axis=-1, keepdims=True) + EPSILON)
    unit_rows = centered * inverse
    normed_own = (unit_rows * norm_gain + norm_bias).astype(jnp.bfloat16)

    attention_shard = jnp.concatenate([qkv_weight, out_weight.T[:, None, :]], axis=1)
    attention_weight = gather_weight(attention_shard)
    normed = gather_rows(normed_own)
    up_full = gather_weight(up_weight[:, None, :])
    grads = gather_rows(cotangent[0])
    down_full = gather_weight(down_weight.T[:, None, :])

    qkv_full = attention_weight[:, : 3 * width]
    out_full = attention_weight[:, 3 * width :]
    bias = lax.dynamic_slice_in_dim(qkv_bias, part * width, width, 1).reshape(3 * width)
    mixed = dot(normed, qkv_full) + bias
    out_grads = dot(grads, out_full).astype(jnp.bfloat16)
    places = local_places(positions)
    groups = places[::GROUP] // GROUP
    order = jnp.sum(
        jnp.where(
            groups[None, :] == jnp.arange(groups.shape[0])[:, None],
            jnp.arange(groups.shape[0])[None, :],
            0,
        ),
        axis=1,
    ).astype(jnp.int32)
    cosine_table, sine_table = turning(places)
    mixed = mixed.reshape(-1, 3, width)
    short = -width % PAIR
    attended, *head_grads = attention(
        order,
        jnp.pad(mixed, ((0, 0), (0, 0), (0, short))),
        jnp.pad(out_grads, ((0, 0), (0, short))),
        cosine_table,
        sine_table,
    )
    attended = attended[:, :width]
    qkv_grad = jnp.concatenate([item[:, :width] for item in head_grads], axis=1)

    own_bias = lax.dynamic_slice_in_dim(up_bias, part * units, units, 0)
    hidden = dot(normed, up_full) + own_bias
    bent = jnp.tanh(GELU_SLOPE * (hidden + GELU_CUBE * hidden * hidden * hidden))
    activated = (0.5 * hidden * (1.0 + bent)).astype(jnp.bfloat16)
    slope = 0.5 * (1.0 + bent) + 0.5 * hidden * (1.0 - bent * bent) * GELU_SLOPE * (
        1.0 + 3.0 * GELU_CUBE * hidden * hidden
    )
    hidden_grad = (dot(grads, down_full, NN) * slope).astype(jnp.bfloat16)

    branch = dot(attended, out_full, NT) + dot(activated, down_full, NT)
    branch_sum = scatter_rows(branch.astype(jnp.bfloat16))
    layer_output = (inputs + branch_sum + out_bias + down_bias).astype(jnp.bfloat16)

    def across(left, right):
        return dot(left, right, (((0,), (0,)), ((), ()))).astype(jnp.bfloat16)

    attention_grad = scatter_grad(
        jnp.concatenate([across(normed, qkv_grad), across(grads, attended)], axis=1), 4
    )
    down_grad = scatter_grad(across(grads, activated), 1)
    up_grad = scatter_grad(across(normed, hidden_grad), 1)

    normed_part = dot(qkv_grad, qkv_full, NT) + dot(hidden_grad, up_full, NT)
    normed_back = scatter_rows(normed_part.astype(jnp.bfloat16))
    unit_grad = normed_back * norm_gain
    tokens_grad = cotangent[0].astype(jnp.float32) + inverse * (
        unit_grad
        - jnp.mean(unit_grad, axis=-1, keepdims=True)
        - unit_rows * jnp.mean(unit_grad * unit_rows, axis=-1, keepdims=True)
    )

    qkv_sums = jnp.sum(qkv_grad, axis=0, dtype=jnp.float32).reshape(3, width)
    up_sums = jnp.sum(hidden_grad, axis=0, dtype=jnp.float32)
    bias_sums = jnp.concatenate(
        [
            lax.dynamic_update_slice_in_dim(
                jnp.zeros(qkv_bias.shape, jnp.float32), qkv_sums, part * width, 1
            ).reshape(-1),
            lax.dynamic_update_slice_in_dim(
                jnp.zeros(up_bias.shape, jnp.float32), up_sums, part * units, 0
            ),
        ]
    )
    bias_sums = total(bias_sums, ("fsdp", "ctx"))
    norm_sums = total(
        jnp.stack(
            [
                jnp.sum(normed_back * unit_rows, axis=0),
                jnp.sum(normed_back, axis=0),
                jnp.sum(cotangent[0], axis=0, dtype=jnp.float32),
            ]
        ),
        ("ctx", "tp", "fsdp"),
    )
    return (
        layer_output[None],
        tokens_grad[None],
        norm_sums[0],
        norm_sums[1],
        attention_grad[:, :3],
        bias_sums[: qkv_bias.size].reshape(qkv_bias.shape),
        attention_grad[:, 3].T,
        norm_sums[2],
        up_grad[:, 0],
        bias_sums[qkv_bias.size :],
        down_grad[:, 0].T,
        norm_sums[2],
    )


def solution(mesh):
    rows = P("fsdp", ("ctx", "tp"), None)
    placed = (
        rows,
        P(),
        rows,
        P(),
        P(),
        P(("fsdp", "ctx"), None, "tp"),
        P(None, "tp"),
        P("tp", ("fsdp", "ctx")),
        P(),
        P(("fsdp", "ctx"), "tp"),
        P("tp"),
        P("tp", ("fsdp", "ctx")),
        P(),
    )
    return jax.shard_map(
        on_device,
        mesh=mesh,
        in_specs=placed,
        out_specs=(
            rows,
            rows,
            P(),
            P(),
            P(("fsdp", "ctx"), None, "tp"),
            P(None, "tp"),
            P("tp", ("fsdp", "ctx")),
            P(),
            P(("fsdp", "ctx"), "tp"),
            P("tp"),
            P("tp", ("fsdp", "ctx")),
            P(),
        ),
        check_vma=False,
    )
```

```python
import functools
import types

import jax
import jax.numpy as jnp
from jax import lax
from jax.experimental import pallas as pl
from jax.experimental.pallas import tpu as pltpu
from jax.sharding import PartitionSpec as P

FSDP, CTX, TP = "fsdp", "ctx", "tp"

D = 2048
HEAD_DIM = 64
ROT = 32
GROUP = 256
PAIR = 2 * HEAD_DIM

EPSILON = 1e-05
MASKED = -1e30
GELU_SLOPE = 0.7978845608028654
GELU_CUBE = 0.044715


TURNS = ((3, 2, 1, 0), (3, 2, 0, 1), (0, 1, 3, 2), (0, 1, 2, 3))

NT = (((1,), (1,)), ((), ()))
NN = (((1,), (0,)), ((), ()))


NO_COST = pl.CostEstimate(flops=0, bytes_accessed=0, transcendentals=0)


def params(mebibytes=48):
    return pltpu.CompilerParams(vmem_limit_bytes=mebibytes * 1024 * 1024)


def dot(left, right, dims=NN):
    return lax.dot_general(left, right, dims, preferred_element_type=jnp.float32)


def turning(places):
    halfway = ROT // 2
    lane = jnp.arange(PAIR) % HEAD_DIM
    frequencies = 10000.0 ** (-((lane % halfway).astype(jnp.float32) * 2.0 / ROT))
    frequencies = jnp.where(lane < ROT, frequencies, 0.0)
    angles = places.astype(jnp.float32)[:, None] * frequencies[None, :]
    return jnp.cos(angles), jnp.sin(angles) * jnp.where(lane < halfway, -1.0, 1.0)[None, :]


def turn(values, cosine, sine):
    halfway = ROT // 2
    lane = lax.broadcasted_iota(jnp.int32, values.shape, 1) % HEAD_DIM
    partner = jnp.where(
        lane < halfway,
        pltpu.roll(values, PAIR - halfway, 1),
        pltpu.roll(values, halfway, 1),
    )
    return values * cosine + partner * sine


def attention_kernel(
    order,
    query_in,
    key_all,
    value_all,
    key_turned,
    value_turned,
    grad_in,
    grad_turned,
    cosine_all,
    sine_all,
    *refs,
):
    (attended_out, query_out, key_out, value_out, key_total, value_total, strip) = refs[-7:]
    groups, group = pl.num_programs(0), pl.program_id(0)
    tall, wide = strip.shape[1:]
    blocks = tall // GROUP

    def rows(place):
        return pl.ds(pl.multiple_of(order[place] * GROUP, GROUP), GROUP)

    def load(ref, step):
        return jnp.concatenate([ref[rows(step * blocks + at), :] for at in range(blocks)], axis=0)

    def load_turned(ref, step, head):
        here = slice(head * HEAD_DIM, (head + 1) * HEAD_DIM)
        return jnp.concatenate([ref[here, rows(step * blocks + at)] for at in range(blocks)], axis=1)

    def put(ref, step, values):
        for at in range(blocks):
            ref[rows(step * blocks + at), :] += values[at * GROUP : (at + 1) * GROUP]

    def fold(tile):
        return tile.reshape(tall // 8, 8, wide)

    def pair_up(values):
        first = lax.broadcasted_iota(jnp.int32, (GROUP, PAIR), 1) < HEAD_DIM
        nothing = jnp.zeros((GROUP, PAIR), jnp.bfloat16)
        return jnp.concatenate(
            [jnp.where(first, values, nothing), jnp.where(first, nothing, values)], axis=0
        )

    @pl.when(group == 0)
    def _():
        key_total[...] = jnp.zeros_like(key_total)
        value_total[...] = jnp.zeros_like(value_total)

    query_pair, grad_pair = pair_up(query_in[...]), pair_up(grad_in[...])
    steps = (group + blocks) // blocks
    ahead = lax.broadcasted_iota(jnp.int32, (tall, wide), 0) - (
        lax.broadcasted_iota(jnp.int32, (tall, wide), 1) % GROUP
    )

    def scores(step, most):
        tile = dot(load(key_all, step), query_pair, NT)
        tile = jnp.where(ahead <= (group - step * blocks) * GROUP, tile, MASKED)
        strip[step] = tile
        return jnp.maximum(most, jnp.max(fold(tile), axis=0))

    most = lax.fori_loop(0, steps, scores, jnp.full((8, wide), MASKED, jnp.float32))
    most = jnp.max(most, axis=0, keepdims=True)

    def weigh(step, carry):
        total, upper, lower = carry
        tile = jnp.exp(strip[step] - most)
        strip[step] = tile
        low = tile.astype(jnp.bfloat16)
        upper = upper + dot(load_turned(value_turned, step, 0), low[:, :GROUP])
        lower = lower + dot(load_turned(value_turned, step, 1), low[:, GROUP:])
        return total + jnp.sum(fold(tile), axis=0), upper, lower

    blank = jnp.zeros((HEAD_DIM, GROUP), jnp.float32)
    total, upper, lower = lax.fori_loop(
        0, steps, weigh, (jnp.zeros((8, wide), jnp.float32), blank, blank)
    )
    share = 1.0 / jnp.sum(total, axis=0, keepdims=True)
    upper = upper * share[:, :GROUP]
    lower = lower * share[:, GROUP:]
    attended_out[...] = jnp.concatenate([upper, lower], axis=0).astype(jnp.bfloat16).T
    grad = grad_turned[...].astype(jnp.float32)
    delta = jnp.concatenate(
        [
            jnp.sum(upper * grad[:HEAD_DIM], axis=0, keepdims=True),
            jnp.sum(lower * grad[HEAD_DIM:], axis=0, keepdims=True),
        ],
        axis=1,
    )

    def back(step, carry):
        upper, lower = carry
        part = strip[step] * share
        put(value_total, step, dot(part.astype(jnp.bfloat16), grad_pair))
        part = part * (dot(load(value_all, step), grad_pair, NT) - delta)
        low = part.astype(jnp.bfloat16)
        put(key_total, step, dot(low, query_pair))
        upper = upper + dot(load_turned(key_turned, step, 0), low[:, :GROUP])
        lower = lower + dot(load_turned(key_turned, step, 1), low[:, GROUP:])
        return upper, lower

    upper, lower = lax.fori_loop(0, steps, back, (blank, blank))
    own = rows(group)
    query_grad = jnp.concatenate([upper, lower], axis=0).T * HEAD_DIM ** (-0.5)
    query_out[...] = turn(query_grad, cosine_all[own, :], -sine_all[own, :]).astype(jnp.bfloat16)

    @pl.when(group == groups - 1)
    def _():
        key_grad = turn(key_total[...], cosine_all[...], -sine_all[...])
        key_out[...] = key_grad.astype(jnp.bfloat16)
        value_out[...] = value_total[...].astype(jnp.bfloat16)


def attention(order, projected, tables, pair, earlier=()):
    length, width = projected[0].shape
    groups = length // GROUP
    block = pl.BlockSpec((GROUP, PAIR), lambda group, order: (order[group], pair))
    turned_block = pl.BlockSpec((PAIR, GROUP), lambda group, order: (pair, order[group]))
    column = pl.BlockSpec((length, PAIR), lambda group, order: (0, pair))
    turned_column = pl.BlockSpec((PAIR, length), lambda group, order: (pair, 0))
    table = pl.BlockSpec((length, PAIR), lambda group, order: (0, 0))
    specs = [block, column, column, turned_column, turned_column, block, turned_block, table, table]
    return pl.pallas_call(
        attention_kernel,
        grid_spec=pltpu.PrefetchScalarGridSpec(
            num_scalar_prefetch=1,
            grid=(groups,),
            in_specs=specs + [pl.BlockSpec(memory_space=pl.ANY)] * len(earlier),
            out_specs=[block, block, column, column],
            scratch_shapes=[
                pltpu.VMEM((length, PAIR), jnp.float32),
                pltpu.VMEM((length, PAIR), jnp.float32),
                pltpu.VMEM((groups // 2, 2 * GROUP, 2 * GROUP), jnp.float32),
            ],
        ),
        out_shape=[jax.ShapeDtypeStruct((length, width), jnp.bfloat16)] * 4,
        input_output_aliases={1 + len(specs) + at: at for at in range(len(earlier))},
        compiler_params=params(60),
        cost_estimate=NO_COST,
        name=f"attention_{pair}",
    )(order, *projected, *tables, *earlier)


ROWS = 512


def chunk(place, which, size):
    return pl.ds(pl.multiple_of(place[which] * size, size), size)


def row_call(name, kernel, row_inputs, full_inputs, outputs, size=ROWS, turn=0, mebibytes=48):
    count = row_inputs[0].shape[0] // size
    rows = count * size

    def out(item):
        if len(item) == 4 and item[3] is None:
            shape, spec = item[:2], pl.BlockSpec(item[:2], lambda at: (0, 0))
        elif len(item) == 4:
            shape = ((item[3] - item[2]) * size, item[0])
            spec = pl.BlockSpec(
                (size, item[0]),
                lambda at: (jnp.clip(at, item[2], item[3] - 1) - item[2], 0),
            )
        elif len(item) == 3:
            shape = (item[0], rows)
            spec = pl.BlockSpec((item[0], size), lambda at: (0, at))
        else:
            shape = (rows, item[0])
            spec = pl.BlockSpec((size, item[0]), lambda at: (at, 0))
        kind = item[2] if len(item) == 4 and item[3] is None else item[1]
        return spec, jax.ShapeDtypeStruct(shape, kind)

    return pl.pallas_call(
        kernel,
        grid=(count,),
        in_specs=[
            pl.BlockSpec((size, item.shape[1]), lambda at: (lax.rem(at + turn, count), 0))
            for item in row_inputs
        ]
        + [pl.BlockSpec(item.shape, lambda at: (0, 0)) for item in full_inputs],
        out_specs=[out(item)[0] for item in outputs],
        out_shape=[out(item)[1] for item in outputs],
        compiler_params=params(mebibytes),
        cost_estimate=NO_COST,
        name=name,
    )(*row_inputs, *full_inputs)


def add_up(target, at, values):
    part = jnp.sum(values.astype(jnp.float32), axis=0, keepdims=True)

    @pl.when(pl.program_id(0) == 0)
    def _():
        target[at : at + 1, :] = part

    @pl.when(pl.program_id(0) > 0)
    def _():
        target[at : at + 1, :] += part


def project_kernel(normed, grads, cosine, sine, weight, bias, *refs):
    query, key, value, key_turned, value_turned, out_grads, grads_turned = refs
    width = weight.shape[1] // 4
    mixed = dot(normed[...], weight[:, : 3 * width]) + bias[...]
    parts = [mixed[:, which * width : (which + 1) * width] for which in range(3)]
    parts.append(dot(grads[...], weight[:, 3 * width :]))
    for pair in range(-(-width // PAIR)):
        here = slice(pair * PAIR, (pair + 1) * PAIR)
        items = [part[:, here] for part in parts]
        if width < PAIR:
            nothing = jnp.zeros((ROWS, PAIR - width), jnp.float32)
            items = [jnp.concatenate([item, nothing], axis=1) for item in items]
        turned = [turn(item, cosine[...], sine[...]) for item in items[:2]]
        low = turned[0].astype(jnp.bfloat16).astype(jnp.float32) * HEAD_DIM ** (-0.5)
        query[:, here] = low.astype(jnp.bfloat16)
        for target, target_turned, item in (
            (key, key_turned, turned[1]),
            (value, value_turned, items[2]),
            (out_grads, grads_turned, items[3]),
        ):
            low = item.astype(jnp.bfloat16)
            target[:, here] = low
            target_turned[here, :] = low.T


def hidden_kernel(normed, weight, bias, activated, slope):
    hidden = dot(normed[...], weight[...]) + bias[...]
    square = hidden * hidden
    bent = jnp.tanh(GELU_SLOPE * hidden * (1.0 + GELU_CUBE * square))
    half = 0.5 * (1.0 + bent)
    activated[...] = (hidden * half).astype(jnp.bfloat16)
    slope[...] = (
        half
        + 0.5 * GELU_SLOPE * hidden * (1.0 - bent * bent) * (1.0 + 3.0 * GELU_CUBE * square)
    ).astype(jnp.bfloat16)


def hidden_grad_kernel(grads, slope, weight, target, sums):
    low = (dot(grads[...], weight[...]) * slope[...].astype(jnp.float32)).astype(jnp.bfloat16)
    target[...] = low
    add_up(sums, 0, low)


def back_kernel(columns, start, summing, halves, *refs):
    lefts = refs[: len(columns)]
    weights, outs = refs[len(columns) + start : -1 - summing - halves], refs[-1 - summing - halves :]
    result = refs[len(columns)][...].astype(jnp.float32) if start else None
    for left, (which, here) in zip(lefts, columns):
        part = dot(left[:, : here.stop - here.start], weights[which][:, here], NT)
        result = part if result is None else result + part
    if halves:
        early = pl.program_id(0) < pl.num_programs(0) // 2

        @pl.when(early)
        def _():
            outs[0][...] = result.astype(jnp.bfloat16)

        @pl.when(jnp.logical_not(early))
        def _():
            outs[1][...] = result.astype(jnp.bfloat16)

    else:
        outs[0][...] = result.astype(jnp.bfloat16)
    if summing:
        for at, left in enumerate(lefts):
            add_up(outs[1], at, left[...])


def back(lefts, columns, weights, start=None, halves=False, summing=False):
    size = ROWS
    count = lefts[0].shape[0] // size
    starts = [] if start is None else [start]
    outputs = [(weights[0].shape[0], jnp.bfloat16)]
    if halves:
        outputs = [outputs[0] + (0, count // 2), outputs[0] + (count // 2, count)]
    if summing:
        outputs.append((len(lefts), lefts[0].shape[1], jnp.float32, None))
    got = row_call(
        "back",
        functools.partial(back_kernel, columns, len(starts), int(summing), int(halves)),
        lefts + starts,
        weights,
        outputs,
        size,
        count // 2 if halves else 0,
    )
    return got if summing or halves else got[0]


def grad_kernel(counts, width, turns, *refs):
    target = refs[-1]
    refs = list(refs[:-1])
    at = 0
    for count in counts:
        left = refs.pop(0)
        for _ in range(count):
            right = refs.pop(0)
            columns = min(width, right.shape[1])
            target[0, :, at : at + columns] = dot(
                left[...], right[:, :columns], (((0,), (0,)), ((), ()))
            ).astype(jnp.bfloat16)
            at += columns


def grad_pieces(products, turns, first, count, width):
    size = lax.axis_size(FSDP)
    specs, items, columns = [], [], 0
    for left, rights in products:
        rows = left.shape[1] // size
        specs.append(
            pl.BlockSpec((left.shape[0], rows), lambda at, turns: (0, turns[first + at]))
        )
        specs += [pl.BlockSpec(item.shape, lambda at, turns: (0, 0)) for item in rights]
        items += [left, *rights]
        columns += sum(min(width, item.shape[1]) for item in rights)
    return pl.pallas_call(
        functools.partial(grad_kernel, [len(rights) for _, rights in products], width),
        grid_spec=pltpu.PrefetchScalarGridSpec(
            num_scalar_prefetch=1,
            grid=(count,),
            in_specs=specs,
            out_specs=pl.BlockSpec((1, rows, columns), lambda at, turns: (at, 0, 0)),
        ),
        out_shape=jax.ShapeDtypeStruct((count, rows, columns), jnp.bfloat16),
        compiler_params=params(),
        cost_estimate=NO_COST,
        name=f"grad_{first}",
    )(turns, *items)


def pointwise(name, function, scalars, inputs, outputs):
    def spec(item):
        if not isinstance(item, tuple):
            return pl.BlockSpec(item.shape, lambda at, n=item.ndim: (0,) * n)
        array, rows, index = item
        return pl.BlockSpec(
            (rows,) + array.shape[1:], lambda at, n=array.ndim, index=index: (index,) + (0,) * (n - 1)
        )

    def kernel(*refs):
        count = len(scalars) + len(inputs)
        for target, value in zip(refs[count:], function(*refs[:count])):
            target[...] = value.astype(target.dtype)

    return pl.pallas_call(
        kernel,
        grid=(1,),
        in_specs=[pl.BlockSpec(memory_space=pltpu.SMEM)] * len(scalars) + [spec(i) for i in inputs],
        out_specs=[pl.BlockSpec(shape, lambda at, n=len(shape): (0,) * n) for shape, _ in outputs],
        out_shape=[jax.ShapeDtypeStruct(shape, kind) for shape, kind in outputs],
        compiler_params=params(),
        cost_estimate=NO_COST,
        name=name,
    )(*scalars, *[item[0] if isinstance(item, tuple) else item for item in inputs])


def stack_kernel(parts, *refs):
    *sources, target, arrived = refs
    copies = [
        pltpu.make_async_copy(
            source.at[pl.ds(first, rows)], target.at[pl.ds(start, rows)], arrived.at[at]
        )
        for at, (source, (first, rows, start)) in enumerate(zip(sources, parts))
    ]
    for copy in copies:
        copy.start()
    for copy in copies:
        copy.wait()


def stack(parts, rows):
    array = parts[0][0]
    return pl.pallas_call(
        functools.partial(stack_kernel, [part[1:] for part in parts]),
        in_specs=[pl.BlockSpec(memory_space=pl.ANY)] * len(parts),
        out_specs=pl.BlockSpec(memory_space=pltpu.VMEM),
        out_shape=jax.ShapeDtypeStruct((rows, array.shape[1]), array.dtype),
        scratch_shapes=[pltpu.SemaphoreType.DMA((len(parts),))],
        compiler_params=params(),
        cost_estimate=NO_COST,
        name="stack",
    )(*[part[0] for part in parts])


def fill_kernel(starts, *refs):
    count = len(starts)
    sources, target = refs[:count], refs[count + 1]
    held, arrived, left = refs[count + 2 :]
    rows = [source.shape[0] for source in sources]
    slots = [pl.ds(sum(rows[:at]), rows[at]) for at in range(count)]
    inward = [
        pltpu.make_async_copy(source, held.at[slots[at]], arrived.at[at])
        for at, source in enumerate(sources)
    ]
    outward = [
        pltpu.make_async_copy(held.at[slots[at]], target.at[pl.ds(start, rows[at])], left.at[at])
        for at, start in enumerate(starts)
    ]
    for copy in inward:
        copy.start()
    for first, second in zip(inward, outward):
        first.wait()
        second.start()
    for copy in outward:
        copy.wait()


def fill(target, parts):
    anywhere = pl.BlockSpec(memory_space=pl.ANY)
    count = len(parts)
    rows = sum(array.shape[0] for array, _ in parts)
    return pl.pallas_call(
        functools.partial(fill_kernel, [start for _, start in parts]),
        in_specs=[anywhere] * (count + 1),
        out_specs=anywhere,
        out_shape=jax.ShapeDtypeStruct(target.shape, target.dtype),
        scratch_shapes=[
            pltpu.VMEM((rows, target.shape[1]), target.dtype),
            pltpu.SemaphoreType.DMA((count,)),
            pltpu.SemaphoreType.DMA((count,)),
        ],
        input_output_aliases={count: 0},
        compiler_params=params(),
        cost_estimate=NO_COST,
        name="fill",
    )(*[array for array, _ in parts], target)


def line_kernel(place, *refs):
    own, up_one, down_one, up_two, down_two, up_three, down_three, target, arrived = refs
    rows = own.shape[0]
    for where, sources in enumerate(
        (
            (own, down_one, down_two, down_three),
            (up_one, own, down_one, down_two),
            (up_two, up_one, own, down_one),
            (up_three, up_two, up_one, own),
        )
    ):

        @pl.when(place[0] == where)
        def _(sources=sources):
            copies = [
                pltpu.make_async_copy(source, target.at[pl.ds(at * rows, rows)], arrived.at[at])
                for at, source in enumerate(sources)
            ]
            for copy in copies:
                copy.start()
            for copy in copies:
                copy.wait()


def in_line(got):
    anywhere = pl.BlockSpec(memory_space=pl.ANY)
    rows, columns = got[0].shape
    return pl.pallas_call(
        line_kernel,
        in_specs=[pl.BlockSpec(memory_space=pltpu.SMEM)] + [anywhere] * len(got),
        out_specs=pl.BlockSpec(memory_space=pltpu.VMEM),
        out_shape=jax.ShapeDtypeStruct((4 * rows, columns), got[0].dtype),
        scratch_shapes=[pltpu.SemaphoreType.DMA((4,))],
        compiler_params=params(),
        cost_estimate=NO_COST,
        name="in_line",
    )(lax.axis_index(FSDP).astype(jnp.int32).reshape(1), *got)


def swap(values, axis, bit):
    size = lax.axis_size(axis)
    with jax.named_scope(f"{axis}_{bit}"):
        return lax.ppermute(values, axis, [(place, place ^ bit) for place in range(size)])


def total(values, axis):
    bit = 1
    while bit < lax.axis_size(axis):
        values = values + swap(values, axis, bit)
        bit *= 2
    return values


def move(values, pairs):
    with jax.named_scope("line"):
        return lax.ppermute(values, FSDP, pairs)


def spread_first(own):
    return [own, move(own, [(0, 1), (1, 2), (2, 3)]), move(own, [(1, 0), (2, 1), (3, 2)])]


def spread_second(got):
    return got + [move(got[1], [(1, 2), (2, 3)]), move(got[2], [(1, 0), (2, 1)])]


def spread_third(got):
    return got + [move(got[3], [(2, 3)]), move(got[4], [(1, 0)])]


def reduce_first(parts):
    return move(parts[0], [(0, 1), (3, 2)])


def square_first(own):
    return [own, swap(own, FSDP, 1), swap(own, FSDP, 2)]


def square_second(got):
    return got + [swap(got[2], FSDP, 1)]


def square_kernel(place, *refs):
    *sources, target, arrived = refs
    rows = sources[0].shape[0]
    copies = []
    for which, source in enumerate(sources):
        here = pl.ds(pl.multiple_of((place[0] ^ which) * rows, rows), rows)
        copies.append(pltpu.make_async_copy(source, target.at[here], arrived.at[which]))
    for copy in copies:
        copy.start()
    for copy in copies:
        copy.wait()


def in_square(got, place):
    rows, columns = got[0].shape
    return pl.pallas_call(
        square_kernel,
        in_specs=[pl.BlockSpec(memory_space=pltpu.SMEM)]
        + [pl.BlockSpec(memory_space=pl.ANY)] * len(got),
        out_specs=pl.BlockSpec(memory_space=pltpu.VMEM),
        out_shape=jax.ShapeDtypeStruct((len(got) * rows, columns), got[0].dtype),
        scratch_shapes=[pltpu.SemaphoreType.DMA((len(got),))],
        compiler_params=params(),
        cost_estimate=NO_COST,
        name="in_square",
    )(place, *got)


UP, DOWN = [(0, 1), (1, 2), (2, 3)], [(1, 0), (2, 1), (3, 2)]


def second_of(place, first, second, got):
    ends = (place[0] == 0) | (place[0] == 3)
    return jnp.where(ends, sum_of(second)[0], sum_of(first) + got)


def third_of(place, second, third, upward, downward):
    one, two = sum_of(second)[0], sum_of(third)[0]
    return (
        jnp.where(place[0] == 1, one, two) + sum_of(upward),
        jnp.where(place[0] == 2, one, two) + sum_of(downward),
    )


def reduce_second(sums, place):
    inputs = []
    for (first, rest), got in sums:
        inputs += [first, (rest, 1, 0), got]
    rows, columns = sums[0][0][0].shape

    def choose(place, *refs):
        sent = [
            second_of(place, first, second, sum_of(got))
            for first, second, got in zip(refs[::3], refs[1::3], refs[2::3])
        ]
        return [jnp.concatenate(sent, axis=0)]

    sent = pointwise(
        "second", choose, [place], inputs, [((len(sums) * rows, columns), jnp.bfloat16)]
    )[0]
    return [move(sent, UP[:2]), move(sent, DOWN[1:])]


def reduce_third(parts, got, place, new=None):
    first, rest = parts
    rows, columns = first.shape
    shape = (rows if new is None else 2 * rows, columns)

    def choose(place, second, third, upward, downward, *others):
        sent = third_of(place, second, third, upward, downward)
        if not others:
            return sent
        first, second, got = others
        other = second_of(place, first, second, sum_of(got))
        return [jnp.concatenate([item, other], axis=0) for item in sent]

    inputs = [(rest, 1, 0), (rest, 1, 1), *got]
    if new is not None:
        inputs += [new[0][0], (new[0][1], 1, 0), new[1]]
    upward, downward = pointwise(
        "third", choose, [place], inputs, [(shape, jnp.bfloat16)] * 2
    )
    return [move(upward, UP), move(downward, DOWN)]


def reduce_last(parts, got, index=0):
    first, rest = parts
    return pointwise(
        "last",
        lambda last, *got: [sum_of(last)[0] + sum_of(*got)],
        [],
        [(rest, 1, 2)] + [(item, first.shape[0], index) for item in got],
        [(first.shape, jnp.bfloat16)],
    )[0]


def paired():
    return lax.axis_size(CTX) == 4 and lax.axis_size(TP) == 2


def gather_first(own):
    if not paired():
        return [own]
    return [own, swap(own, TP, 1), swap(own, CTX, 2), swap(own, CTX, 1)]


def gather_second(got):
    if not paired():
        return got
    size = got[0].shape[0] // 2
    corner = [swap(got[1][:size], CTX, 2), swap(got[2][size:], TP, 1)]
    return got + [swap(got[1], CTX, 1), swap(got[2], CTX, 1)] + corner


def gather_third(got):
    if not paired():
        size = got[0].shape[0] // 2
        return [
            lax.all_gather(item, (CTX, TP), axis=0, tiled=True)
            for item in (got[0][:size], got[0][size:])
        ]
    own, across, along, far_own, far_across, far_along, *corner = got
    size = corner[0].shape[0]
    half = size // 2
    results = []
    for which in range(2):
        sides = (own, across, along, None, far_own, far_across, far_along, None)
        parts = [
            (item, which * size, size, at * size)
            for at, item in enumerate(sides)
            if item is not None
        ]
        results.append(stack(parts, 8 * size))
    corner, results = lax.optimization_barrier((corner, results))
    for which in range(2):
        parts = [(corner[which], 3 * size)]
        for at in (0, half):
            parts.append((swap(corner[which][at : at + half], CTX, 1), 7 * size + at))
        results[which] = fill(results[which], parts)
    return results


def scatter_first(near, far):
    return [near, swap(far, CTX, 1) if paired() else far]


def sum_of(*refs):
    result = None
    for ref in refs:
        values = ref[...].astype(jnp.float32)
        result = values if result is None else result + values
    return result


def scatter_second(*all_got):
    if not paired():
        return list(all_got)
    size, columns = all_got[0][0].shape[0] // 4, all_got[0][0].shape[1]
    half = size // 2

    def corners(*refs):
        sums = [sum_of(*refs[at : at + 2]) for at in range(0, len(refs), 2)]
        return [
            jnp.concatenate([item[:half] for item in sums], axis=0),
            jnp.concatenate([item[half:] for item in sums], axis=0),
        ]

    sent = pointwise(
        "corners",
        corners,
        [],
        [(item, size, 3) for got in all_got for item in got],
        [((len(all_got) * half, columns), jnp.bfloat16)] * 2,
    )
    from_across, from_along = swap(sent[0], TP, 1), swap(sent[1], CTX, 2)
    return [got + [from_across, from_along] for got in all_got]


def scatter_third(*all_got):
    if not paired():
        return [
            [lax.psum_scatter(jnp.concatenate(got), (CTX, TP), scatter_dimension=0, tiled=True)]
            for got in all_got
        ]
    size, columns = all_got[0][0].shape[0] // 4, all_got[0][0].shape[1]
    half = size // 2

    def sides(*refs):
        acrosses, alongs = [], []
        for at in range(0, len(refs), 6):
            across, along = sum_of(*refs[at : at + 2]), sum_of(*refs[at + 2 : at + 4])
            from_across, from_along = refs[at + 4 : at + 6]
            acrosses += [across[:half], across[half:] + sum_of(from_along)]
            alongs += [along[:half] + sum_of(from_across), along[half:]]
        return [jnp.concatenate(acrosses, axis=0), jnp.concatenate(alongs, axis=0)]

    inputs = []
    for at, (near, far, from_across, from_along) in enumerate(all_got):
        inputs += [(near, size, 1), (far, size, 1), (near, size, 2), (far, size, 2)]
        inputs += [(from_across, half, at), (from_along, half, at)]
    across, along = pointwise(
        "sides", sides, [], inputs, [((len(all_got) * size, columns), jnp.bfloat16)] * 2
    )
    across, along = swap(across, TP, 1), swap(along, CTX, 2)
    return [[near, far, across, along] for near, far, *_ in all_got]


def addends(got, index):
    if not paired():
        return got
    size = got[0].shape[0] // 4
    return [(got[0], size, 0), (got[1], size, 0), (got[2], size, index), (got[3], size, index)]


def local_places(positions):
    if not paired():
        return positions
    devices = jnp.array([2 * along + near for near in (0, 1) for along in (0, 1) for _ in (0, 1)])
    blocks = (lax.axis_index(CTX) ^ devices) * 2 + (
        lax.axis_index(TP) ^ jnp.array([0, 1] * 4)
    )
    return positions.reshape(8, -1)[blocks].reshape(-1)


def hold(values, *after):
    return lax.optimization_barrier((values,) + after)[0]


def tick(live):
    vars(live).update(lax.optimization_barrier(dict(vars(live))))


def small_call(name, kernel, place, items, shapes, kind):
    vmem = pl.BlockSpec(memory_space=pltpu.VMEM)
    return pl.pallas_call(
        kernel,
        in_specs=[pl.BlockSpec(memory_space=pltpu.SMEM)] + [vmem] * len(items),
        out_specs=[vmem] * len(shapes),
        out_shape=[jax.ShapeDtypeStruct(shape, kind) for shape in shapes],
        compiler_params=params(),
        cost_estimate=NO_COST,
        name=name,
    )(place, *items)


def small_call(name, kernel, items, shapes, kind):
    vmem = pl.BlockSpec(memory_space=pltpu.VMEM)
    return pl.pallas_call(
        kernel,
        in_specs=[vmem] * len(items),
        out_specs=[vmem] * len(shapes),
        out_shape=[jax.ShapeDtypeStruct(shape, kind) for shape in shapes],
        compiler_params=params(),
        cost_estimate=NO_COST,
        name=name,
    )(*items)


def pieces(kind, *sources):
    parts = lax.axis_size(CTX)
    rows = sources[-1].shape[0 if kind == "up" else 1]
    width = sources[-1].shape[1 if kind == "up" else 0] // parts
    columns = 4 * width if kind == "attention" else width
    if width % PAIR:
        items = jnp.stack([*sources[0], sources[1].T]).reshape(4, rows, parts, width)
        return jnp.transpose(items, (2, 1, 0, 3)).reshape(parts, rows, columns)

    def kernel(*refs):
        *sources, target = refs
        for r in range(parts):
            here = slice(r * width, (r + 1) * width)
            if kind == "attention":
                for which in range(3):
                    target[r, :, which * width : (which + 1) * width] = sources[0][which, :, here]
                target[r, :, 3 * width :] = sources[1][here, :].T
            elif kind == "up":
                target[r] = sources[0][:, here]
            else:
                target[r] = sources[0][here, :].T

    return small_call("pieces", kernel, sources, [(parts, rows, columns)], sources[0].dtype)[0]


def trade(sent):
    return lax.all_to_all(sent, CTX, 0, 0, tiled=True)


def gather_rows_of(sent):
    got = trade(sent)
    return got.reshape(-1, got.shape[2])


def trade_back(*summed):
    parts = lax.axis_size(CTX)
    split = [item.reshape(parts, -1, item.shape[1]) for item in summed]
    return trade(split[0] if len(split) == 1 else jnp.concatenate(split, axis=1))


def finish(received, kind, index=0, count=1):
    parts, rows, columns = received.shape
    rows //= count
    width = columns // 4 if kind == "attention" else columns
    if width % PAIR:
        items = received[:, index * rows : (index + 1) * rows].astype(jnp.float32)
        items = jnp.transpose(items.reshape(parts, rows, 4, width), (2, 1, 0, 3))
        items = items.reshape(4, rows, parts * width)
        return items[:3], items[3].T

    def kernel(source, *targets):
        for r in range(parts):
            here = slice(r * width, (r + 1) * width)
            values = source[r, index * rows : (index + 1) * rows].astype(jnp.float32)
            if kind == "attention":
                for which in range(3):
                    targets[0][which, :, here] = values[:, which * width : (which + 1) * width]
                targets[1][here, :] = values[:, 3 * width :].T
            elif kind == "up":
                targets[0][:, here] = values
            else:
                targets[0][here, :] = values.T

    shapes = {
        "attention": [(3, rows, parts * width), (parts * width, rows)],
        "up": [(rows, parts * width)],
        "down": [(parts * width, rows)],
    }[kind]
    return small_call("finish", kernel, [received], shapes, jnp.float32)


def unit_of(tokens):
    inputs = tokens.astype(jnp.float32)
    centered = inputs - jnp.mean(inputs, axis=-1, keepdims=True)
    inverse = lax.rsqrt(jnp.mean(centered * centered, axis=-1, keepdims=True) + EPSILON)
    return centered * inverse, inverse


def tokens_grad_of(tokens, cotangent, norm_gain, *refs):
    unit, inverse = unit_of(tokens[...])
    grads = cotangent[...].astype(jnp.float32)
    normed_grad = sum_of(*refs)
    unit_grad = normed_grad * norm_gain[...].astype(jnp.float32)
    tokens_grad = grads + inverse * (
        unit_grad
        - jnp.mean(unit_grad, axis=-1, keepdims=True)
        - unit * jnp.mean(unit_grad * unit, axis=-1, keepdims=True)
    )
    sums = [
        jnp.sum(item, axis=0, keepdims=True) for item in (normed_grad * unit, normed_grad, grads)
    ]
    return [tokens_grad, jnp.concatenate(sums, axis=0)]


def on_device(
    tokens,
    positions,
    cotangent,
    norm_gain,
    norm_bias,
    qkv_weight,
    qkv_bias,
    out_weight,
    out_bias,
    up_weight,
    up_bias,
    down_weight,
    down_bias,
):
    parts = lax.axis_size(CTX)
    part = lax.axis_index(CTX)
    width = qkv_weight.shape[2] // parts
    units = up_weight.shape[1] // parts

    unit_rows, _ = unit_of(tokens[0])
    normed_own = (unit_rows * norm_gain + norm_bias).astype(jnp.bfloat16)

    place = lax.axis_index(FSDP)
    turns = jnp.array(TURNS, jnp.int32)[place]
    place = place.astype(jnp.int32).reshape(1)

    def first_grad(columns, *products):
        return grad_pieces(products, turns, 0, 1, columns)[0]

    def later_grads(columns, *products):
        return [grad_pieces(products, turns, 1, 3, columns)]

    live = types.SimpleNamespace(
        attention=gather_rows_of(pieces("attention", jnp.swapaxes(qkv_weight, 0, 1), out_weight)),
        rows=jnp.concatenate([normed_own, cotangent[0]], axis=0),
        tokens=tokens[0],
        cotangent=cotangent[0],
        weights=(up_weight, down_weight),
        positions=positions,
    )
    tick(live)
    live.attention = square_first(live.attention)
    live.rows = gather_first(live.rows)
    live.places = local_places(live.positions)
    live.turning = turning(live.places)
    tick(live)
    live.attention = square_second(live.attention)
    live.normed, live.grads = gather_third(gather_second(live.rows))
    live.up = gather_rows_of(pieces("up", live.weights[0]))
    live.down = pieces("down", live.weights[1])
    del live.rows
    tick(live)
    live.up = square_first(live.up)
    live.down = gather_rows_of(live.down)
    live.attention = in_square(live.attention, place)
    qkv_part = lax.dynamic_slice_in_dim(qkv_bias, part * width, width, 1).astype(jnp.float32)
    padded = width + -width % PAIR
    pairs = padded // PAIR
    projected = row_call(
        "project",
        project_kernel,
        [live.normed, live.grads, *live.turning],
        [live.attention, qkv_part.reshape(1, 3 * width)],
        [(padded, jnp.bfloat16)] * 3
        + [(padded, jnp.bfloat16, True)] * 2
        + [(padded, jnp.bfloat16), (padded, jnp.bfloat16, True)],
        mebibytes=60,
    )
    groups = live.places[::GROUP] // GROUP
    order = jnp.sum(
        jnp.where(
            groups[None, :] == jnp.arange(groups.shape[0])[:, None],
            jnp.arange(groups.shape[0])[None, :],
            0,
        ),
        axis=1,
    ).astype(jnp.int32)
    heads = ()
    for pair in range(pairs // 2):
        heads = attention(order, projected, live.turning, pair, heads)
    live.projected, live.order, live.heads = projected, order, heads
    tick(live)
    live.up = square_second(live.up)
    live.down = spread_first(live.down)
    heads = live.heads
    for pair in range(pairs // 2, pairs):
        heads = attention(live.order, live.projected, live.turning, pair, heads)
    live.heads = heads
    attended, *head_grads = live.heads
    head_products = ((live.normed, head_grads), (live.grads, [attended]))
    live.head_parts = [first_grad(width, *head_products)]
    tick(live)
    live.down = spread_second(live.down)
    live.head_sum = reduce_first(live.head_parts)
    attended, *head_grads = live.heads
    head_products = ((live.normed, head_grads), (live.grads, [attended]))
    live.up = in_square(live.up, place)
    own_bias = lax.dynamic_slice_in_dim(up_bias, part * units, units, 0).astype(jnp.float32)
    live.activated, live.slope = row_call(
        "hidden",
        hidden_kernel,
        [live.normed],
        [live.up, own_bias[None]],
        [(units, jnp.bfloat16), (units, jnp.bfloat16)],
    )
    live.head_parts = live.head_parts + later_grads(width, *head_products)
    tick(live)
    live.down = spread_third(live.down)
    live.head_sum = reduce_second([(live.head_parts, live.head_sum)], place)
    down_products = (live.grads, [live.activated])
    live.down_parts = [first_grad(units, down_products)] + later_grads(units, down_products)
    columns = [(0, slice(which * width, (which + 1) * width)) for which in range(4)]
    live.normed_part, live.qkv_sums = back(
        list(live.heads[1:]), columns[:3], [live.attention], summing=True
    )
    tick(live)
    live.head_sum = reduce_third(live.head_parts, live.head_sum, place)
    live.down_sum = reduce_first(live.down_parts)
    live.down = in_line(live.down)
    live.hidden_grad, live.up_sums = row_call(
        "hidden_grad",
        hidden_grad_kernel,
        [live.grads, live.slope],
        [live.down],
        [(units, jnp.bfloat16), (1, units, jnp.float32, None)],
    )
    everything = (0, slice(0, units))
    live.branch = back(
        [live.activated, live.heads[0]],
        [everything, (1, columns[3][1])],
        [live.down, live.attention],
        halves=True,
    )
    tick(live)
    live.down_sum = reduce_second([(live.down_parts, live.down_sum)], place)
    far, near = live.branch
    (live.branch,) = scatter_third(*scatter_second(scatter_first(near, far)))
    up_products = (live.normed, [live.hidden_grad])
    live.up_parts = [first_grad(units, up_products)]
    live.up_sum = reduce_first(live.up_parts)
    live.up_parts = live.up_parts + later_grads(units, up_products)
    live.normed_part = back(
        [live.hidden_grad], [everything], [live.up], live.normed_part, halves=True
    )
    tick(live)
    live.down_sum = reduce_third(
        live.down_parts, live.down_sum, place, (live.up_parts, live.up_sum)
    )
    far, near = live.normed_part
    (live.normed_part,) = scatter_third(*scatter_second(scatter_first(near, far)))
    live.head_sum = reduce_last(live.head_parts, live.head_sum)
    live.sums = jnp.concatenate(
        [
            lax.dynamic_update_slice_in_dim(
                jnp.zeros(qkv_bias.shape, jnp.float32),
                live.qkv_sums[:, :width],
                part * width,
                1,
            ).reshape(-1),
            lax.dynamic_update_slice_in_dim(
                jnp.zeros(up_bias.shape, jnp.float32), live.up_sums[0], part * units, 0
            ),
        ]
    )
    tick(live)
    second = [(item, live.up_parts[0].shape[0], 1) for item in live.down_sum]
    live.up_sum = reduce_third(live.up_parts, second, place)
    down_sum = reduce_last(live.down_parts, live.down_sum)
    live.both = trade_back(live.head_sum, down_sum)
    live.tokens_grad, norm_sums = pointwise(
        "tokens_grad",
        tokens_grad_of,
        [],
        [live.tokens, live.cotangent, norm_gain[None]] + addends(live.normed_part, 0),
        [(tokens.shape[1:], jnp.float32), ((3, D), jnp.float32)],
    )
    (live.layer_output,) = pointwise(
        "layer_output",
        lambda tokens, *refs: [sum_of(tokens, *refs)],
        [],
        [live.tokens, out_bias[None], down_bias[None]] + addends(live.branch, 0),
        [(tokens.shape[1:], jnp.bfloat16)],
    )
    norm_sums = total(norm_sums.reshape(-1), TP)
    live.sums = jnp.concatenate([live.sums, norm_sums])
    tick(live)
    up_sum = trade_back(reduce_last(live.up_parts, live.up_sum))
    (down_weight_grad,) = finish(live.both, "down", 1, 2)
    qkv_weight_grad, out_weight_grad = finish(live.both, "attention", 0, 2)
    sums = total(total(live.sums, FSDP), CTX)
    (up_weight_grad,) = finish(up_sum, "up")
    bias_sums = sums[: -3 * D]
    norm_sums = sums[-3 * D :].reshape(3, D)
    tokens_grad, layer_output = live.tokens_grad, live.layer_output

    return (
        layer_output[None],
        tokens_grad[None],
        norm_sums[0],
        norm_sums[1],
        jnp.swapaxes(qkv_weight_grad, 0, 1),
        bias_sums[: qkv_bias.size].reshape(qkv_bias.shape),
        out_weight_grad,
        norm_sums[2],
        up_weight_grad,
        bias_sums[qkv_bias.size :],
        down_weight_grad,
        norm_sums[2],
    )


def solution(mesh):
    rows = P(FSDP, (CTX, TP), None)
    placed = (
        rows,
        P(),
        rows,
        P(),
        P(),
        P((FSDP, CTX), None, TP),
        P(None, TP),
        P(TP, (FSDP, CTX)),
        P(),
        P((FSDP, CTX), TP),
        P(TP),
        P(TP, (FSDP, CTX)),
        P(),
    )
    return jax.shard_map(
        on_device,
        mesh=mesh,
        in_specs=placed,
        out_specs=(
            rows,
            rows,
            P(),
            P(),
            P((FSDP, CTX), None, TP),
            P(None, TP),
            P(TP, (FSDP, CTX)),
            P(),
            P((FSDP, CTX), TP),
            P(TP),
            P(TP, (FSDP, CTX)),
            P(),
        ),
        check_vma=False,
    )
```

```python
import functools
import types

import jax
import jax.numpy as jnp
from jax import lax
from jax.experimental import pallas as pl
from jax.experimental.pallas import tpu as pltpu
from jax.sharding import PartitionSpec as P

FSDP, CTX, TP = "fsdp", "ctx", "tp"

D = 2048
HEAD_DIM = 64
ROT = 32
GROUP = 256
PAIR = 2 * HEAD_DIM

EPSILON = 1e-05
MASKED = -1e30
GELU_SLOPE = 0.7978845608028654
GELU_CUBE = 0.044715


TURNS = ((3, 2, 1, 0), (3, 2, 0, 1), (0, 1, 3, 2), (0, 1, 2, 3))

NT = (((1,), (1,)), ((), ()))
NN = (((1,), (0,)), ((), ()))


NO_COST = pl.CostEstimate(flops=0, bytes_accessed=0, transcendentals=0)


def params(mebibytes=48):
    return pltpu.CompilerParams(vmem_limit_bytes=mebibytes * 1024 * 1024)


def dot(left, right, dims=NN):
    return lax.dot_general(left, right, dims, preferred_element_type=jnp.float32)


def turning(places):
    halfway = ROT // 2
    lane = jnp.arange(PAIR) % HEAD_DIM
    frequencies = 10000.0 ** (-((lane % halfway).astype(jnp.float32) * 2.0 / ROT))
    frequencies = jnp.where(lane < ROT, frequencies, 0.0)
    angles = places.astype(jnp.float32)[:, None] * frequencies[None, :]
    return jnp.cos(angles), jnp.sin(angles) * jnp.where(lane < halfway, -1.0, 1.0)[None, :]


def turn(values, cosine, sine):
    halfway = ROT // 2
    lane = lax.broadcasted_iota(jnp.int32, values.shape, 1) % HEAD_DIM
    partner = jnp.where(
        lane < halfway,
        pltpu.roll(values, PAIR - halfway, 1),
        pltpu.roll(values, halfway, 1),
    )
    return values * cosine + partner * sine


def attention_kernel(
    order,
    query_in,
    key_all,
    value_all,
    key_turned,
    value_turned,
    grad_in,
    grad_turned,
    cosine_all,
    sine_all,
    *refs,
):
    (attended_out, query_out, key_out, value_out, key_total, value_total, strip) = refs[-7:]
    groups, group = pl.num_programs(0), pl.program_id(0)
    tall, wide = strip.shape[1:]
    blocks = tall // GROUP

    def rows(place):
        return pl.ds(pl.multiple_of(order[place] * GROUP, GROUP), GROUP)

    def load(ref, step):
        return jnp.concatenate([ref[rows(step * blocks + at), :] for at in range(blocks)], axis=0)

    def load_turned(ref, step, head):
        here = slice(head * HEAD_DIM, (head + 1) * HEAD_DIM)
        return jnp.concatenate([ref[here, rows(step * blocks + at)] for at in range(blocks)], axis=1)

    def put(ref, step, values):
        for at in range(blocks):
            ref[rows(step * blocks + at), :] += values[at * GROUP : (at + 1) * GROUP]

    def fold(tile):
        return tile.reshape(tall // 8, 8, wide)

    def pair_up(values):
        first = lax.broadcasted_iota(jnp.int32, (GROUP, PAIR), 1) < HEAD_DIM
        nothing = jnp.zeros((GROUP, PAIR), jnp.bfloat16)
        return jnp.concatenate(
            [jnp.where(first, values, nothing), jnp.where(first, nothing, values)], axis=0
        )

    @pl.when(group == 0)
    def _():
        key_total[...] = jnp.zeros_like(key_total)
        value_total[...] = jnp.zeros_like(value_total)

    query_pair, grad_pair = pair_up(query_in[...]), pair_up(grad_in[...])
    steps = (group + blocks) // blocks
    ahead = lax.broadcasted_iota(jnp.int32, (tall, wide), 0) - (
        lax.broadcasted_iota(jnp.int32, (tall, wide), 1) % GROUP
    )

    def scores(step, most):
        tile = dot(load(key_all, step), query_pair, NT)
        tile = jnp.where(ahead <= (group - step * blocks) * GROUP, tile, MASKED)
        strip[step] = tile
        return jnp.maximum(most, jnp.max(fold(tile), axis=0))

    most = lax.fori_loop(0, steps, scores, jnp.full((8, wide), MASKED, jnp.float32))
    most = jnp.max(most, axis=0, keepdims=True)

    def weigh(step, carry):
        total, upper, lower = carry
        tile = jnp.exp(strip[step] - most)
        strip[step] = tile
        low = tile.astype(jnp.bfloat16)
        upper = upper + dot(load_turned(value_turned, step, 0), low[:, :GROUP])
        lower = lower + dot(load_turned(value_turned, step, 1), low[:, GROUP:])
        return total + jnp.sum(fold(tile), axis=0), upper, lower

    blank = jnp.zeros((HEAD_DIM, GROUP), jnp.float32)
    total, upper, lower = lax.fori_loop(
        0, steps, weigh, (jnp.zeros((8, wide), jnp.float32), blank, blank)
    )
    share = 1.0 / jnp.sum(total, axis=0, keepdims=True)
    upper = upper * share[:, :GROUP]
    lower = lower * share[:, GROUP:]
    attended_out[...] = jnp.concatenate([upper, lower], axis=0).astype(jnp.bfloat16).T
    grad = grad_turned[...].astype(jnp.float32)
    delta = jnp.concatenate(
        [
            jnp.sum(upper * grad[:HEAD_DIM], axis=0, keepdims=True),
            jnp.sum(lower * grad[HEAD_DIM:], axis=0, keepdims=True),
        ],
        axis=1,
    )

    def back(step, carry):
        upper, lower = carry
        part = strip[step] * share
        put(value_total, step, dot(part.astype(jnp.bfloat16), grad_pair))
        part = part * (dot(load(value_all, step), grad_pair, NT) - delta)
        low = part.astype(jnp.bfloat16)
        put(key_total, step, dot(low, query_pair))
        upper = upper + dot(load_turned(key_turned, step, 0), low[:, :GROUP])
        lower = lower + dot(load_turned(key_turned, step, 1), low[:, GROUP:])
        return upper, lower

    upper, lower = lax.fori_loop(0, steps, back, (blank, blank))
    own = rows(group)
    query_grad = jnp.concatenate([upper, lower], axis=0).T * HEAD_DIM ** (-0.5)
    query_out[...] = turn(query_grad, cosine_all[own, :], -sine_all[own, :]).astype(jnp.bfloat16)

    @pl.when(group == groups - 1)
    def _():
        key_grad = turn(key_total[...], cosine_all[...], -sine_all[...])
        key_out[...] = key_grad.astype(jnp.bfloat16)
        value_out[...] = value_total[...].astype(jnp.bfloat16)


def attention(order, projected, tables, pair, earlier=()):
    length, width = projected[0].shape
    groups = length // GROUP
    block = pl.BlockSpec((GROUP, PAIR), lambda group, order: (order[group], pair))
    turned_block = pl.BlockSpec((PAIR, GROUP), lambda group, order: (pair, order[group]))
    column = pl.BlockSpec((length, PAIR), lambda group, order: (0, pair))
    turned_column = pl.BlockSpec((PAIR, length), lambda group, order: (pair, 0))
    table = pl.BlockSpec((length, PAIR), lambda group, order: (0, 0))
    specs = [block, column, column, turned_column, turned_column, block, turned_block, table, table]
    return pl.pallas_call(
        attention_kernel,
        grid_spec=pltpu.PrefetchScalarGridSpec(
            num_scalar_prefetch=1,
            grid=(groups,),
            in_specs=specs + [pl.BlockSpec(memory_space=pl.ANY)] * len(earlier),
            out_specs=[block, block, column, column],
            scratch_shapes=[
                pltpu.VMEM((length, PAIR), jnp.float32),
                pltpu.VMEM((length, PAIR), jnp.float32),
                pltpu.VMEM((groups // 2, 2 * GROUP, 2 * GROUP), jnp.float32),
            ],
        ),
        out_shape=[jax.ShapeDtypeStruct((length, width), jnp.bfloat16)] * 4,
        input_output_aliases={1 + len(specs) + at: at for at in range(len(earlier))},
        compiler_params=params(60),
        cost_estimate=NO_COST,
        name=f"attention_{pair}",
    )(order, *projected, *tables, *earlier)


ROWS = 512


def chunk(place, which, size):
    return pl.ds(pl.multiple_of(place[which] * size, size), size)


def row_call(name, kernel, row_inputs, full_inputs, outputs, size=ROWS, turn=0, mebibytes=48):
    count = row_inputs[0].shape[0] // size
    rows = count * size

    def out(item):
        if len(item) == 4 and item[3] is None:
            shape, spec = item[:2], pl.BlockSpec(item[:2], lambda at: (0, 0))
        elif len(item) == 4:
            shape = ((item[3] - item[2]) * size, item[0])
            spec = pl.BlockSpec(
                (size, item[0]),
                lambda at: (jnp.clip(at, item[2], item[3] - 1) - item[2], 0),
            )
        elif len(item) == 3:
            shape = (item[0], rows)
            spec = pl.BlockSpec((item[0], size), lambda at: (0, at))
        else:
            shape = (rows, item[0])
            spec = pl.BlockSpec((size, item[0]), lambda at: (at, 0))
        kind = item[2] if len(item) == 4 and item[3] is None else item[1]
        return spec, jax.ShapeDtypeStruct(shape, kind)

    return pl.pallas_call(
        kernel,
        grid=(count,),
        in_specs=[
            pl.BlockSpec((size, item.shape[1]), lambda at: (lax.rem(at + turn, count), 0))
            for item in row_inputs
        ]
        + [pl.BlockSpec(item.shape, lambda at: (0, 0)) for item in full_inputs],
        out_specs=[out(item)[0] for item in outputs],
        out_shape=[out(item)[1] for item in outputs],
        compiler_params=params(mebibytes),
        cost_estimate=NO_COST,
        name=name,
    )(*row_inputs, *full_inputs)


def add_up(target, at, values):
    part = jnp.sum(values.astype(jnp.float32), axis=0, keepdims=True)

    @pl.when(pl.program_id(0) == 0)
    def _():
        target[at : at + 1, :] = part

    @pl.when(pl.program_id(0) > 0)
    def _():
        target[at : at + 1, :] += part


def project_kernel(normed, grads, cosine, sine, weight, bias, *refs):
    query, key, value, key_turned, value_turned, out_grads, grads_turned = refs
    width = weight.shape[1] // 4
    mixed = dot(normed[...], weight[:, : 3 * width]) + bias[...]
    parts = [mixed[:, which * width : (which + 1) * width] for which in range(3)]
    parts.append(dot(grads[...], weight[:, 3 * width :]))
    for pair in range(-(-width // PAIR)):
        here = slice(pair * PAIR, (pair + 1) * PAIR)
        items = [part[:, here] for part in parts]
        if width < PAIR:
            nothing = jnp.zeros((ROWS, PAIR - width), jnp.float32)
            items = [jnp.concatenate([item, nothing], axis=1) for item in items]
        turned = [turn(item, cosine[...], sine[...]) for item in items[:2]]
        low = turned[0].astype(jnp.bfloat16).astype(jnp.float32) * HEAD_DIM ** (-0.5)
        query[:, here] = low.astype(jnp.bfloat16)
        for target, target_turned, item in (
            (key, key_turned, turned[1]),
            (value, value_turned, items[2]),
            (out_grads, grads_turned, items[3]),
        ):
            low = item.astype(jnp.bfloat16)
            target[:, here] = low
            target_turned[here, :] = low.T


def hidden_kernel(normed, weight, bias, activated, slope):
    hidden = dot(normed[...], weight[...]) + bias[...]
    square = hidden * hidden
    bent = jnp.tanh(GELU_SLOPE * hidden * (1.0 + GELU_CUBE * square))
    half = 0.5 * (1.0 + bent)
    activated[...] = (hidden * half).astype(jnp.bfloat16)
    slope[...] = (
        half
        + 0.5 * GELU_SLOPE * hidden * (1.0 - bent * bent) * (1.0 + 3.0 * GELU_CUBE * square)
    ).astype(jnp.bfloat16)


def hidden_grad_kernel(grads, slope, weight, target, sums):
    low = (dot(grads[...], weight[...]) * slope[...].astype(jnp.float32)).astype(jnp.bfloat16)
    target[...] = low
    add_up(sums, 0, low)


def back_kernel(columns, start, summing, halves, *refs):
    lefts = refs[: len(columns)]
    weights, outs = refs[len(columns) + start : -1 - summing - halves], refs[-1 - summing - halves :]
    result = refs[len(columns)][...].astype(jnp.float32) if start else None
    for left, (which, here) in zip(lefts, columns):
        part = dot(left[:, : here.stop - here.start], weights[which][:, here], NT)
        result = part if result is None else result + part
    if halves:
        early = pl.program_id(0) < pl.num_programs(0) // 2

        @pl.when(early)
        def _():
            outs[0][...] = result.astype(jnp.bfloat16)

        @pl.when(jnp.logical_not(early))
        def _():
            outs[1][...] = result.astype(jnp.bfloat16)

    else:
        outs[0][...] = result.astype(jnp.bfloat16)
    if summing:
        for at, left in enumerate(lefts):
            add_up(outs[1], at, left[...])


def back(lefts, columns, weights, start=None, halves=False, summing=False):
    size = ROWS
    count = lefts[0].shape[0] // size
    starts = [] if start is None else [start]
    outputs = [(weights[0].shape[0], jnp.bfloat16)]
    if halves:
        outputs = [outputs[0] + (0, count // 2), outputs[0] + (count // 2, count)]
    if summing:
        outputs.append((len(lefts), lefts[0].shape[1], jnp.float32, None))
    got = row_call(
        "back",
        functools.partial(back_kernel, columns, len(starts), int(summing), int(halves)),
        lefts + starts,
        weights,
        outputs,
        size,
        count // 2 if halves else 0,
    )
    return got if summing or halves else got[0]


def grad_kernel(counts, width, turns, *refs):
    target = refs[-1]
    refs = list(refs[:-1])
    at = 0
    for count in counts:
        left = refs.pop(0)
        for _ in range(count):
            right = refs.pop(0)
            columns = min(width, right.shape[1])
            target[0, :, at : at + columns] = dot(
                left[...], right[:, :columns], (((0,), (0,)), ((), ()))
            ).astype(jnp.bfloat16)
            at += columns


def grad_pieces(products, turns, first, count, width, mebibytes=48):
    size = lax.axis_size(FSDP)
    specs, items, columns = [], [], 0
    for left, rights in products:
        rows = left.shape[1] // size
        specs.append(
            pl.BlockSpec((left.shape[0], rows), lambda at, turns: (0, turns[first + at]))
        )
        specs += [pl.BlockSpec(item.shape, lambda at, turns: (0, 0)) for item in rights]
        items += [left, *rights]
        columns += sum(min(width, item.shape[1]) for item in rights)
    return pl.pallas_call(
        functools.partial(grad_kernel, [len(rights) for _, rights in products], width),
        grid_spec=pltpu.PrefetchScalarGridSpec(
            num_scalar_prefetch=1,
            grid=(count,),
            in_specs=specs,
            out_specs=pl.BlockSpec((1, rows, columns), lambda at, turns: (at, 0, 0)),
        ),
        out_shape=jax.ShapeDtypeStruct((count, rows, columns), jnp.bfloat16),
        compiler_params=params(mebibytes),
        cost_estimate=NO_COST,
        name=f"grad_{first}",
    )(turns, *items)


def pointwise(name, function, scalars, inputs, outputs):
    def spec(item):
        if not isinstance(item, tuple):
            return pl.BlockSpec(item.shape, lambda at, n=item.ndim: (0,) * n)
        array, rows, index = item
        return pl.BlockSpec(
            (rows,) + array.shape[1:], lambda at, n=array.ndim, index=index: (index,) + (0,) * (n - 1)
        )

    def kernel(*refs):
        count = len(scalars) + len(inputs)
        for target, value in zip(refs[count:], function(*refs[:count])):
            target[...] = value.astype(target.dtype)

    return pl.pallas_call(
        kernel,
        grid=(1,),
        in_specs=[pl.BlockSpec(memory_space=pltpu.SMEM)] * len(scalars) + [spec(i) for i in inputs],
        out_specs=[pl.BlockSpec(shape, lambda at, n=len(shape): (0,) * n) for shape, _ in outputs],
        out_shape=[jax.ShapeDtypeStruct(shape, kind) for shape, kind in outputs],
        compiler_params=params(),
        cost_estimate=NO_COST,
        name=name,
    )(*scalars, *[item[0] if isinstance(item, tuple) else item for item in inputs])


def stack_kernel(parts, *refs):
    *sources, target, arrived = refs
    copies = [
        pltpu.make_async_copy(
            source.at[pl.ds(first, rows)], target.at[pl.ds(start, rows)], arrived.at[at]
        )
        for at, (source, (first, rows, start)) in enumerate(zip(sources, parts))
    ]
    for copy in copies:
        copy.start()
    for copy in copies:
        copy.wait()


def stack(parts, rows):
    array = parts[0][0]
    return pl.pallas_call(
        functools.partial(stack_kernel, [part[1:] for part in parts]),
        in_specs=[pl.BlockSpec(memory_space=pl.ANY)] * len(parts),
        out_specs=pl.BlockSpec(memory_space=pltpu.VMEM),
        out_shape=jax.ShapeDtypeStruct((rows, array.shape[1]), array.dtype),
        scratch_shapes=[pltpu.SemaphoreType.DMA((len(parts),))],
        compiler_params=params(),
        cost_estimate=NO_COST,
        name="stack",
    )(*[part[0] for part in parts])


def fill_kernel(starts, *refs):
    count = len(starts)
    sources, target = refs[:count], refs[count + 1]
    held, arrived, left = refs[count + 2 :]
    rows = [source.shape[0] for source in sources]
    slots = [pl.ds(sum(rows[:at]), rows[at]) for at in range(count)]
    inward = [
        pltpu.make_async_copy(source, held.at[slots[at]], arrived.at[at])
        for at, source in enumerate(sources)
    ]
    outward = [
        pltpu.make_async_copy(held.at[slots[at]], target.at[pl.ds(start, rows[at])], left.at[at])
        for at, start in enumerate(starts)
    ]
    for copy in inward:
        copy.start()
    for first, second in zip(inward, outward):
        first.wait()
        second.start()
    for copy in outward:
        copy.wait()


def fill(target, parts):
    anywhere = pl.BlockSpec(memory_space=pl.ANY)
    count = len(parts)
    rows = sum(array.shape[0] for array, _ in parts)
    return pl.pallas_call(
        functools.partial(fill_kernel, [start for _, start in parts]),
        in_specs=[anywhere] * (count + 1),
        out_specs=anywhere,
        out_shape=jax.ShapeDtypeStruct(target.shape, target.dtype),
        scratch_shapes=[
            pltpu.VMEM((rows, target.shape[1]), target.dtype),
            pltpu.SemaphoreType.DMA((count,)),
            pltpu.SemaphoreType.DMA((count,)),
        ],
        input_output_aliases={count: 0},
        compiler_params=params(),
        cost_estimate=NO_COST,
        name="fill",
    )(*[array for array, _ in parts], target)


def line_kernel(place, *refs):
    own, up_one, down_one, up_two, down_two, up_three, down_three, target, arrived = refs
    rows = own.shape[0]
    for where, sources in enumerate(
        (
            (own, down_one, down_two, down_three),
            (up_one, own, down_one, down_two),
            (up_two, up_one, own, down_one),
            (up_three, up_two, up_one, own),
        )
    ):

        @pl.when(place[0] == where)
        def _(sources=sources):
            copies = [
                pltpu.make_async_copy(source, target.at[pl.ds(at * rows, rows)], arrived.at[at])
                for at, source in enumerate(sources)
            ]
            for copy in copies:
                copy.start()
            for copy in copies:
                copy.wait()


def in_line(got):
    anywhere = pl.BlockSpec(memory_space=pl.ANY)
    rows, columns = got[0].shape
    return pl.pallas_call(
        line_kernel,
        in_specs=[pl.BlockSpec(memory_space=pltpu.SMEM)] + [anywhere] * len(got),
        out_specs=pl.BlockSpec(memory_space=pltpu.VMEM),
        out_shape=jax.ShapeDtypeStruct((4 * rows, columns), got[0].dtype),
        scratch_shapes=[pltpu.SemaphoreType.DMA((4,))],
        compiler_params=params(),
        cost_estimate=NO_COST,
        name="in_line",
    )(lax.axis_index(FSDP).astype(jnp.int32).reshape(1), *got)


def swap(values, axis, bit):
    size = lax.axis_size(axis)
    with jax.named_scope(f"{axis}_{bit}"):
        return lax.ppermute(values, axis, [(place, place ^ bit) for place in range(size)])


def total(values, axis):
    bit = 1
    while bit < lax.axis_size(axis):
        values = values + swap(values, axis, bit)
        bit *= 2
    return values


def move(values, pairs):
    with jax.named_scope("line"):
        return lax.ppermute(values, FSDP, pairs)


def spread_first(own):
    return [own, move(own, [(0, 1), (1, 2), (2, 3)]), move(own, [(1, 0), (2, 1), (3, 2)])]


def spread_second(got):
    return got + [move(got[1], [(1, 2), (2, 3)]), move(got[2], [(1, 0), (2, 1)])]


def spread_third(got):
    return got + [move(got[3], [(2, 3)]), move(got[4], [(1, 0)])]


def reduce_first(parts):
    return move(parts[0], [(0, 1), (3, 2)])


def square_first(own):
    return [own, swap(own, FSDP, 1), swap(own, FSDP, 2)]


def square_second(got):
    return got + [swap(got[2], FSDP, 1)]


def square_kernel(place, *refs):
    *sources, target, arrived = refs
    rows = sources[0].shape[0]
    copies = []
    for which, source in enumerate(sources):
        here = pl.ds(pl.multiple_of((place[0] ^ which) * rows, rows), rows)
        copies.append(pltpu.make_async_copy(source, target.at[here], arrived.at[which]))
    for copy in copies:
        copy.start()
    for copy in copies:
        copy.wait()


def in_square(got, place):
    rows, columns = got[0].shape
    return pl.pallas_call(
        square_kernel,
        in_specs=[pl.BlockSpec(memory_space=pltpu.SMEM)]
        + [pl.BlockSpec(memory_space=pl.ANY)] * len(got),
        out_specs=pl.BlockSpec(memory_space=pltpu.VMEM),
        out_shape=jax.ShapeDtypeStruct((len(got) * rows, columns), got[0].dtype),
        scratch_shapes=[pltpu.SemaphoreType.DMA((len(got),))],
        compiler_params=params(),
        cost_estimate=NO_COST,
        name="in_square",
    )(place, *got)


UP, DOWN = [(0, 1), (1, 2), (2, 3)], [(1, 0), (2, 1), (3, 2)]


def second_of(place, first, second, got):
    ends = (place[0] == 0) | (place[0] == 3)
    return jnp.where(ends, sum_of(second)[0], sum_of(first) + got)


def third_of(place, second, third, upward, downward):
    one, two = sum_of(second)[0], sum_of(third)[0]
    return (
        jnp.where(place[0] == 1, one, two) + sum_of(upward),
        jnp.where(place[0] == 2, one, two) + sum_of(downward),
    )


def reduce_second(sums, place):
    inputs = []
    for (first, rest), got in sums:
        inputs += [first, (rest, 1, 0), got]
    rows, columns = sums[0][0][0].shape

    def choose(place, *refs):
        sent = [
            second_of(place, first, second, sum_of(got))
            for first, second, got in zip(refs[::3], refs[1::3], refs[2::3])
        ]
        return [jnp.concatenate(sent, axis=0)]

    sent = pointwise(
        "second", choose, [place], inputs, [((len(sums) * rows, columns), jnp.bfloat16)]
    )[0]
    return [move(sent, UP[:2]), move(sent, DOWN[1:])]


def reduce_third(parts, got, place, new=None):
    first, rest = parts
    rows, columns = first.shape
    shape = (rows if new is None else 2 * rows, columns)

    def choose(place, second, third, upward, downward, *others):
        sent = third_of(place, second, third, upward, downward)
        if not others:
            return sent
        first, second, got = others
        other = second_of(place, first, second, sum_of(got))
        return [jnp.concatenate([item, other], axis=0) for item in sent]

    inputs = [(rest, 1, 0), (rest, 1, 1), *got]
    if new is not None:
        inputs += [new[0][0], (new[0][1], 1, 0), new[1]]
    upward, downward = pointwise(
        "third", choose, [place], inputs, [(shape, jnp.bfloat16)] * 2
    )
    return [move(upward, UP), move(downward, DOWN)], upward


def reduce_last(parts, got, index=0):
    first, rest = parts
    return pointwise(
        "last",
        lambda last, *got: [sum_of(last)[0] + sum_of(*got)],
        [],
        [(rest, 1, 2)] + [(item, first.shape[0], index) for item in got],
        [(first.shape, jnp.bfloat16)],
    )[0]


def paired():
    return lax.axis_size(CTX) == 4 and lax.axis_size(TP) == 2


def gather_first(own):
    if not paired():
        return [own]
    return [own, swap(own, TP, 1), swap(own, CTX, 2), swap(own, CTX, 1)]


def gather_second(got):
    if not paired():
        return got
    size = got[0].shape[0] // 2
    corner = [swap(got[1][:size], CTX, 2), swap(got[2][size:], TP, 1)]
    return got + [swap(got[1], CTX, 1), swap(got[2], CTX, 1)] + corner


def gather_third(got):
    if not paired():
        size = got[0].shape[0] // 2
        return [
            lax.all_gather(item, (CTX, TP), axis=0, tiled=True)
            for item in (got[0][:size], got[0][size:])
        ]
    own, across, along, far_own, far_across, far_along, *corner = got
    size = corner[0].shape[0]
    half = size // 2
    results = []
    for which in range(2):
        sides = (own, across, along, None, far_own, far_across, far_along, None)
        parts = [
            (item, which * size, size, at * size)
            for at, item in enumerate(sides)
            if item is not None
        ]
        results.append(stack(parts, 8 * size))
    corner, results = lax.optimization_barrier((corner, results))
    for which in range(2):
        parts = [(corner[which], 3 * size)]
        for at in (0, half):
            parts.append((swap(corner[which][at : at + half], CTX, 1), 7 * size + at))
        results[which] = fill(results[which], parts)
    return results


def scatter_first(near, far):
    return [near, swap(far, CTX, 1) if paired() else far]


def sum_of(*refs):
    result = None
    for ref in refs:
        values = ref[...].astype(jnp.float32)
        result = values if result is None else result + values
    return result


def scatter_second(*all_got):
    if not paired():
        return list(all_got)
    size, columns = all_got[0][0].shape[0] // 4, all_got[0][0].shape[1]
    half = size // 2

    def corners(*refs):
        sums = [sum_of(*refs[at : at + 2]) for at in range(0, len(refs), 2)]
        return [
            jnp.concatenate([item[:half] for item in sums], axis=0),
            jnp.concatenate([item[half:] for item in sums], axis=0),
        ]

    sent = pointwise(
        "corners",
        corners,
        [],
        [(item, size, 3) for got in all_got for item in got],
        [((len(all_got) * half, columns), jnp.bfloat16)] * 2,
    )
    from_across, from_along = swap(sent[0], TP, 1), swap(sent[1], CTX, 2)
    return [got + [from_across, from_along] for got in all_got]


def scatter_third(*all_got):
    if not paired():
        return [
            [lax.psum_scatter(jnp.concatenate(got), (CTX, TP), scatter_dimension=0, tiled=True)]
            for got in all_got
        ]
    size, columns = all_got[0][0].shape[0] // 4, all_got[0][0].shape[1]
    half = size // 2

    def sides(*refs):
        acrosses, alongs = [], []
        for at in range(0, len(refs), 6):
            across, along = sum_of(*refs[at : at + 2]), sum_of(*refs[at + 2 : at + 4])
            from_across, from_along = refs[at + 4 : at + 6]
            acrosses += [across[:half], across[half:] + sum_of(from_along)]
            alongs += [along[:half] + sum_of(from_across), along[half:]]
        return [jnp.concatenate(acrosses, axis=0), jnp.concatenate(alongs, axis=0)]

    inputs = []
    for at, (near, far, from_across, from_along) in enumerate(all_got):
        inputs += [(near, size, 1), (far, size, 1), (near, size, 2), (far, size, 2)]
        inputs += [(from_across, half, at), (from_along, half, at)]
    across, along = pointwise(
        "sides", sides, [], inputs, [((len(all_got) * size, columns), jnp.bfloat16)] * 2
    )
    across, along = swap(across, TP, 1), swap(along, CTX, 2)
    return [[near, far, across, along] for near, far, *_ in all_got]


def addends(got, index):
    if not paired():
        return got
    size = got[0].shape[0] // 4
    return [(got[0], size, 0), (got[1], size, 0), (got[2], size, index), (got[3], size, index)]


def local_places(positions):
    if not paired():
        return positions
    devices = jnp.array([2 * along + near for near in (0, 1) for along in (0, 1) for _ in (0, 1)])
    blocks = (lax.axis_index(CTX) ^ devices) * 2 + (
        lax.axis_index(TP) ^ jnp.array([0, 1] * 4)
    )
    return positions.reshape(8, -1)[blocks].reshape(-1)


def hold(values, *after):
    return lax.optimization_barrier((values,) + after)[0]


def hold(values, *after):
    return lax.optimization_barrier((values,) + after)[0]


def tick(live):
    vars(live).update(lax.optimization_barrier(dict(vars(live))))


def small_call(name, kernel, place, items, shapes, kind):
    vmem = pl.BlockSpec(memory_space=pltpu.VMEM)
    return pl.pallas_call(
        kernel,
        in_specs=[pl.BlockSpec(memory_space=pltpu.SMEM)] + [vmem] * len(items),
        out_specs=[vmem] * len(shapes),
        out_shape=[jax.ShapeDtypeStruct(shape, kind) for shape in shapes],
        compiler_params=params(),
        cost_estimate=NO_COST,
        name=name,
    )(place, *items)


def small_call(name, kernel, items, shapes, kind, *places):
    vmem = pl.BlockSpec(memory_space=pltpu.VMEM)
    return pl.pallas_call(
        kernel,
        in_specs=[pl.BlockSpec(memory_space=pltpu.SMEM)] * len(places) + [vmem] * len(items),
        out_specs=[vmem] * len(shapes),
        out_shape=[jax.ShapeDtypeStruct(shape, kind) for shape in shapes],
        compiler_params=params(),
        cost_estimate=NO_COST,
        name=name,
    )(*places, *items)


def pieces(kind, *sources):
    parts = lax.axis_size(CTX)
    rows = sources[-1].shape[0 if kind == "up" else 1]
    width = sources[-1].shape[1 if kind == "up" else 0] // parts
    columns = 4 * width if kind == "attention" else width
    if width % PAIR:
        items = jnp.stack([*sources[0], sources[1].T]).reshape(4, rows, parts, width)
        return jnp.transpose(items, (2, 1, 0, 3)).reshape(parts, rows, columns)

    def kernel(*refs):
        *sources, target = refs
        for r in range(parts):
            here = slice(r * width, (r + 1) * width)
            if kind == "attention":
                for which in range(3):
                    target[r, :, which * width : (which + 1) * width] = sources[0][which, :, here]
                target[r, :, 3 * width :] = sources[1][here, :].T
            elif kind == "up":
                target[r] = sources[0][:, here]
            else:
                target[r] = sources[0][here, :].T

    return small_call("pieces", kernel, sources, [(parts, rows, columns)], sources[0].dtype)[0]


def near_pieces(kind, *sources):
    parts = lax.axis_size(CTX)
    place = lax.axis_index(CTX).astype(jnp.int32)
    sent = pieces(kind, *sources) if sources[-1].shape[0] // parts % PAIR else None
    if sent is not None:
        return [lax.dynamic_index_in_dim(sent, place ^ r, 0, False) for r in range(parts)]
    rows, width = sources[1].shape[1], sources[1].shape[0] // parts

    def kernel(place, qkv, out, *targets):
        for r, target in enumerate(targets):
            here = pl.ds(pl.multiple_of((place[0] ^ r) * width, width), width)
            for which in range(3):
                target[:, which * width : (which + 1) * width] = qkv[which, :, here]
            target[:, 3 * width :] = out[here, :].T

    return small_call(
        "pieces", kernel, sources, [(rows, 4 * width)] * parts, sources[0].dtype, place.reshape(1)
    )


def near_trade(sent):
    return [sent[0]] + [swap(sent[r], CTX, r) for r in range(1, len(sent))]


def laid(received):
    def kernel(place, *refs):
        *sources, target = refs
        for r, source in enumerate(sources):
            rows = source.shape[0]
            target[pl.ds(pl.multiple_of((place[0] ^ r) * rows, rows), rows), :] = source[...]

    rows, columns = received[0].shape
    place = lax.axis_index(CTX).astype(jnp.int32).reshape(1)
    shape = (len(received) * rows, columns)
    return small_call("laid", kernel, received, [shape], received[0].dtype, place)[0]


def trade(sent):
    return lax.all_to_all(sent, CTX, 0, 0, tiled=True)


def gather_rows_of(sent):
    got = trade(sent)
    return got.reshape(-1, got.shape[2])


def trade_back(summed):
    return trade(summed.reshape(lax.axis_size(CTX), -1, summed.shape[1]))


def last_beside(other, parts, got):
    first, rest = parts
    count = lax.axis_size(CTX)
    rows, columns = first.shape[0] // count, first.shape[1]

    def choose(other, last, *got):
        total = (sum_of(last)[0] + sum_of(*got)).reshape(count, rows, columns)
        return [jnp.concatenate([sum_of(other).reshape(count, rows, columns), total], axis=1)]

    return pointwise(
        "last",
        choose,
        [],
        [other, (rest, 1, 2)] + [(item, first.shape[0], 0) for item in got],
        [((count, 2 * rows, columns), jnp.bfloat16)],
    )[0]


def finish(received, kind, index=0, count=1):
    parts, rows, columns = received.shape
    rows //= count
    width = columns // 4 if kind == "attention" else columns
    if width % PAIR:
        items = received[:, index * rows : (index + 1) * rows].astype(jnp.float32)
        items = jnp.transpose(items.reshape(parts, rows, 4, width), (2, 1, 0, 3))
        items = items.reshape(4, rows, parts * width)
        return items[:3], items[3].T

    def kernel(source, *targets):
        for r in range(parts):
            here = slice(r * width, (r + 1) * width)
            values = source[r, index * rows : (index + 1) * rows].astype(jnp.float32)
            if kind == "attention":
                for which in range(3):
                    targets[0][which, :, here] = values[:, which * width : (which + 1) * width]
                targets[1][here, :] = values[:, 3 * width :].T
            elif kind == "up":
                targets[0][:, here] = values
            else:
                targets[0][here, :] = values.T

    shapes = {
        "attention": [(3, rows, parts * width), (parts * width, rows)],
        "up": [(rows, parts * width)],
        "down": [(parts * width, rows)],
    }[kind]
    return small_call("finish", kernel, [received], shapes, jnp.float32)


def unit_of(tokens):
    inputs = tokens.astype(jnp.float32)
    centered = inputs - jnp.mean(inputs, axis=-1, keepdims=True)
    inverse = lax.rsqrt(jnp.mean(centered * centered, axis=-1, keepdims=True) + EPSILON)
    return centered * inverse, inverse


def tokens_grad_of(tokens, cotangent, norm_gain, *refs):
    unit, inverse = unit_of(tokens[...])
    grads = cotangent[...].astype(jnp.float32)
    normed_grad = sum_of(*refs)
    unit_grad = normed_grad * norm_gain[...].astype(jnp.float32)
    tokens_grad = grads + inverse * (
        unit_grad
        - jnp.mean(unit_grad, axis=-1, keepdims=True)
        - unit * jnp.mean(unit_grad * unit, axis=-1, keepdims=True)
    )
    sums = [
        jnp.sum(item, axis=0, keepdims=True) for item in (normed_grad * unit, normed_grad, grads)
    ]
    return [tokens_grad, jnp.concatenate(sums, axis=0)]


def on_device(
    tokens,
    positions,
    cotangent,
    norm_gain,
    norm_bias,
    qkv_weight,
    qkv_bias,
    out_weight,
    out_bias,
    up_weight,
    up_bias,
    down_weight,
    down_bias,
):
    parts = lax.axis_size(CTX)
    part = lax.axis_index(CTX)
    width = qkv_weight.shape[2] // parts
    units = up_weight.shape[1] // parts

    unit_rows, _ = unit_of(tokens[0])
    normed_own = (unit_rows * norm_gain + norm_bias).astype(jnp.bfloat16)

    place = lax.axis_index(FSDP)
    turns = jnp.array(TURNS, jnp.int32)[place]
    place = place.astype(jnp.int32).reshape(1)

    def first_grad(columns, *products, mebibytes=48):
        return grad_pieces(products, turns, 0, 1, columns, mebibytes)[0]

    def later_grads(columns, *products):
        return [grad_pieces(products, turns, 1, 3, columns)]

    live = types.SimpleNamespace(
        attention=laid(
            near_trade(near_pieces("attention", jnp.swapaxes(qkv_weight, 0, 1), out_weight))
        ),
        rows=jnp.concatenate([normed_own, cotangent[0]], axis=0),
        tokens=tokens[0],
        cotangent=cotangent[0],
        weights=(up_weight, down_weight),
        positions=positions,
    )
    tick(live)
    live.attention = square_first(live.attention)
    live.rows = gather_first(live.rows)
    live.places = local_places(live.positions)
    live.turning = turning(live.places)
    tick(live)
    live.attention = square_second(live.attention)
    live.normed, live.grads = gather_third(gather_second(live.rows))
    live.up = gather_rows_of(pieces("up", live.weights[0]))
    live.down = pieces("down", live.weights[1])
    del live.rows
    tick(live)
    live.up = square_first(live.up)
    live.down = gather_rows_of(live.down)
    live.attention = in_square(live.attention, place)
    qkv_part = lax.dynamic_slice_in_dim(qkv_bias, part * width, width, 1).astype(jnp.float32)
    padded = width + -width % PAIR
    pairs = padded // PAIR
    projected = row_call(
        "project",
        project_kernel,
        [live.normed, live.grads, *live.turning],
        [live.attention, qkv_part.reshape(1, 3 * width)],
        [(padded, jnp.bfloat16)] * 3
        + [(padded, jnp.bfloat16, True)] * 2
        + [(padded, jnp.bfloat16), (padded, jnp.bfloat16, True)],
        mebibytes=60,
    )
    groups = live.places[::GROUP] // GROUP
    order = jnp.sum(
        jnp.where(
            groups[None, :] == jnp.arange(groups.shape[0])[:, None],
            jnp.arange(groups.shape[0])[None, :],
            0,
        ),
        axis=1,
    ).astype(jnp.int32)
    heads = ()
    for pair in range(pairs // 2):
        heads = attention(order, projected, live.turning, pair, heads)
    live.projected, live.order, live.heads = projected, order, heads
    tick(live)
    live.up = square_second(live.up)
    live.down = spread_first(live.down)
    heads = live.heads
    for pair in range(pairs // 2, pairs):
        heads = attention(live.order, live.projected, live.turning, pair, heads)
    live.heads = heads
    attended, *head_grads = live.heads
    head_products = ((live.normed, head_grads), (live.grads, [attended]))
    live.head_parts = [first_grad(width, *head_products, mebibytes=60)]
    tick(live)
    live.down = spread_second(live.down)
    live.head_sum = reduce_first(live.head_parts)
    attended, *head_grads = live.heads
    head_products = ((live.normed, head_grads), (live.grads, [attended]))
    live.up = in_square(live.up, place)
    own_bias = lax.dynamic_slice_in_dim(up_bias, part * units, units, 0).astype(jnp.float32)
    live.activated, live.slope = row_call(
        "hidden",
        hidden_kernel,
        [live.normed],
        [live.up, own_bias[None]],
        [(units, jnp.bfloat16), (units, jnp.bfloat16)],
    )
    live.head_parts = live.head_parts + later_grads(width, *head_products)
    tick(live)
    live.down = spread_third(live.down)
    live.head_sum = reduce_second([(live.head_parts, live.head_sum)], place)
    down_products = (live.grads, [live.activated])
    live.down_parts = [first_grad(units, down_products)] + later_grads(units, down_products)
    columns = [(0, slice(which * width, (which + 1) * width)) for which in range(4)]
    live.normed_part, live.qkv_sums = back(
        list(live.heads[1:]), columns[:3], [live.attention], summing=True
    )
    tick(live)
    live.head_sum, _ = reduce_third(live.head_parts, live.head_sum, place)
    live.down_sum = reduce_first(live.down_parts)
    live.down = in_line(live.down)
    live.hidden_grad, live.up_sums = row_call(
        "hidden_grad",
        hidden_grad_kernel,
        [live.grads, live.slope],
        [live.down],
        [(units, jnp.bfloat16), (1, units, jnp.float32, None)],
    )
    everything = (0, slice(0, units))
    live.branch = back(
        [live.activated, live.heads[0]],
        [everything, (1, columns[3][1])],
        [live.down, live.attention],
        halves=True,
    )
    tick(live)
    live.down_sum = reduce_second([(live.down_parts, live.down_sum)], place)
    up_products = (live.normed, [live.hidden_grad])
    live.up_parts = [first_grad(units, up_products)]
    live.up_sum = reduce_first(live.up_parts)
    far, near = live.branch
    got = hold(scatter_first(near, far), live.up_parts[0])
    (live.branch,) = scatter_third(*scatter_second(got))
    live.up_parts = live.up_parts + later_grads(units, up_products)
    live.normed_part = back(
        [live.hidden_grad], [everything], [live.up], live.normed_part, halves=True
    )
    tick(live)
    live.down_sum, sent = reduce_third(
        live.down_parts, live.down_sum, place, (live.up_parts, live.up_sum)
    )
    live.head_sum = reduce_last(live.head_parts, hold(live.head_sum, sent))
    far, near = live.normed_part
    (live.normed_part,) = scatter_third(*scatter_second(scatter_first(near, far)))
    live.sums = jnp.concatenate(
        [
            lax.dynamic_update_slice_in_dim(
                jnp.zeros(qkv_bias.shape, jnp.float32),
                live.qkv_sums[:, :width],
                part * width,
                1,
            ).reshape(-1),
            lax.dynamic_update_slice_in_dim(
                jnp.zeros(up_bias.shape, jnp.float32), live.up_sums[0], part * units, 0
            ),
        ]
    )
    tick(live)
    second = [(item, live.up_parts[0].shape[0], 1) for item in live.down_sum]
    live.up_sum, sent = reduce_third(live.up_parts, second, place)
    live.both = trade(last_beside(live.head_sum, live.down_parts, hold(live.down_sum, sent)))
    live.tokens_grad, norm_sums = pointwise(
        "tokens_grad",
        tokens_grad_of,
        [],
        [live.tokens, live.cotangent, norm_gain[None]] + addends(live.normed_part, 0),
        [(tokens.shape[1:], jnp.float32), ((3, D), jnp.float32)],
    )
    (live.layer_output,) = pointwise(
        "layer_output",
        lambda tokens, *refs: [sum_of(tokens, *refs)],
        [],
        [live.tokens, out_bias[None], down_bias[None]] + addends(live.branch, 0),
        [(tokens.shape[1:], jnp.bfloat16)],
    )
    norm_sums = total(norm_sums.reshape(-1), TP)
    live.sums = jnp.concatenate([live.sums, norm_sums])
    tick(live)
    up_sum = trade_back(reduce_last(live.up_parts, live.up_sum))
    (down_weight_grad,) = finish(live.both, "down", 1, 2)
    qkv_weight_grad, out_weight_grad = finish(live.both, "attention", 0, 2)
    sums = total(total(live.sums, FSDP), CTX)
    (up_weight_grad,) = finish(up_sum, "up")
    bias_sums = sums[: -3 * D]
    norm_sums = sums[-3 * D :].reshape(3, D)
    tokens_grad, layer_output = live.tokens_grad, live.layer_output

    return (
        layer_output[None],
        tokens_grad[None],
        norm_sums[0],
        norm_sums[1],
        jnp.swapaxes(qkv_weight_grad, 0, 1),
        bias_sums[: qkv_bias.size].reshape(qkv_bias.shape),
        out_weight_grad,
        norm_sums[2],
        up_weight_grad,
        bias_sums[qkv_bias.size :],
        down_weight_grad,
        norm_sums[2],
    )


def solution(mesh):
    rows = P(FSDP, (CTX, TP), None)
    placed = (
        rows,
        P(),
        rows,
        P(),
        P(),
        P((FSDP, CTX), None, TP),
        P(None, TP),
        P(TP, (FSDP, CTX)),
        P(),
        P((FSDP, CTX), TP),
        P(TP),
        P(TP, (FSDP, CTX)),
        P(),
    )
    return jax.shard_map(
        on_device,
        mesh=mesh,
        in_specs=placed,
        out_specs=(
            rows,
            rows,
            P(),
            P(),
            P((FSDP, CTX), None, TP),
            P(None, TP),
            P(TP, (FSDP, CTX)),
            P(),
            P((FSDP, CTX), TP),
            P(TP),
            P(TP, (FSDP, CTX)),
            P(),
        ),
        check_vma=False,
    )
```

```python
import functools
import types

import jax
import jax.numpy as jnp
from jax import lax
from jax.experimental import pallas as pl
from jax.experimental.pallas import tpu as pltpu
from jax.sharding import PartitionSpec as P

FSDP, CTX, TP = "fsdp", "ctx", "tp"

D = 2048
HEAD_DIM = 64
ROT = 32
GROUP = 256
PAIR = 2 * HEAD_DIM

EPSILON = 1e-05
MASKED = -1e30
GELU_SLOPE = 0.7978845608028654
GELU_CUBE = 0.044715


TURNS = ((3, 2, 1, 0), (3, 2, 0, 1), (0, 1, 3, 2), (0, 1, 2, 3))

NT = (((1,), (1,)), ((), ()))
NN = (((1,), (0,)), ((), ()))


NO_COST = pl.CostEstimate(flops=0, bytes_accessed=0, transcendentals=0)


def params(mebibytes=48):
    return pltpu.CompilerParams(vmem_limit_bytes=mebibytes * 1024 * 1024)


def dot(left, right, dims=NN):
    return lax.dot_general(left, right, dims, preferred_element_type=jnp.float32)


def turning(places):
    halfway = ROT // 2
    lane = jnp.arange(PAIR) % HEAD_DIM
    frequencies = 10000.0 ** (-((lane % halfway).astype(jnp.float32) * 2.0 / ROT))
    frequencies = jnp.where(lane < ROT, frequencies, 0.0)
    angles = places.astype(jnp.float32)[:, None] * frequencies[None, :]
    return jnp.cos(angles), jnp.sin(angles) * jnp.where(lane < halfway, -1.0, 1.0)[None, :]


def turn(values, cosine, sine):
    halfway = ROT // 2
    lane = lax.broadcasted_iota(jnp.int32, values.shape, 1) % HEAD_DIM
    partner = jnp.where(
        lane < halfway,
        pltpu.roll(values, PAIR - halfway, 1),
        pltpu.roll(values, halfway, 1),
    )
    return values * cosine + partner * sine


def attention_kernel(
    order,
    query_in,
    key_all,
    value_all,
    key_turned,
    value_turned,
    grad_in,
    grad_turned,
    cosine_all,
    sine_all,
    *refs,
):
    (attended_out, query_out, key_out, value_out, key_total, value_total, strip) = refs[-7:]
    groups, group = pl.num_programs(0), pl.program_id(0)
    tall, wide = strip.shape[1:]
    blocks = tall // GROUP

    def rows(place):
        return pl.ds(pl.multiple_of(order[place] * GROUP, GROUP), GROUP)

    def load(ref, step):
        return jnp.concatenate([ref[rows(step * blocks + at), :] for at in range(blocks)], axis=0)

    def load_turned(ref, step, head):
        here = slice(head * HEAD_DIM, (head + 1) * HEAD_DIM)
        return jnp.concatenate([ref[here, rows(step * blocks + at)] for at in range(blocks)], axis=1)

    def put(ref, step, values):
        for at in range(blocks):
            ref[rows(step * blocks + at), :] += values[at * GROUP : (at + 1) * GROUP]

    def fold(tile):
        return tile.reshape(tall // 8, 8, wide)

    def pair_up(values):
        first = lax.broadcasted_iota(jnp.int32, (GROUP, PAIR), 1) < HEAD_DIM
        nothing = jnp.zeros((GROUP, PAIR), jnp.bfloat16)
        return jnp.concatenate(
            [jnp.where(first, values, nothing), jnp.where(first, nothing, values)], axis=0
        )

    @pl.when(group == 0)
    def _():
        key_total[...] = jnp.zeros_like(key_total)
        value_total[...] = jnp.zeros_like(value_total)

    query_pair, grad_pair = pair_up(query_in[...]), pair_up(grad_in[...])
    steps = (group + blocks) // blocks
    ahead = lax.broadcasted_iota(jnp.int32, (tall, wide), 0) - (
        lax.broadcasted_iota(jnp.int32, (tall, wide), 1) % GROUP
    )

    def scores(step, most):
        tile = dot(load(key_all, step), query_pair, NT)
        tile = jnp.where(ahead <= (group - step * blocks) * GROUP, tile, MASKED)
        strip[step] = tile
        return jnp.maximum(most, jnp.max(fold(tile), axis=0))

    most = lax.fori_loop(0, steps, scores, jnp.full((8, wide), MASKED, jnp.float32))
    most = jnp.max(most, axis=0, keepdims=True)

    def weigh(step, carry):
        total, upper, lower = carry
        tile = jnp.exp(strip[step] - most)
        strip[step] = tile
        low = tile.astype(jnp.bfloat16)
        upper = upper + dot(load_turned(value_turned, step, 0), low[:, :GROUP])
        lower = lower + dot(load_turned(value_turned, step, 1), low[:, GROUP:])
        return total + jnp.sum(fold(tile), axis=0), upper, lower

    blank = jnp.zeros((HEAD_DIM, GROUP), jnp.float32)
    total, upper, lower = lax.fori_loop(
        0, steps, weigh, (jnp.zeros((8, wide), jnp.float32), blank, blank)
    )
    share = 1.0 / jnp.sum(total, axis=0, keepdims=True)
    upper = upper * share[:, :GROUP]
    lower = lower * share[:, GROUP:]
    attended_out[...] = jnp.concatenate([upper, lower], axis=0).astype(jnp.bfloat16).T
    grad = grad_turned[...].astype(jnp.float32)
    delta = jnp.concatenate(
        [
            jnp.sum(upper * grad[:HEAD_DIM], axis=0, keepdims=True),
            jnp.sum(lower * grad[HEAD_DIM:], axis=0, keepdims=True),
        ],
        axis=1,
    )

    def back(step, carry):
        upper, lower = carry
        part = strip[step] * share
        put(value_total, step, dot(part.astype(jnp.bfloat16), grad_pair))
        part = part * (dot(load(value_all, step), grad_pair, NT) - delta)
        low = part.astype(jnp.bfloat16)
        put(key_total, step, dot(low, query_pair))
        upper = upper + dot(load_turned(key_turned, step, 0), low[:, :GROUP])
        lower = lower + dot(load_turned(key_turned, step, 1), low[:, GROUP:])
        return upper, lower

    upper, lower = lax.fori_loop(0, steps, back, (blank, blank))
    own = rows(group)
    query_grad = jnp.concatenate([upper, lower], axis=0).T * HEAD_DIM ** (-0.5)
    query_out[...] = turn(query_grad, cosine_all[own, :], -sine_all[own, :]).astype(jnp.bfloat16)

    @pl.when(group == groups - 1)
    def _():
        key_grad = turn(key_total[...], cosine_all[...], -sine_all[...])
        key_out[...] = key_grad.astype(jnp.bfloat16)
        value_out[...] = value_total[...].astype(jnp.bfloat16)


def attention(order, projected, tables, pair, earlier=()):
    length, width = projected[0].shape
    groups = length // GROUP
    block = pl.BlockSpec((GROUP, PAIR), lambda group, order: (order[group], pair))
    turned_block = pl.BlockSpec((PAIR, GROUP), lambda group, order: (pair, order[group]))
    column = pl.BlockSpec((length, PAIR), lambda group, order: (0, pair))
    turned_column = pl.BlockSpec((PAIR, length), lambda group, order: (pair, 0))
    table = pl.BlockSpec((length, PAIR), lambda group, order: (0, 0))
    specs = [block, column, column, turned_column, turned_column, block, turned_block, table, table]
    return pl.pallas_call(
        attention_kernel,
        grid_spec=pltpu.PrefetchScalarGridSpec(
            num_scalar_prefetch=1,
            grid=(groups,),
            in_specs=specs + [pl.BlockSpec(memory_space=pl.ANY)] * len(earlier),
            out_specs=[block, block, column, column],
            scratch_shapes=[
                pltpu.VMEM((length, PAIR), jnp.float32),
                pltpu.VMEM((length, PAIR), jnp.float32),
                pltpu.VMEM((groups // 2, 2 * GROUP, 2 * GROUP), jnp.float32),
            ],
        ),
        out_shape=[jax.ShapeDtypeStruct((length, width), jnp.bfloat16)] * 4,
        input_output_aliases={1 + len(specs) + at: at for at in range(len(earlier))},
        compiler_params=params(60),
        cost_estimate=NO_COST,
        name=f"attention_{pair}",
    )(order, *projected, *tables, *earlier)


ROWS = 512


def chunk(place, which, size):
    return pl.ds(pl.multiple_of(place[which] * size, size), size)


def row_call(name, kernel, row_inputs, full_inputs, outputs, size=ROWS, turn=0, mebibytes=48):
    count = row_inputs[0].shape[0] // size
    rows = count * size

    def out(item):
        if len(item) == 4 and item[3] is None:
            shape, spec = item[:2], pl.BlockSpec(item[:2], lambda at: (0, 0))
        elif len(item) == 4:
            shape = ((item[3] - item[2]) * size, item[0])
            spec = pl.BlockSpec(
                (size, item[0]),
                lambda at: (jnp.clip(at, item[2], item[3] - 1) - item[2], 0),
            )
        elif len(item) == 3:
            shape = (item[0], rows)
            spec = pl.BlockSpec((item[0], size), lambda at: (0, at))
        else:
            shape = (rows, item[0])
            spec = pl.BlockSpec((size, item[0]), lambda at: (at, 0))
        kind = item[2] if len(item) == 4 and item[3] is None else item[1]
        return spec, jax.ShapeDtypeStruct(shape, kind)

    return pl.pallas_call(
        kernel,
        grid=(count,),
        in_specs=[
            pl.BlockSpec((size, item.shape[1]), lambda at: (lax.rem(at + turn, count), 0))
            for item in row_inputs
        ]
        + [pl.BlockSpec(item.shape, lambda at: (0, 0)) for item in full_inputs],
        out_specs=[out(item)[0] for item in outputs],
        out_shape=[out(item)[1] for item in outputs],
        compiler_params=params(mebibytes),
        cost_estimate=NO_COST,
        name=name,
    )(*row_inputs, *full_inputs)


def add_up(target, at, values):
    part = jnp.sum(values.astype(jnp.float32), axis=0, keepdims=True)

    @pl.when(pl.program_id(0) == 0)
    def _():
        target[at : at + 1, :] = part

    @pl.when(pl.program_id(0) > 0)
    def _():
        target[at : at + 1, :] += part


def project_kernel(normed, grads, cosine, sine, weight, bias, *refs):
    query, key, value, key_turned, value_turned, out_grads, grads_turned = refs
    width = weight.shape[1] // 4
    mixed = dot(normed[...], weight[:, : 3 * width]) + bias[...]
    parts = [mixed[:, which * width : (which + 1) * width] for which in range(3)]
    parts.append(dot(grads[...], weight[:, 3 * width :]))
    for pair in range(-(-width // PAIR)):
        here = slice(pair * PAIR, (pair + 1) * PAIR)
        items = [part[:, here] for part in parts]
        if width < PAIR:
            nothing = jnp.zeros((ROWS, PAIR - width), jnp.float32)
            items = [jnp.concatenate([item, nothing], axis=1) for item in items]
        turned = [turn(item, cosine[...], sine[...]) for item in items[:2]]
        low = turned[0].astype(jnp.bfloat16).astype(jnp.float32) * HEAD_DIM ** (-0.5)
        query[:, here] = low.astype(jnp.bfloat16)
        for target, target_turned, item in (
            (key, key_turned, turned[1]),
            (value, value_turned, items[2]),
            (out_grads, grads_turned, items[3]),
        ):
            low = item.astype(jnp.bfloat16)
            target[:, here] = low
            target_turned[here, :] = low.T


def hidden_kernel(normed, weight, bias, activated, slope):
    hidden = dot(normed[...], weight[...]) + bias[...]
    square = hidden * hidden
    bent = jnp.tanh(GELU_SLOPE * hidden * (1.0 + GELU_CUBE * square))
    half = 0.5 * (1.0 + bent)
    activated[...] = (hidden * half).astype(jnp.bfloat16)
    slope[...] = (
        half
        + 0.5 * GELU_SLOPE * hidden * (1.0 - bent * bent) * (1.0 + 3.0 * GELU_CUBE * square)
    ).astype(jnp.bfloat16)


def hidden_grad_kernel(grads, slope, weight, target, sums):
    low = (dot(grads[...], weight[...]) * slope[...].astype(jnp.float32)).astype(jnp.bfloat16)
    target[...] = low
    add_up(sums, 0, low)


def back_kernel(columns, start, summing, halves, *refs):
    lefts = refs[: len(columns)]
    weights, outs = refs[len(columns) + start : -1 - summing - halves], refs[-1 - summing - halves :]
    result = refs[len(columns)][...].astype(jnp.float32) if start else None
    for left, (which, here) in zip(lefts, columns):
        part = dot(left[:, : here.stop - here.start], weights[which][:, here], NT)
        result = part if result is None else result + part
    if halves:
        early = pl.program_id(0) < pl.num_programs(0) // 2

        @pl.when(early)
        def _():
            outs[0][...] = result.astype(jnp.bfloat16)

        @pl.when(jnp.logical_not(early))
        def _():
            outs[1][...] = result.astype(jnp.bfloat16)

    else:
        outs[0][...] = result.astype(jnp.bfloat16)
    if summing:
        for at, left in enumerate(lefts):
            add_up(outs[1], at, left[...])


def back(lefts, columns, weights, start=None, halves=False, summing=False):
    size = ROWS
    count = lefts[0].shape[0] // size
    starts = [] if start is None else [start]
    outputs = [(weights[0].shape[0], jnp.bfloat16)]
    if halves:
        outputs = [outputs[0] + (0, count // 2), outputs[0] + (count // 2, count)]
    if summing:
        outputs.append((len(lefts), lefts[0].shape[1], jnp.float32, None))
    got = row_call(
        "back",
        functools.partial(back_kernel, columns, len(starts), int(summing), int(halves)),
        lefts + starts,
        weights,
        outputs,
        size,
        count // 2 if halves else 0,
    )
    return got if summing or halves else got[0]


def grad_kernel(counts, width, turns, *refs):
    target = refs[-1]
    refs = list(refs[:-1])
    at = 0
    for count in counts:
        left = refs.pop(0)
        for _ in range(count):
            right = refs.pop(0)
            columns = min(width, right.shape[1])
            target[0, :, at : at + columns] = dot(
                left[...], right[:, :columns], (((0,), (0,)), ((), ()))
            ).astype(jnp.bfloat16)
            at += columns


def grad_pieces(products, turns, first, count, width, mebibytes=48):
    size = lax.axis_size(FSDP)
    specs, items, columns = [], [], 0
    for left, rights in products:
        rows = left.shape[1] // size
        specs.append(
            pl.BlockSpec((left.shape[0], rows), lambda at, turns: (0, turns[first + at]))
        )
        specs += [pl.BlockSpec(item.shape, lambda at, turns: (0, 0)) for item in rights]
        items += [left, *rights]
        columns += sum(min(width, item.shape[1]) for item in rights)
    return pl.pallas_call(
        functools.partial(grad_kernel, [len(rights) for _, rights in products], width),
        grid_spec=pltpu.PrefetchScalarGridSpec(
            num_scalar_prefetch=1,
            grid=(count,),
            in_specs=specs,
            out_specs=pl.BlockSpec((1, rows, columns), lambda at, turns: (at, 0, 0)),
        ),
        out_shape=jax.ShapeDtypeStruct((count, rows, columns), jnp.bfloat16),
        compiler_params=params(mebibytes),
        cost_estimate=NO_COST,
        name=f"grad_{first}",
    )(turns, *items)


def pointwise(name, function, scalars, inputs, outputs):
    def spec(item):
        if not isinstance(item, tuple):
            return pl.BlockSpec(item.shape, lambda at, n=item.ndim: (0,) * n)
        array, rows, index = item
        return pl.BlockSpec(
            (rows,) + array.shape[1:], lambda at, n=array.ndim, index=index: (index,) + (0,) * (n - 1)
        )

    def kernel(*refs):
        count = len(scalars) + len(inputs)
        for target, value in zip(refs[count:], function(*refs[:count])):
            target[...] = value.astype(target.dtype)

    return pl.pallas_call(
        kernel,
        grid=(1,),
        in_specs=[pl.BlockSpec(memory_space=pltpu.SMEM)] * len(scalars) + [spec(i) for i in inputs],
        out_specs=[pl.BlockSpec(shape, lambda at, n=len(shape): (0,) * n) for shape, _ in outputs],
        out_shape=[jax.ShapeDtypeStruct(shape, kind) for shape, kind in outputs],
        compiler_params=params(),
        cost_estimate=NO_COST,
        name=name,
    )(*scalars, *[item[0] if isinstance(item, tuple) else item for item in inputs])


def stack_kernel(parts, *refs):
    *sources, target, arrived = refs
    copies = [
        pltpu.make_async_copy(
            source.at[pl.ds(first, rows)], target.at[pl.ds(start, rows)], arrived.at[at]
        )
        for at, (source, (first, rows, start)) in enumerate(zip(sources, parts))
    ]
    for copy in copies:
        copy.start()
    for copy in copies:
        copy.wait()


def stack(parts, rows):
    array = parts[0][0]
    return pl.pallas_call(
        functools.partial(stack_kernel, [part[1:] for part in parts]),
        in_specs=[pl.BlockSpec(memory_space=pl.ANY)] * len(parts),
        out_specs=pl.BlockSpec(memory_space=pltpu.VMEM),
        out_shape=jax.ShapeDtypeStruct((rows, array.shape[1]), array.dtype),
        scratch_shapes=[pltpu.SemaphoreType.DMA((len(parts),))],
        compiler_params=params(),
        cost_estimate=NO_COST,
        name="stack",
    )(*[part[0] for part in parts])


def fill_kernel(starts, *refs):
    count = len(starts)
    sources, target = refs[:count], refs[count + 1]
    held, arrived, left = refs[count + 2 :]
    rows = [source.shape[0] for source in sources]
    slots = [pl.ds(sum(rows[:at]), rows[at]) for at in range(count)]
    inward = [
        pltpu.make_async_copy(source, held.at[slots[at]], arrived.at[at])
        for at, source in enumerate(sources)
    ]
    outward = [
        pltpu.make_async_copy(held.at[slots[at]], target.at[pl.ds(start, rows[at])], left.at[at])
        for at, start in enumerate(starts)
    ]
    for copy in inward:
        copy.start()
    for first, second in zip(inward, outward):
        first.wait()
        second.start()
    for copy in outward:
        copy.wait()


def fill(target, parts):
    anywhere = pl.BlockSpec(memory_space=pl.ANY)
    count = len(parts)
    rows = sum(array.shape[0] for array, _ in parts)
    return pl.pallas_call(
        functools.partial(fill_kernel, [start for _, start in parts]),
        in_specs=[anywhere] * (count + 1),
        out_specs=anywhere,
        out_shape=jax.ShapeDtypeStruct(target.shape, target.dtype),
        scratch_shapes=[
            pltpu.VMEM((rows, target.shape[1]), target.dtype),
            pltpu.SemaphoreType.DMA((count,)),
            pltpu.SemaphoreType.DMA((count,)),
        ],
        input_output_aliases={count: 0},
        compiler_params=params(),
        cost_estimate=NO_COST,
        name="fill",
    )(*[array for array, _ in parts], target)


def line_kernel(place, *refs):
    own, up_one, down_one, up_two, down_two, up_three, down_three, target, arrived = refs
    rows = own.shape[0]
    for where, sources in enumerate(
        (
            (own, down_one, down_two, down_three),
            (up_one, own, down_one, down_two),
            (up_two, up_one, own, down_one),
            (up_three, up_two, up_one, own),
        )
    ):

        @pl.when(place[0] == where)
        def _(sources=sources):
            copies = [
                pltpu.make_async_copy(source, target.at[pl.ds(at * rows, rows)], arrived.at[at])
                for at, source in enumerate(sources)
            ]
            for copy in copies:
                copy.start()
            for copy in copies:
                copy.wait()


def in_line(got):
    anywhere = pl.BlockSpec(memory_space=pl.ANY)
    rows, columns = got[0].shape
    return pl.pallas_call(
        line_kernel,
        in_specs=[pl.BlockSpec(memory_space=pltpu.SMEM)] + [anywhere] * len(got),
        out_specs=pl.BlockSpec(memory_space=pltpu.VMEM),
        out_shape=jax.ShapeDtypeStruct((4 * rows, columns), got[0].dtype),
        scratch_shapes=[pltpu.SemaphoreType.DMA((4,))],
        compiler_params=params(),
        cost_estimate=NO_COST,
        name="in_line",
    )(lax.axis_index(FSDP).astype(jnp.int32).reshape(1), *got)


def swap(values, axis, bit):
    size = lax.axis_size(axis)
    with jax.named_scope(f"{axis}_{bit}"):
        return lax.ppermute(values, axis, [(place, place ^ bit) for place in range(size)])


def total(values, axis, *between):
    between = list(between)
    bit = 1
    while bit < lax.axis_size(axis):
        values = values + swap(values, axis, bit)
        if between:
            values = hold(values, between.pop(0))
        bit *= 2
    return values


def move(values, pairs):
    with jax.named_scope("line"):
        return lax.ppermute(values, FSDP, pairs)


def spread_first(own):
    return [own, move(own, [(0, 1), (1, 2), (2, 3)]), move(own, [(1, 0), (2, 1), (3, 2)])]


def spread_second(got):
    return got + [move(got[1], [(1, 2), (2, 3)]), move(got[2], [(1, 0), (2, 1)])]


def spread_third(got):
    return got + [move(got[3], [(2, 3)]), move(got[4], [(1, 0)])]


def reduce_first(parts):
    return move(parts[0], [(0, 1), (3, 2)])


def square_first(own):
    return [own, swap(own, FSDP, 1), swap(own, FSDP, 2)]


def square_second(got):
    return got + [swap(got[2], FSDP, 1)]


def square_kernel(place, *refs):
    *sources, target, arrived = refs
    rows = sources[0].shape[0]
    copies = []
    for which, source in enumerate(sources):
        here = pl.ds(pl.multiple_of((place[0] ^ which) * rows, rows), rows)
        copies.append(pltpu.make_async_copy(source, target.at[here], arrived.at[which]))
    for copy in copies:
        copy.start()
    for copy in copies:
        copy.wait()


def in_square(got, place):
    rows, columns = got[0].shape
    return pl.pallas_call(
        square_kernel,
        in_specs=[pl.BlockSpec(memory_space=pltpu.SMEM)]
        + [pl.BlockSpec(memory_space=pl.ANY)] * len(got),
        out_specs=pl.BlockSpec(memory_space=pltpu.VMEM),
        out_shape=jax.ShapeDtypeStruct((len(got) * rows, columns), got[0].dtype),
        scratch_shapes=[pltpu.SemaphoreType.DMA((len(got),))],
        compiler_params=params(),
        cost_estimate=NO_COST,
        name="in_square",
    )(place, *got)


UP, DOWN = [(0, 1), (1, 2), (2, 3)], [(1, 0), (2, 1), (3, 2)]


def second_of(place, first, second, got):
    ends = (place[0] == 0) | (place[0] == 3)
    return jnp.where(ends, sum_of(second)[0], sum_of(first) + got)


def third_of(place, second, third, upward, downward):
    one, two = sum_of(second)[0], sum_of(third)[0]
    return (
        jnp.where(place[0] == 1, one, two) + sum_of(upward),
        jnp.where(place[0] == 2, one, two) + sum_of(downward),
    )


def reduce_second(sums, place):
    inputs = []
    for (first, rest), got in sums:
        inputs += [first, (rest, 1, 0), got]
    rows, columns = sums[0][0][0].shape

    def choose(place, *refs):
        sent = [
            second_of(place, first, second, sum_of(got))
            for first, second, got in zip(refs[::3], refs[1::3], refs[2::3])
        ]
        return [jnp.stack(sent)]

    shape = (len(sums), rows, columns)
    sent = pointwise("second", choose, [place], inputs, [(shape, jnp.bfloat16)])[0]
    sent = sent.reshape(-1, columns)
    return [move(sent, UP[:2]), move(sent, DOWN[1:])]


def reduce_third(parts, got, place, new=None):
    first, rest = parts
    rows, columns = first.shape
    shape = (1 if new is None else 2, rows, columns)

    def choose(place, second, third, upward, downward, *others):
        sent = third_of(place, second, third, upward, downward)
        if not others:
            return [item[None] for item in sent]
        first, second, got = others
        other = second_of(place, first, second, sum_of(got))
        return [jnp.stack([item, other]) for item in sent]

    inputs = [(rest, 1, 0), (rest, 1, 1), *got]
    if new is not None:
        inputs += [new[0][0], (new[0][1], 1, 0), new[1]]
    upward, downward = pointwise(
        "third", choose, [place], inputs, [(shape, jnp.bfloat16)] * 2
    )
    upward, downward = upward.reshape(-1, columns), downward.reshape(-1, columns)
    return [move(upward, UP), move(downward, DOWN)], upward


def reduce_last(parts, got, index=0):
    first, rest = parts
    return pointwise(
        "last",
        lambda last, *got: [sum_of(last)[0] + sum_of(*got)],
        [],
        [(rest, 1, 2)] + [(item, first.shape[0], index) for item in got],
        [(first.shape, jnp.bfloat16)],
    )[0]


def paired():
    return lax.axis_size(CTX) == 4 and lax.axis_size(TP) == 2


def gather_first(own):
    if not paired():
        return [own]
    return [own, swap(own, TP, 1), swap(own, CTX, 2), swap(own, CTX, 1)]


def gather_second(got):
    if not paired():
        return got
    size = got[0].shape[0] // 2
    corner = [swap(got[1][:size], CTX, 2), swap(got[2][size:], TP, 1)]
    return got + [swap(got[1], CTX, 1), swap(got[2], CTX, 1)] + corner


def gather_third(got):
    if not paired():
        size = got[0].shape[0] // 2
        return [
            lax.all_gather(item, (CTX, TP), axis=0, tiled=True)
            for item in (got[0][:size], got[0][size:])
        ]
    own, across, along, far_own, far_across, far_along, *corner = got
    size = corner[0].shape[0]
    half = size // 2
    results = []
    for which in range(2):
        sides = (own, across, along, None, far_own, far_across, far_along, None)
        parts = [
            (item, which * size, size, at * size)
            for at, item in enumerate(sides)
            if item is not None
        ]
        results.append(stack(parts, 8 * size))
    corner, results = lax.optimization_barrier((corner, results))
    for which in range(2):
        parts = [(corner[which], 3 * size)]
        for at in (0, half):
            parts.append((swap(corner[which][at : at + half], CTX, 1), 7 * size + at))
        results[which] = fill(results[which], parts)
    return results


def scatter_first(near, far):
    return [near, swap(far, CTX, 1) if paired() else far]


def sum_of(*refs):
    result = None
    for ref in refs:
        values = ref[...].astype(jnp.float32)
        result = values if result is None else result + values
    return result


def scatter_second(*all_got):
    if not paired():
        return list(all_got)
    size, columns = all_got[0][0].shape[0] // 4, all_got[0][0].shape[1]
    half = size // 2

    def corners(*refs):
        sums = [sum_of(*refs[at : at + 2]) for at in range(0, len(refs), 2)]
        return [
            jnp.concatenate([item[:half] for item in sums], axis=0),
            jnp.concatenate([item[half:] for item in sums], axis=0),
        ]

    sent = pointwise(
        "corners",
        corners,
        [],
        [(item, size, 3) for got in all_got for item in got],
        [((len(all_got) * half, columns), jnp.bfloat16)] * 2,
    )
    from_across, from_along = swap(sent[0], TP, 1), swap(sent[1], CTX, 2)
    return [got + [from_across, from_along] for got in all_got]


def scatter_third(*all_got):
    if not paired():
        return [
            [lax.psum_scatter(jnp.concatenate(got), (CTX, TP), scatter_dimension=0, tiled=True)]
            for got in all_got
        ]
    size, columns = all_got[0][0].shape[0] // 4, all_got[0][0].shape[1]
    half = size // 2

    def sides(*refs):
        acrosses, alongs = [], []
        for at in range(0, len(refs), 6):
            across, along = sum_of(*refs[at : at + 2]), sum_of(*refs[at + 2 : at + 4])
            from_across, from_along = refs[at + 4 : at + 6]
            acrosses += [across[:half], across[half:] + sum_of(from_along)]
            alongs += [along[:half] + sum_of(from_across), along[half:]]
        return [jnp.concatenate(acrosses, axis=0), jnp.concatenate(alongs, axis=0)]

    inputs = []
    for at, (near, far, from_across, from_along) in enumerate(all_got):
        inputs += [(near, size, 1), (far, size, 1), (near, size, 2), (far, size, 2)]
        inputs += [(from_across, half, at), (from_along, half, at)]
    across, along = pointwise(
        "sides", sides, [], inputs, [((len(all_got) * size, columns), jnp.bfloat16)] * 2
    )
    across, along = swap(across, TP, 1), swap(along, CTX, 2)
    return [[near, far, across, along] for near, far, *_ in all_got]


def addends(got, index):
    if not paired():
        return got
    size = got[0].shape[0] // 4
    return [(got[0], size, 0), (got[1], size, 0), (got[2], size, index), (got[3], size, index)]


def local_places(positions):
    if not paired():
        return positions
    devices = jnp.array([2 * along + near for near in (0, 1) for along in (0, 1) for _ in (0, 1)])
    blocks = (lax.axis_index(CTX) ^ devices) * 2 + (
        lax.axis_index(TP) ^ jnp.array([0, 1] * 4)
    )
    return positions.reshape(8, -1)[blocks].reshape(-1)


def hold(values, *after):
    return lax.optimization_barrier((values,) + after)[0]


def hold(values, *after):
    return lax.optimization_barrier((values,) + after)[0]


def tick(live):
    vars(live).update(lax.optimization_barrier(dict(vars(live))))


def small_call(name, kernel, place, items, shapes, kind):
    vmem = pl.BlockSpec(memory_space=pltpu.VMEM)
    return pl.pallas_call(
        kernel,
        in_specs=[pl.BlockSpec(memory_space=pltpu.SMEM)] + [vmem] * len(items),
        out_specs=[vmem] * len(shapes),
        out_shape=[jax.ShapeDtypeStruct(shape, kind) for shape in shapes],
        compiler_params=params(),
        cost_estimate=NO_COST,
        name=name,
    )(place, *items)


def small_call(name, kernel, items, shapes, kind, *places):
    vmem = pl.BlockSpec(memory_space=pltpu.VMEM)
    return pl.pallas_call(
        kernel,
        in_specs=[pl.BlockSpec(memory_space=pltpu.SMEM)] * len(places) + [vmem] * len(items),
        out_specs=[vmem] * len(shapes),
        out_shape=[jax.ShapeDtypeStruct(shape, kind) for shape in shapes],
        compiler_params=params(),
        cost_estimate=NO_COST,
        name=name,
    )(*places, *items)


def pieces(kind, *sources):
    parts = lax.axis_size(CTX)
    rows = sources[-1].shape[0 if kind == "up" else 1]
    width = sources[-1].shape[1 if kind == "up" else 0] // parts
    columns = 4 * width if kind == "attention" else width
    if width % PAIR:
        items = jnp.stack([*sources[0], sources[1].T]).reshape(4, rows, parts, width)
        return jnp.transpose(items, (2, 1, 0, 3)).reshape(parts, rows, columns)

    def kernel(*refs):
        *sources, target = refs
        for r in range(parts):
            here = slice(r * width, (r + 1) * width)
            if kind == "attention":
                for which in range(3):
                    target[r, :, which * width : (which + 1) * width] = sources[0][which, :, here]
                target[r, :, 3 * width :] = sources[1][here, :].T
            elif kind == "up":
                target[r] = sources[0][:, here]
            else:
                target[r] = sources[0][here, :].T

    return small_call("pieces", kernel, sources, [(parts, rows, columns)], sources[0].dtype)[0]


def near_pieces(kind, *sources):
    parts = lax.axis_size(CTX)
    place = lax.axis_index(CTX).astype(jnp.int32)
    sent = pieces(kind, *sources) if sources[-1].shape[0] // parts % PAIR else None
    if sent is not None:
        return [lax.dynamic_index_in_dim(sent, place ^ r, 0, False) for r in range(parts)]
    rows, width = sources[1].shape[1], sources[1].shape[0] // parts

    def kernel(place, qkv, out, *targets):
        for r, target in enumerate(targets):
            here = pl.ds(pl.multiple_of((place[0] ^ r) * width, width), width)
            for which in range(3):
                target[:, which * width : (which + 1) * width] = qkv[which, :, here]
            target[:, 3 * width :] = out[here, :].T

    return small_call(
        "pieces", kernel, sources, [(rows, 4 * width)] * parts, sources[0].dtype, place.reshape(1)
    )


def near_trade(sent):
    return [sent[0]] + [swap(sent[r], CTX, r) for r in range(1, len(sent))]


def laid(received):
    def kernel(place, *refs):
        *sources, target = refs
        for r, source in enumerate(sources):
            rows = source.shape[0]
            target[pl.ds(pl.multiple_of((place[0] ^ r) * rows, rows), rows), :] = source[...]

    rows, columns = received[0].shape
    place = lax.axis_index(CTX).astype(jnp.int32).reshape(1)
    shape = (len(received) * rows, columns)
    return small_call("laid", kernel, received, [shape], received[0].dtype, place)[0]


def trade(sent):
    return lax.all_to_all(sent, CTX, 0, 0, tiled=True)


def gather_rows_of(sent):
    got = trade(sent)
    return got.reshape(-1, got.shape[2])


def trade_back(summed):
    return trade(summed.reshape(lax.axis_size(CTX), -1, summed.shape[1]))


def last_beside(other, parts, got):
    first, rest = parts
    count = lax.axis_size(CTX)
    rows, columns = first.shape[0] // count, first.shape[1]

    def choose(other, last, *got):
        total = (sum_of(last)[0] + sum_of(*got)).reshape(count, rows, columns)
        return [jnp.concatenate([sum_of(other).reshape(count, rows, columns), total], axis=1)]

    return pointwise(
        "last",
        choose,
        [],
        [other, (rest, 1, 2)] + [(item, first.shape[0], 0) for item in got],
        [((count, 2 * rows, columns), jnp.bfloat16)],
    )[0]


def finish(received, kind, index=0, count=1):
    parts, rows, columns = received.shape
    rows //= count
    width = columns // 4 if kind == "attention" else columns
    if width % PAIR:
        items = received[:, index * rows : (index + 1) * rows].astype(jnp.float32)
        items = jnp.transpose(items.reshape(parts, rows, 4, width), (2, 1, 0, 3))
        items = items.reshape(4, rows, parts * width)
        return items[:3], items[3].T

    def kernel(source, *targets):
        for r in range(parts):
            here = slice(r * width, (r + 1) * width)
            values = source[r, index * rows : (index + 1) * rows].astype(jnp.float32)
            if kind == "attention":
                for which in range(3):
                    targets[0][which, :, here] = values[:, which * width : (which + 1) * width]
                targets[1][here, :] = values[:, 3 * width :].T
            elif kind == "up":
                targets[0][:, here] = values
            else:
                targets[0][here, :] = values.T

    shapes = {
        "attention": [(3, rows, parts * width), (parts * width, rows)],
        "up": [(rows, parts * width)],
        "down": [(parts * width, rows)],
    }[kind]
    return small_call("finish", kernel, [received], shapes, jnp.float32)


def unit_of(tokens):
    inputs = tokens.astype(jnp.float32)
    centered = inputs - jnp.mean(inputs, axis=-1, keepdims=True)
    inverse = lax.rsqrt(jnp.mean(centered * centered, axis=-1, keepdims=True) + EPSILON)
    return centered * inverse, inverse


def tokens_grad_of(tokens, cotangent, norm_gain, *refs):
    unit, inverse = unit_of(tokens[...])
    grads = cotangent[...].astype(jnp.float32)
    normed_grad = sum_of(*refs)
    unit_grad = normed_grad * norm_gain[...].astype(jnp.float32)
    tokens_grad = grads + inverse * (
        unit_grad
        - jnp.mean(unit_grad, axis=-1, keepdims=True)
        - unit * jnp.mean(unit_grad * unit, axis=-1, keepdims=True)
    )
    sums = [
        jnp.sum(item, axis=0, keepdims=True) for item in (normed_grad * unit, normed_grad, grads)
    ]
    return [tokens_grad, jnp.concatenate(sums, axis=0)]


def on_device(
    tokens,
    positions,
    cotangent,
    norm_gain,
    norm_bias,
    qkv_weight,
    qkv_bias,
    out_weight,
    out_bias,
    up_weight,
    up_bias,
    down_weight,
    down_bias,
):
    parts = lax.axis_size(CTX)
    part = lax.axis_index(CTX)
    width = qkv_weight.shape[2] // parts
    units = up_weight.shape[1] // parts

    unit_rows, _ = unit_of(tokens[0])
    normed_own = (unit_rows * norm_gain + norm_bias).astype(jnp.bfloat16)

    place = lax.axis_index(FSDP)
    turns = jnp.array(TURNS, jnp.int32)[place]
    place = place.astype(jnp.int32).reshape(1)

    def first_grad(columns, *products, mebibytes=48):
        return grad_pieces(products, turns, 0, 1, columns, mebibytes)[0]

    def later_grads(columns, *products):
        return [grad_pieces(products, turns, 1, 3, columns)]

    live = types.SimpleNamespace(
        attention=laid(
            near_trade(near_pieces("attention", jnp.swapaxes(qkv_weight, 0, 1), out_weight))
        ),
        rows=jnp.concatenate([normed_own, cotangent[0]], axis=0),
        tokens=tokens[0],
        cotangent=cotangent[0],
        weights=(up_weight, down_weight),
        positions=positions,
    )
    tick(live)
    live.attention = square_first(live.attention)
    live.rows = gather_first(live.rows)
    live.places = local_places(live.positions)
    live.turning = turning(live.places)
    live.down = pieces("down", live.weights[1])
    tick(live)
    live.attention = square_second(live.attention)
    live.normed, live.grads = gather_third(gather_second(live.rows))
    live.up = gather_rows_of(pieces("up", live.weights[0]))
    del live.rows
    tick(live)
    live.up = square_first(live.up)
    live.down = gather_rows_of(live.down)
    live.attention = in_square(live.attention, place)
    qkv_part = lax.dynamic_slice_in_dim(qkv_bias, part * width, width, 1).astype(jnp.float32)
    padded = width + -width % PAIR
    pairs = padded // PAIR
    projected = row_call(
        "project",
        project_kernel,
        [live.normed, live.grads, *live.turning],
        [live.attention, qkv_part.reshape(1, 3 * width)],
        [(padded, jnp.bfloat16)] * 3
        + [(padded, jnp.bfloat16, True)] * 2
        + [(padded, jnp.bfloat16), (padded, jnp.bfloat16, True)],
        mebibytes=60,
    )
    groups = live.places[::GROUP] // GROUP
    order = jnp.sum(
        jnp.where(
            groups[None, :] == jnp.arange(groups.shape[0])[:, None],
            jnp.arange(groups.shape[0])[None, :],
            0,
        ),
        axis=1,
    ).astype(jnp.int32)
    heads = ()
    for pair in range(pairs // 2):
        heads = attention(order, projected, live.turning, pair, heads)
    live.projected, live.order, live.heads = projected, order, heads
    tick(live)
    live.up = square_second(live.up)
    live.down = spread_first(live.down)
    heads = live.heads
    for pair in range(pairs // 2, pairs):
        heads = attention(live.order, live.projected, live.turning, pair, heads)
    live.heads = heads
    attended, *head_grads = live.heads
    head_products = ((live.normed, head_grads), (live.grads, [attended]))
    live.head_parts = [first_grad(width, *head_products, mebibytes=60)]
    tick(live)
    live.down = spread_second(live.down)
    live.head_sum = reduce_first(live.head_parts)
    attended, *head_grads = live.heads
    head_products = ((live.normed, head_grads), (live.grads, [attended]))
    live.up = in_square(live.up, place)
    own_bias = lax.dynamic_slice_in_dim(up_bias, part * units, units, 0).astype(jnp.float32)
    live.activated, live.slope = row_call(
        "hidden",
        hidden_kernel,
        [live.normed],
        [live.up, own_bias[None]],
        [(units, jnp.bfloat16), (units, jnp.bfloat16)],
    )
    live.head_parts = live.head_parts + later_grads(width, *head_products)
    tick(live)
    live.down = spread_third(live.down)
    live.head_sum = reduce_second([(live.head_parts, live.head_sum)], place)
    down_products = (live.grads, [live.activated])
    live.down_parts = [first_grad(units, down_products)] + later_grads(units, down_products)
    columns = [(0, slice(which * width, (which + 1) * width)) for which in range(4)]
    live.normed_part, live.qkv_sums = back(
        list(live.heads[1:]), columns[:3], [live.attention], summing=True
    )
    tick(live)
    live.head_sum, _ = reduce_third(live.head_parts, live.head_sum, place)
    live.down_sum = reduce_first(live.down_parts)
    live.down = in_line(live.down)
    live.hidden_grad, live.up_sums = row_call(
        "hidden_grad",
        hidden_grad_kernel,
        [live.grads, live.slope],
        [live.down],
        [(units, jnp.bfloat16), (1, units, jnp.float32, None)],
    )
    everything = (0, slice(0, units))
    live.branch = back(
        [live.activated, live.heads[0]],
        [everything, (1, columns[3][1])],
        [live.down, live.attention],
        halves=True,
    )
    tick(live)
    live.down_sum = reduce_second([(live.down_parts, live.down_sum)], place)
    up_products = (live.normed, [live.hidden_grad])
    live.up_parts = [first_grad(units, up_products)]
    live.up_sum = reduce_first(live.up_parts)
    far, near = live.branch
    got = hold(scatter_first(near, far), live.up_parts[0])
    (live.branch,) = scatter_third(*scatter_second(got))
    live.up_parts = live.up_parts + later_grads(units, up_products)
    live.normed_part = back(
        [live.hidden_grad], [everything], [live.up], live.normed_part, halves=True
    )
    tick(live)
    live.down_sum, sent = reduce_third(
        live.down_parts, live.down_sum, place, (live.up_parts, live.up_sum)
    )
    live.head_sum = reduce_last(live.head_parts, hold(live.head_sum, sent))
    far, near = live.normed_part
    (live.normed_part,) = scatter_third(*scatter_second(scatter_first(near, far)))
    live.sums = jnp.concatenate(
        [
            lax.dynamic_update_slice_in_dim(
                jnp.zeros(qkv_bias.shape, jnp.float32),
                live.qkv_sums[:, :width],
                part * width,
                1,
            ).reshape(-1),
            lax.dynamic_update_slice_in_dim(
                jnp.zeros(up_bias.shape, jnp.float32), live.up_sums[0], part * units, 0
            ),
        ]
    )
    tick(live)
    second = [(item, live.up_parts[0].shape[0], 1) for item in live.down_sum]
    live.up_sum, sent = reduce_third(live.up_parts, second, place)
    live.both = trade(last_beside(live.head_sum, live.down_parts, hold(live.down_sum, sent)))
    live.tokens_grad, norm_sums = pointwise(
        "tokens_grad",
        tokens_grad_of,
        [],
        [live.tokens, live.cotangent, norm_gain[None]] + addends(live.normed_part, 0),
        [(tokens.shape[1:], jnp.float32), ((3, D), jnp.float32)],
    )
    (live.layer_output,) = pointwise(
        "layer_output",
        lambda tokens, *refs: [sum_of(tokens, *refs)],
        [],
        [live.tokens, out_bias[None], down_bias[None]] + addends(live.branch, 0),
        [(tokens.shape[1:], jnp.bfloat16)],
    )
    norm_sums = total(norm_sums.reshape(-1), TP)
    live.sums = jnp.concatenate([live.sums, norm_sums])
    tick(live)
    up_sum = trade_back(reduce_last(live.up_parts, live.up_sum))
    (down_weight_grad,) = finish(live.both, "down", 1, 2)
    qkv_weight_grad, out_weight_grad = finish(live.both, "attention", 0, 2)
    sums = total(
        live.sums, FSDP, down_weight_grad, (qkv_weight_grad, out_weight_grad)
    )
    sums = total(sums, CTX)
    (up_weight_grad,) = finish(up_sum, "up")
    bias_sums = sums[: -3 * D]
    norm_sums = sums[-3 * D :].reshape(3, D)
    tokens_grad, layer_output = live.tokens_grad, live.layer_output

    return (
        layer_output[None],
        tokens_grad[None],
        norm_sums[0],
        norm_sums[1],
        jnp.swapaxes(qkv_weight_grad, 0, 1),
        bias_sums[: qkv_bias.size].reshape(qkv_bias.shape),
        out_weight_grad,
        norm_sums[2],
        up_weight_grad,
        bias_sums[qkv_bias.size :],
        down_weight_grad,
        norm_sums[2],
    )


def solution(mesh):
    rows = P(FSDP, (CTX, TP), None)
    placed = (
        rows,
        P(),
        rows,
        P(),
        P(),
        P((FSDP, CTX), None, TP),
        P(None, TP),
        P(TP, (FSDP, CTX)),
        P(),
        P((FSDP, CTX), TP),
        P(TP),
        P(TP, (FSDP, CTX)),
        P(),
    )
    return jax.shard_map(
        on_device,
        mesh=mesh,
        in_specs=placed,
        out_specs=(
            rows,
            rows,
            P(),
            P(),
            P((FSDP, CTX), None, TP),
            P(None, TP),
            P(TP, (FSDP, CTX)),
            P(),
            P((FSDP, CTX), TP),
            P(TP),
            P(TP, (FSDP, CTX)),
            P(),
        ),
        check_vma=False,
    )
```

```python
import functools
import types

import jax
import jax.numpy as jnp
from jax import lax
from jax.experimental import pallas as pl
from jax.experimental.pallas import tpu as pltpu
from jax.sharding import PartitionSpec as P

FSDP, CTX, TP = "fsdp", "ctx", "tp"

D = 2048
HEAD_DIM = 64
ROT = 32
GROUP = 256
PAIR = 2 * HEAD_DIM

EPSILON = 1e-05
MASKED = -1e30
GELU_SLOPE = 0.7978845608028654
GELU_CUBE = 0.044715


TURNS = ((3, 2, 1, 0), (3, 2, 0, 1), (0, 1, 3, 2), (0, 1, 2, 3))

NT = (((1,), (1,)), ((), ()))
NN = (((1,), (0,)), ((), ()))


NO_COST = pl.CostEstimate(flops=0, bytes_accessed=0, transcendentals=0)


def params(mebibytes=48):
    return pltpu.CompilerParams(vmem_limit_bytes=mebibytes * 1024 * 1024)


def dot(left, right, dims=NN):
    return lax.dot_general(left, right, dims, preferred_element_type=jnp.float32)


def turning(places):
    halfway = ROT // 2
    lane = jnp.arange(PAIR) % HEAD_DIM
    frequencies = 10000.0 ** (-((lane % halfway).astype(jnp.float32) * 2.0 / ROT))
    frequencies = jnp.where(lane < ROT, frequencies, 0.0)
    angles = places.astype(jnp.float32)[:, None] * frequencies[None, :]
    return jnp.cos(angles), jnp.sin(angles) * jnp.where(lane < halfway, -1.0, 1.0)[None, :]


def turn(values, cosine, sine):
    halfway = ROT // 2
    lane = lax.broadcasted_iota(jnp.int32, values.shape, 1) % HEAD_DIM
    partner = jnp.where(
        lane < halfway,
        pltpu.roll(values, PAIR - halfway, 1),
        pltpu.roll(values, halfway, 1),
    )
    return values * cosine + partner * sine


def attention_kernel(
    order,
    query_in,
    key_all,
    value_all,
    key_turned,
    value_turned,
    grad_in,
    grad_turned,
    cosine_all,
    sine_all,
    *refs,
):
    (attended_out, query_out, key_out, value_out, key_total, value_total, strip) = refs[-7:]
    groups, group = pl.num_programs(0), pl.program_id(0)
    tall, wide = strip.shape[1:]
    blocks = tall // GROUP

    def rows(place):
        return pl.ds(pl.multiple_of(order[place] * GROUP, GROUP), GROUP)

    def load(ref, step):
        return jnp.concatenate([ref[rows(step * blocks + at), :] for at in range(blocks)], axis=0)

    def load_turned(ref, step, head):
        here = slice(head * HEAD_DIM, (head + 1) * HEAD_DIM)
        return jnp.concatenate([ref[here, rows(step * blocks + at)] for at in range(blocks)], axis=1)

    def put(ref, step, values):
        for at in range(blocks):
            ref[rows(step * blocks + at), :] += values[at * GROUP : (at + 1) * GROUP]

    def fold(tile):
        return tile.reshape(tall // 8, 8, wide)

    def pair_up(values):
        first = lax.broadcasted_iota(jnp.int32, (GROUP, PAIR), 1) < HEAD_DIM
        nothing = jnp.zeros((GROUP, PAIR), jnp.bfloat16)
        return jnp.concatenate(
            [jnp.where(first, values, nothing), jnp.where(first, nothing, values)], axis=0
        )

    @pl.when(group == 0)
    def _():
        key_total[...] = jnp.zeros_like(key_total)
        value_total[...] = jnp.zeros_like(value_total)

    query_pair, grad_pair = pair_up(query_in[...]), pair_up(grad_in[...])
    steps = (group + blocks) // blocks
    ahead = lax.broadcasted_iota(jnp.int32, (tall, wide), 0) - (
        lax.broadcasted_iota(jnp.int32, (tall, wide), 1) % GROUP
    )

    def scores(step, most):
        tile = dot(load(key_all, step), query_pair, NT)
        tile = jnp.where(ahead <= (group - step * blocks) * GROUP, tile, MASKED)
        strip[step] = tile
        return jnp.maximum(most, jnp.max(fold(tile), axis=0))

    most = lax.fori_loop(0, steps, scores, jnp.full((8, wide), MASKED, jnp.float32))
    most = jnp.max(most, axis=0, keepdims=True)

    def weigh(step, carry):
        total, upper, lower = carry
        tile = jnp.exp(strip[step] - most)
        strip[step] = tile
        low = tile.astype(jnp.bfloat16)
        upper = upper + dot(load_turned(value_turned, step, 0), low[:, :GROUP])
        lower = lower + dot(load_turned(value_turned, step, 1), low[:, GROUP:])
        return total + jnp.sum(fold(tile), axis=0), upper, lower

    blank = jnp.zeros((HEAD_DIM, GROUP), jnp.float32)
    total, upper, lower = lax.fori_loop(
        0, steps, weigh, (jnp.zeros((8, wide), jnp.float32), blank, blank)
    )
    share = 1.0 / jnp.sum(total, axis=0, keepdims=True)
    upper = upper * share[:, :GROUP]
    lower = lower * share[:, GROUP:]
    attended_out[...] = jnp.concatenate([upper, lower], axis=0).astype(jnp.bfloat16).T
    grad = grad_turned[...].astype(jnp.float32)
    delta = jnp.concatenate(
        [
            jnp.sum(upper * grad[:HEAD_DIM], axis=0, keepdims=True),
            jnp.sum(lower * grad[HEAD_DIM:], axis=0, keepdims=True),
        ],
        axis=1,
    )

    def back(step, carry):
        upper, lower = carry
        part = strip[step] * share
        put(value_total, step, dot(part.astype(jnp.bfloat16), grad_pair))
        part = part * (dot(load(value_all, step), grad_pair, NT) - delta)
        low = part.astype(jnp.bfloat16)
        put(key_total, step, dot(low, query_pair))
        upper = upper + dot(load_turned(key_turned, step, 0), low[:, :GROUP])
        lower = lower + dot(load_turned(key_turned, step, 1), low[:, GROUP:])
        return upper, lower

    upper, lower = lax.fori_loop(0, steps, back, (blank, blank))
    own = rows(group)
    query_grad = jnp.concatenate([upper, lower], axis=0).T * HEAD_DIM ** (-0.5)
    query_out[...] = turn(query_grad, cosine_all[own, :], -sine_all[own, :]).astype(jnp.bfloat16)

    @pl.when(group == groups - 1)
    def _():
        key_grad = turn(key_total[...], cosine_all[...], -sine_all[...])
        key_out[...] = key_grad.astype(jnp.bfloat16)
        value_out[...] = value_total[...].astype(jnp.bfloat16)


def attention(order, projected, tables, pair, earlier=()):
    length, width = projected[0].shape
    groups = length // GROUP
    block = pl.BlockSpec((GROUP, PAIR), lambda group, order: (order[group], pair))
    turned_block = pl.BlockSpec((PAIR, GROUP), lambda group, order: (pair, order[group]))
    column = pl.BlockSpec((length, PAIR), lambda group, order: (0, pair))
    turned_column = pl.BlockSpec((PAIR, length), lambda group, order: (pair, 0))
    table = pl.BlockSpec((length, PAIR), lambda group, order: (0, 0))
    specs = [block, column, column, turned_column, turned_column, block, turned_block, table, table]
    return pl.pallas_call(
        attention_kernel,
        grid_spec=pltpu.PrefetchScalarGridSpec(
            num_scalar_prefetch=1,
            grid=(groups,),
            in_specs=specs + [pl.BlockSpec(memory_space=pl.ANY)] * len(earlier),
            out_specs=[block, block, column, column],
            scratch_shapes=[
                pltpu.VMEM((length, PAIR), jnp.float32),
                pltpu.VMEM((length, PAIR), jnp.float32),
                pltpu.VMEM((groups // 2, 2 * GROUP, 2 * GROUP), jnp.float32),
            ],
        ),
        out_shape=[jax.ShapeDtypeStruct((length, width), jnp.bfloat16)] * 4,
        input_output_aliases={1 + len(specs) + at: at for at in range(len(earlier))},
        compiler_params=params(60),
        cost_estimate=NO_COST,
        name=f"attention_{pair}",
    )(order, *projected, *tables, *earlier)


ROWS = 512


def chunk(place, which, size):
    return pl.ds(pl.multiple_of(place[which] * size, size), size)


def row_call(name, kernel, row_inputs, full_inputs, outputs, size=ROWS, turn=0, mebibytes=48):
    count = row_inputs[0].shape[0] // size
    rows = count * size

    def out(item):
        if len(item) == 4 and item[3] is None:
            shape, spec = item[:2], pl.BlockSpec(item[:2], lambda at: (0, 0))
        elif len(item) == 4:
            shape = ((item[3] - item[2]) * size, item[0])
            spec = pl.BlockSpec(
                (size, item[0]),
                lambda at: (jnp.clip(at, item[2], item[3] - 1) - item[2], 0),
            )
        elif len(item) == 3:
            shape = (item[0], rows)
            spec = pl.BlockSpec((item[0], size), lambda at: (0, at))
        else:
            shape = (rows, item[0])
            spec = pl.BlockSpec((size, item[0]), lambda at: (at, 0))
        kind = item[2] if len(item) == 4 and item[3] is None else item[1]
        return spec, jax.ShapeDtypeStruct(shape, kind)

    return pl.pallas_call(
        kernel,
        grid=(count,),
        in_specs=[
            pl.BlockSpec((size, item.shape[1]), lambda at: (lax.rem(at + turn, count), 0))
            for item in row_inputs
        ]
        + [pl.BlockSpec(item.shape, lambda at: (0, 0)) for item in full_inputs],
        out_specs=[out(item)[0] for item in outputs],
        out_shape=[out(item)[1] for item in outputs],
        compiler_params=params(mebibytes),
        cost_estimate=NO_COST,
        name=name,
    )(*row_inputs, *full_inputs)


def add_up(target, at, values):
    part = jnp.sum(values.astype(jnp.float32), axis=0, keepdims=True)

    @pl.when(pl.program_id(0) == 0)
    def _():
        target[at : at + 1, :] = part

    @pl.when(pl.program_id(0) > 0)
    def _():
        target[at : at + 1, :] += part


def project_kernel(normed, grads, cosine, sine, weight, bias, *refs):
    query, key, value, key_turned, value_turned, out_grads, grads_turned = refs
    width = weight.shape[1] // 4
    mixed = dot(normed[...], weight[:, : 3 * width]) + bias[...]
    parts = [mixed[:, which * width : (which + 1) * width] for which in range(3)]
    parts.append(dot(grads[...], weight[:, 3 * width :]))
    for pair in range(-(-width // PAIR)):
        here = slice(pair * PAIR, (pair + 1) * PAIR)
        items = [part[:, here] for part in parts]
        if width < PAIR:
            nothing = jnp.zeros((ROWS, PAIR - width), jnp.float32)
            items = [jnp.concatenate([item, nothing], axis=1) for item in items]
        turned = [turn(item, cosine[...], sine[...]) for item in items[:2]]
        low = turned[0].astype(jnp.bfloat16).astype(jnp.float32) * HEAD_DIM ** (-0.5)
        query[:, here] = low.astype(jnp.bfloat16)
        for target, target_turned, item in (
            (key, key_turned, turned[1]),
            (value, value_turned, items[2]),
            (out_grads, grads_turned, items[3]),
        ):
            low = item.astype(jnp.bfloat16)
            target[:, here] = low
            target_turned[here, :] = low.T


def hidden_kernel(normed, weight, bias, activated, slope):
    hidden = dot(normed[...], weight[...]) + bias[...]
    square = hidden * hidden
    bent = jnp.tanh(GELU_SLOPE * hidden * (1.0 + GELU_CUBE * square))
    half = 0.5 * (1.0 + bent)
    activated[...] = (hidden * half).astype(jnp.bfloat16)
    slope[...] = (
        half
        + 0.5 * GELU_SLOPE * hidden * (1.0 - bent * bent) * (1.0 + 3.0 * GELU_CUBE * square)
    ).astype(jnp.bfloat16)


def hidden_grad_kernel(grads, slope, weight, target, sums):
    low = (dot(grads[...], weight[...]) * slope[...].astype(jnp.float32)).astype(jnp.bfloat16)
    target[...] = low
    add_up(sums, 0, low)


def back_kernel(columns, start, summing, halves, *refs):
    lefts = refs[: len(columns)]
    weights, outs = refs[len(columns) + start : -1 - summing - halves], refs[-1 - summing - halves :]
    result = refs[len(columns)][...].astype(jnp.float32) if start else None
    for left, (which, here) in zip(lefts, columns):
        part = dot(left[:, : here.stop - here.start], weights[which][:, here], NT)
        result = part if result is None else result + part
    if halves:
        early = pl.program_id(0) < pl.num_programs(0) // 2

        @pl.when(early)
        def _():
            outs[0][...] = result.astype(jnp.bfloat16)

        @pl.when(jnp.logical_not(early))
        def _():
            outs[1][...] = result.astype(jnp.bfloat16)

    else:
        outs[0][...] = result.astype(jnp.bfloat16)
    if summing:
        for at, left in enumerate(lefts):
            add_up(outs[1], at, left[...])


def back(lefts, columns, weights, start=None, halves=False, summing=False):
    size = ROWS
    count = lefts[0].shape[0] // size
    starts = [] if start is None else [start]
    outputs = [(weights[0].shape[0], jnp.bfloat16)]
    if halves:
        outputs = [outputs[0] + (0, count // 2), outputs[0] + (count // 2, count)]
    if summing:
        outputs.append((len(lefts), lefts[0].shape[1], jnp.float32, None))
    got = row_call(
        "back",
        functools.partial(back_kernel, columns, len(starts), int(summing), int(halves)),
        lefts + starts,
        weights,
        outputs,
        size,
        count // 2 if halves else 0,
    )
    return got if summing or halves else got[0]


def grad_kernel(counts, width, turns, *refs):
    target = refs[-1]
    refs = list(refs[:-1])
    at = 0
    for count in counts:
        left = refs.pop(0)
        for _ in range(count):
            right = refs.pop(0)
            columns = min(width, right.shape[1])
            target[0, :, at : at + columns] = dot(
                left[...], right[:, :columns], (((0,), (0,)), ((), ()))
            ).astype(jnp.bfloat16)
            at += columns


def grad_pieces(products, turns, first, count, width, mebibytes=48):
    size = lax.axis_size(FSDP)
    specs, items, columns = [], [], 0
    for left, rights in products:
        rows = left.shape[1] // size
        specs.append(
            pl.BlockSpec((left.shape[0], rows), lambda at, turns: (0, turns[first + at]))
        )
        specs += [pl.BlockSpec(item.shape, lambda at, turns: (0, 0)) for item in rights]
        items += [left, *rights]
        columns += sum(min(width, item.shape[1]) for item in rights)
    return pl.pallas_call(
        functools.partial(grad_kernel, [len(rights) for _, rights in products], width),
        grid_spec=pltpu.PrefetchScalarGridSpec(
            num_scalar_prefetch=1,
            grid=(count,),
            in_specs=specs,
            out_specs=pl.BlockSpec((1, rows, columns), lambda at, turns: (at, 0, 0)),
        ),
        out_shape=jax.ShapeDtypeStruct((count, rows, columns), jnp.bfloat16),
        compiler_params=params(mebibytes),
        cost_estimate=NO_COST,
        name=f"grad_{first}",
    )(turns, *items)


def pointwise(name, function, scalars, inputs, outputs):
    def spec(item):
        if not isinstance(item, tuple):
            return pl.BlockSpec(item.shape, lambda at, n=item.ndim: (0,) * n)
        array, rows, index = item
        return pl.BlockSpec(
            (rows,) + array.shape[1:], lambda at, n=array.ndim, index=index: (index,) + (0,) * (n - 1)
        )

    def kernel(*refs):
        count = len(scalars) + len(inputs)
        for target, value in zip(refs[count:], function(*refs[:count])):
            target[...] = value.astype(target.dtype)

    return pl.pallas_call(
        kernel,
        grid=(1,),
        in_specs=[pl.BlockSpec(memory_space=pltpu.SMEM)] * len(scalars) + [spec(i) for i in inputs],
        out_specs=[pl.BlockSpec(shape, lambda at, n=len(shape): (0,) * n) for shape, _ in outputs],
        out_shape=[jax.ShapeDtypeStruct(shape, kind) for shape, kind in outputs],
        compiler_params=params(),
        cost_estimate=NO_COST,
        name=name,
    )(*scalars, *[item[0] if isinstance(item, tuple) else item for item in inputs])


def stack_kernel(parts, *refs):
    *sources, target, arrived = refs
    copies = [
        pltpu.make_async_copy(
            source.at[pl.ds(first, rows)], target.at[pl.ds(start, rows)], arrived.at[at]
        )
        for at, (source, (first, rows, start)) in enumerate(zip(sources, parts))
    ]
    for copy in copies:
        copy.start()
    for copy in copies:
        copy.wait()


def stack(parts, rows):
    array = parts[0][0]
    return pl.pallas_call(
        functools.partial(stack_kernel, [part[1:] for part in parts]),
        in_specs=[pl.BlockSpec(memory_space=pl.ANY)] * len(parts),
        out_specs=pl.BlockSpec(memory_space=pltpu.VMEM),
        out_shape=jax.ShapeDtypeStruct((rows, array.shape[1]), array.dtype),
        scratch_shapes=[pltpu.SemaphoreType.DMA((len(parts),))],
        compiler_params=params(),
        cost_estimate=NO_COST,
        name="stack",
    )(*[part[0] for part in parts])


def fill_kernel(starts, *refs):
    count = len(starts)
    sources, target = refs[:count], refs[count + 1]
    held, arrived, left = refs[count + 2 :]
    rows = [source.shape[0] for source in sources]
    slots = [pl.ds(sum(rows[:at]), rows[at]) for at in range(count)]
    inward = [
        pltpu.make_async_copy(source, held.at[slots[at]], arrived.at[at])
        for at, source in enumerate(sources)
    ]
    outward = [
        pltpu.make_async_copy(held.at[slots[at]], target.at[pl.ds(start, rows[at])], left.at[at])
        for at, start in enumerate(starts)
    ]
    for copy in inward:
        copy.start()
    for first, second in zip(inward, outward):
        first.wait()
        second.start()
    for copy in outward:
        copy.wait()


def fill(target, parts):
    anywhere = pl.BlockSpec(memory_space=pl.ANY)
    count = len(parts)
    rows = sum(array.shape[0] for array, _ in parts)
    return pl.pallas_call(
        functools.partial(fill_kernel, [start for _, start in parts]),
        in_specs=[anywhere] * (count + 1),
        out_specs=anywhere,
        out_shape=jax.ShapeDtypeStruct(target.shape, target.dtype),
        scratch_shapes=[
            pltpu.VMEM((rows, target.shape[1]), target.dtype),
            pltpu.SemaphoreType.DMA((count,)),
            pltpu.SemaphoreType.DMA((count,)),
        ],
        input_output_aliases={count: 0},
        compiler_params=params(),
        cost_estimate=NO_COST,
        name="fill",
    )(*[array for array, _ in parts], target)


def line_kernel(place, *refs):
    own, up_one, down_one, up_two, down_two, up_three, down_three, target, arrived = refs
    rows = own.shape[0]
    for where, sources in enumerate(
        (
            (own, down_one, down_two, down_three),
            (up_one, own, down_one, down_two),
            (up_two, up_one, own, down_one),
            (up_three, up_two, up_one, own),
        )
    ):

        @pl.when(place[0] == where)
        def _(sources=sources):
            copies = [
                pltpu.make_async_copy(source, target.at[pl.ds(at * rows, rows)], arrived.at[at])
                for at, source in enumerate(sources)
            ]
            for copy in copies:
                copy.start()
            for copy in copies:
                copy.wait()


def in_line(got):
    anywhere = pl.BlockSpec(memory_space=pl.ANY)
    rows, columns = got[0].shape
    return pl.pallas_call(
        line_kernel,
        in_specs=[pl.BlockSpec(memory_space=pltpu.SMEM)] + [anywhere] * len(got),
        out_specs=pl.BlockSpec(memory_space=pltpu.VMEM),
        out_shape=jax.ShapeDtypeStruct((4 * rows, columns), got[0].dtype),
        scratch_shapes=[pltpu.SemaphoreType.DMA((4,))],
        compiler_params=params(),
        cost_estimate=NO_COST,
        name="in_line",
    )(lax.axis_index(FSDP).astype(jnp.int32).reshape(1), *got)


def swap(values, axis, bit):
    size = lax.axis_size(axis)
    with jax.named_scope(f"{axis}_{bit}"):
        return lax.ppermute(values, axis, [(place, place ^ bit) for place in range(size)])


def total(values, axis, *between):
    between = list(between)
    bit = 1
    while bit < lax.axis_size(axis):
        values = values + swap(values, axis, bit)
        if between:
            values = hold(values, between.pop(0))
        bit *= 2
    return values


def move(values, pairs):
    with jax.named_scope("line"):
        return lax.ppermute(values, FSDP, pairs)


def spread_first(own):
    return [own, move(own, [(0, 1), (1, 2), (2, 3)]), move(own, [(1, 0), (2, 1), (3, 2)])]


def spread_second(got):
    return got + [move(got[1], [(1, 2), (2, 3)]), move(got[2], [(1, 0), (2, 1)])]


def spread_third(got):
    return got + [move(got[3], [(2, 3)]), move(got[4], [(1, 0)])]


def reduce_first(parts):
    return move(parts[0], [(0, 1), (3, 2)])


def square_first(own):
    return [own, swap(own, FSDP, 1), swap(own, FSDP, 2)]


def square_second(got):
    return got + [swap(got[2], FSDP, 1)]


def square_kernel(place, *refs):
    *sources, target, arrived = refs
    rows = sources[0].shape[0]
    copies = []
    for which, source in enumerate(sources):
        here = pl.ds(pl.multiple_of((place[0] ^ which) * rows, rows), rows)
        copies.append(pltpu.make_async_copy(source, target.at[here], arrived.at[which]))
    for copy in copies:
        copy.start()
    for copy in copies:
        copy.wait()


def in_square(got, place):
    rows, columns = got[0].shape
    return pl.pallas_call(
        square_kernel,
        in_specs=[pl.BlockSpec(memory_space=pltpu.SMEM)]
        + [pl.BlockSpec(memory_space=pl.ANY)] * len(got),
        out_specs=pl.BlockSpec(memory_space=pltpu.VMEM),
        out_shape=jax.ShapeDtypeStruct((len(got) * rows, columns), got[0].dtype),
        scratch_shapes=[pltpu.SemaphoreType.DMA((len(got),))],
        compiler_params=params(),
        cost_estimate=NO_COST,
        name="in_square",
    )(place, *got)


UP, DOWN = [(0, 1), (1, 2), (2, 3)], [(1, 0), (2, 1), (3, 2)]


def second_of(place, first, second, got):
    ends = (place[0] == 0) | (place[0] == 3)
    return jnp.where(ends, sum_of(second)[0], sum_of(first) + got)


def third_of(place, second, third, upward, downward):
    one, two = sum_of(second)[0], sum_of(third)[0]
    return (
        jnp.where(place[0] == 1, one, two) + sum_of(upward),
        jnp.where(place[0] == 2, one, two) + sum_of(downward),
    )


def reduce_second(sums, place):
    inputs = []
    for (first, rest), got in sums:
        inputs += [first, (rest, 1, 0), got]
    rows, columns = sums[0][0][0].shape

    def choose(place, *refs):
        sent = [
            second_of(place, first, second, sum_of(got))
            for first, second, got in zip(refs[::3], refs[1::3], refs[2::3])
        ]
        return [jnp.stack(sent)]

    shape = (len(sums), rows, columns)
    sent = pointwise("second", choose, [place], inputs, [(shape, jnp.bfloat16)])[0]
    sent = sent.reshape(-1, columns)
    return [move(sent, UP[:2]), move(sent, DOWN[1:])]


def reduce_third(parts, got, place, new=None):
    first, rest = parts
    rows, columns = first.shape
    shape = (1 if new is None else 2, rows, columns)

    def choose(place, second, third, upward, downward, *others):
        sent = third_of(place, second, third, upward, downward)
        if not others:
            return [item[None] for item in sent]
        first, second, got = others
        other = second_of(place, first, second, sum_of(got))
        return [jnp.stack([item, other]) for item in sent]

    inputs = [(rest, 1, 0), (rest, 1, 1), *got]
    if new is not None:
        inputs += [new[0][0], (new[0][1], 1, 0), new[1]]
    upward, downward = pointwise(
        "third", choose, [place], inputs, [(shape, jnp.bfloat16)] * 2
    )
    upward, downward = upward.reshape(-1, columns), downward.reshape(-1, columns)
    return [move(upward, UP), move(downward, DOWN)], upward


def reduce_last(parts, got, index=0):
    first, rest = parts
    return pointwise(
        "last",
        lambda last, *got: [sum_of(last)[0] + sum_of(*got)],
        [],
        [(rest, 1, 2)] + [(item, first.shape[0], index) for item in got],
        [(first.shape, jnp.bfloat16)],
    )[0]


def paired():
    return lax.axis_size(CTX) == 4 and lax.axis_size(TP) == 2


def cut(parts):
    return pointwise(
        "cut",
        lambda *refs: [ref[...] for ref in refs],
        [],
        parts,
        [((rows, array.shape[1]), array.dtype) for array, rows, _ in parts],
    )


def gather_first(own):
    if not paired():
        return [own]
    return [own, swap(own, TP, 1), swap(own, CTX, 2), swap(own, CTX, 1)]


def gather_second(got):
    if not paired():
        return got
    size = got[0].shape[0] // 2
    sent = cut([(got[1], size, 0), (got[2], size, 1)])
    corner = [swap(sent[0], CTX, 2), swap(sent[1], TP, 1)]
    return got + [swap(got[1], CTX, 1), swap(got[2], CTX, 1)] + corner


def gather_third(got):
    if not paired():
        size = got[0].shape[0] // 2
        return [
            lax.all_gather(item, (CTX, TP), axis=0, tiled=True)
            for item in (got[0][:size], got[0][size:])
        ]
    own, across, along, far_own, far_across, far_along, *corner = got
    size = corner[0].shape[0]
    half = size // 2
    results = []
    for which in range(2):
        sides = (own, across, along, None, far_own, far_across, far_along, None)
        parts = [
            (item, which * size, size, at * size)
            for at, item in enumerate(sides)
            if item is not None
        ]
        results.append(stack(parts, 8 * size))
    corner, results = lax.optimization_barrier((corner, results))
    sent = cut([(item, half, at) for item in corner for at in (0, 1)])
    for which in range(2):
        parts = [(corner[which], 3 * size)]
        for at in (0, 1):
            parts.append((swap(sent[2 * which + at], CTX, 1), 7 * size + at * half))
        results[which] = fill(results[which], parts)
    return results


def scatter_first(near, far):
    return [near, swap(far, CTX, 1) if paired() else far]


def sum_of(*refs):
    result = None
    for ref in refs:
        values = ref[...].astype(jnp.float32)
        result = values if result is None else result + values
    return result


def scatter_second(*all_got):
    if not paired():
        return list(all_got)
    size, columns = all_got[0][0].shape[0] // 4, all_got[0][0].shape[1]
    half = size // 2

    def corners(*refs):
        sums = [sum_of(*refs[at : at + 2]) for at in range(0, len(refs), 2)]
        return [
            jnp.concatenate([item[:half] for item in sums], axis=0),
            jnp.concatenate([item[half:] for item in sums], axis=0),
        ]

    sent = pointwise(
        "corners",
        corners,
        [],
        [(item, size, 3) for got in all_got for item in got],
        [((len(all_got) * half, columns), jnp.bfloat16)] * 2,
    )
    from_across, from_along = swap(sent[0], TP, 1), swap(sent[1], CTX, 2)
    return [got + [from_across, from_along] for got in all_got]


def scatter_third(*all_got):
    if not paired():
        return [
            [lax.psum_scatter(jnp.concatenate(got), (CTX, TP), scatter_dimension=0, tiled=True)]
            for got in all_got
        ]
    size, columns = all_got[0][0].shape[0] // 4, all_got[0][0].shape[1]
    half = size // 2

    def sides(*refs):
        acrosses, alongs = [], []
        for at in range(0, len(refs), 6):
            across, along = sum_of(*refs[at : at + 2]), sum_of(*refs[at + 2 : at + 4])
            from_across, from_along = refs[at + 4 : at + 6]
            acrosses += [across[:half], across[half:] + sum_of(from_along)]
            alongs += [along[:half] + sum_of(from_across), along[half:]]
        return [jnp.concatenate(acrosses, axis=0), jnp.concatenate(alongs, axis=0)]

    inputs = []
    for at, (near, far, from_across, from_along) in enumerate(all_got):
        inputs += [(near, size, 1), (far, size, 1), (near, size, 2), (far, size, 2)]
        inputs += [(from_across, half, at), (from_along, half, at)]
    across, along = pointwise(
        "sides", sides, [], inputs, [((len(all_got) * size, columns), jnp.bfloat16)] * 2
    )
    across, along = swap(across, TP, 1), swap(along, CTX, 2)
    return [[near, far, across, along] for near, far, *_ in all_got]


def addends(got, index):
    if not paired():
        return got
    size = got[0].shape[0] // 4
    return [(got[0], size, 0), (got[1], size, 0), (got[2], size, index), (got[3], size, index)]


def local_places(positions):
    if not paired():
        return positions
    devices = jnp.array([2 * along + near for near in (0, 1) for along in (0, 1) for _ in (0, 1)])
    blocks = (lax.axis_index(CTX) ^ devices) * 2 + (
        lax.axis_index(TP) ^ jnp.array([0, 1] * 4)
    )
    return positions.reshape(8, -1)[blocks].reshape(-1)


def hold(values, *after):
    return lax.optimization_barrier((values,) + after)[0]


def hold(values, *after):
    return lax.optimization_barrier((values,) + after)[0]


def tick(live):
    vars(live).update(lax.optimization_barrier(dict(vars(live))))


def small_call(name, kernel, place, items, shapes, kind):
    vmem = pl.BlockSpec(memory_space=pltpu.VMEM)
    return pl.pallas_call(
        kernel,
        in_specs=[pl.BlockSpec(memory_space=pltpu.SMEM)] + [vmem] * len(items),
        out_specs=[vmem] * len(shapes),
        out_shape=[jax.ShapeDtypeStruct(shape, kind) for shape in shapes],
        compiler_params=params(),
        cost_estimate=NO_COST,
        name=name,
    )(place, *items)


def small_call(name, kernel, items, shapes, kind, *places):
    vmem = pl.BlockSpec(memory_space=pltpu.VMEM)
    return pl.pallas_call(
        kernel,
        in_specs=[pl.BlockSpec(memory_space=pltpu.SMEM)] * len(places) + [vmem] * len(items),
        out_specs=[vmem] * len(shapes),
        out_shape=[jax.ShapeDtypeStruct(shape, kind) for shape in shapes],
        compiler_params=params(),
        cost_estimate=NO_COST,
        name=name,
    )(*places, *items)


def pieces(kind, *sources):
    parts = lax.axis_size(CTX)
    rows = sources[-1].shape[0 if kind == "up" else 1]
    width = sources[-1].shape[1 if kind == "up" else 0] // parts
    columns = 4 * width if kind == "attention" else width
    if width % PAIR:
        items = jnp.stack([*sources[0], sources[1].T]).reshape(4, rows, parts, width)
        return jnp.transpose(items, (2, 1, 0, 3)).reshape(parts, rows, columns)

    def kernel(*refs):
        *sources, target = refs
        for r in range(parts):
            here = slice(r * width, (r + 1) * width)
            if kind == "attention":
                for which in range(3):
                    target[r, :, which * width : (which + 1) * width] = sources[0][which, :, here]
                target[r, :, 3 * width :] = sources[1][here, :].T
            elif kind == "up":
                target[r] = sources[0][:, here]
            else:
                target[r] = sources[0][here, :].T

    return small_call("pieces", kernel, sources, [(parts, rows, columns)], sources[0].dtype)[0]


def near_pieces(kind, *sources):
    parts = lax.axis_size(CTX)
    place = lax.axis_index(CTX).astype(jnp.int32)
    sent = pieces(kind, *sources) if sources[-1].shape[0] // parts % PAIR else None
    if sent is not None:
        return [lax.dynamic_index_in_dim(sent, place ^ r, 0, False) for r in range(parts)]
    rows, width = sources[1].shape[1], sources[1].shape[0] // parts

    def kernel(place, qkv, out, *targets):
        for r, target in enumerate(targets):
            here = pl.ds(pl.multiple_of((place[0] ^ r) * width, width), width)
            for which in range(3):
                target[:, which * width : (which + 1) * width] = qkv[which, :, here]
            target[:, 3 * width :] = out[here, :].T

    return small_call(
        "pieces", kernel, sources, [(rows, 4 * width)] * parts, sources[0].dtype, place.reshape(1)
    )


def near_trade(sent):
    return [sent[0]] + [swap(sent[r], CTX, r) for r in range(1, len(sent))]


def laid(received):
    def kernel(place, *refs):
        *sources, target = refs
        for r, source in enumerate(sources):
            rows = source.shape[0]
            target[pl.ds(pl.multiple_of((place[0] ^ r) * rows, rows), rows), :] = source[...]

    rows, columns = received[0].shape
    place = lax.axis_index(CTX).astype(jnp.int32).reshape(1)
    shape = (len(received) * rows, columns)
    return small_call("laid", kernel, received, [shape], received[0].dtype, place)[0]


def trade(sent):
    return lax.all_to_all(sent, CTX, 0, 0, tiled=True)


def gather_rows_of(sent):
    got = trade(sent)
    return got.reshape(-1, got.shape[2])


def trade_back(summed):
    return trade(summed.reshape(lax.axis_size(CTX), -1, summed.shape[1]))


def last_beside(other, parts, got):
    first, rest = parts
    count = lax.axis_size(CTX)
    rows, columns = first.shape[0] // count, first.shape[1]

    def choose(other, last, *got):
        total = (sum_of(last)[0] + sum_of(*got)).reshape(count, rows, columns)
        return [jnp.concatenate([sum_of(other).reshape(count, rows, columns), total], axis=1)]

    return pointwise(
        "last",
        choose,
        [],
        [other, (rest, 1, 2)] + [(item, first.shape[0], 0) for item in got],
        [((count, 2 * rows, columns), jnp.bfloat16)],
    )[0]


def finish(received, kind, index=0, count=1):
    parts, rows, columns = received.shape
    rows //= count
    width = columns // 4 if kind == "attention" else columns
    if width % PAIR:
        items = received[:, index * rows : (index + 1) * rows].astype(jnp.float32)
        items = jnp.transpose(items.reshape(parts, rows, 4, width), (2, 1, 0, 3))
        items = items.reshape(4, rows, parts * width)
        return items[:3], items[3].T

    def kernel(source, *targets):
        for r in range(parts):
            here = slice(r * width, (r + 1) * width)
            values = source[r, index * rows : (index + 1) * rows].astype(jnp.float32)
            if kind == "attention":
                for which in range(3):
                    targets[0][which, :, here] = values[:, which * width : (which + 1) * width]
                targets[1][here, :] = values[:, 3 * width :].T
            elif kind == "up":
                targets[0][:, here] = values
            else:
                targets[0][here, :] = values.T

    shapes = {
        "attention": [(3, rows, parts * width), (parts * width, rows)],
        "up": [(rows, parts * width)],
        "down": [(parts * width, rows)],
    }[kind]
    return small_call("finish", kernel, [received], shapes, jnp.float32)


def unit_of(tokens):
    inputs = tokens.astype(jnp.float32)
    centered = inputs - jnp.mean(inputs, axis=-1, keepdims=True)
    inverse = lax.rsqrt(jnp.mean(centered * centered, axis=-1, keepdims=True) + EPSILON)
    return centered * inverse, inverse


def tokens_grad_of(tokens, cotangent, norm_gain, *refs):
    unit, inverse = unit_of(tokens[...])
    grads = cotangent[...].astype(jnp.float32)
    normed_grad = sum_of(*refs)
    unit_grad = normed_grad * norm_gain[...].astype(jnp.float32)
    tokens_grad = grads + inverse * (
        unit_grad
        - jnp.mean(unit_grad, axis=-1, keepdims=True)
        - unit * jnp.mean(unit_grad * unit, axis=-1, keepdims=True)
    )
    sums = [
        jnp.sum(item, axis=0, keepdims=True) for item in (normed_grad * unit, normed_grad, grads)
    ]
    return [tokens_grad, jnp.concatenate(sums, axis=0)]


def on_device(
    tokens,
    positions,
    cotangent,
    norm_gain,
    norm_bias,
    qkv_weight,
    qkv_bias,
    out_weight,
    out_bias,
    up_weight,
    up_bias,
    down_weight,
    down_bias,
):
    parts = lax.axis_size(CTX)
    part = lax.axis_index(CTX)
    width = qkv_weight.shape[2] // parts
    units = up_weight.shape[1] // parts

    unit_rows, _ = unit_of(tokens[0])
    normed_own = (unit_rows * norm_gain + norm_bias).astype(jnp.bfloat16)

    place = lax.axis_index(FSDP)
    turns = jnp.array(TURNS, jnp.int32)[place]
    place = place.astype(jnp.int32).reshape(1)

    def first_grad(columns, *products, mebibytes=48):
        return grad_pieces(products, turns, 0, 1, columns, mebibytes)[0]

    def later_grads(columns, *products):
        return [grad_pieces(products, turns, 1, 3, columns)]

    live = types.SimpleNamespace(
        attention=laid(
            near_trade(near_pieces("attention", jnp.swapaxes(qkv_weight, 0, 1), out_weight))
        ),
        rows=jnp.concatenate([normed_own, cotangent[0]], axis=0),
        tokens=tokens[0],
        cotangent=cotangent[0],
        weights=(up_weight, down_weight),
        positions=positions,
    )
    tick(live)
    live.attention = square_first(live.attention)
    live.rows = gather_first(live.rows)
    live.places = local_places(live.positions)
    live.turning = turning(live.places)
    live.down = pieces("down", live.weights[1])
    tick(live)
    live.attention = square_second(live.attention)
    live.normed, live.grads = gather_third(gather_second(live.rows))
    live.up = gather_rows_of(pieces("up", live.weights[0]))
    del live.rows
    tick(live)
    live.up = square_first(live.up)
    live.down = gather_rows_of(live.down)
    live.attention = in_square(live.attention, place)
    qkv_part = lax.dynamic_slice_in_dim(qkv_bias, part * width, width, 1).astype(jnp.float32)
    padded = width + -width % PAIR
    pairs = padded // PAIR
    projected = row_call(
        "project",
        project_kernel,
        [live.normed, live.grads, *live.turning],
        [live.attention, qkv_part.reshape(1, 3 * width)],
        [(padded, jnp.bfloat16)] * 3
        + [(padded, jnp.bfloat16, True)] * 2
        + [(padded, jnp.bfloat16), (padded, jnp.bfloat16, True)],
        mebibytes=60,
    )
    groups = live.places[::GROUP] // GROUP
    order = jnp.sum(
        jnp.where(
            groups[None, :] == jnp.arange(groups.shape[0])[:, None],
            jnp.arange(groups.shape[0])[None, :],
            0,
        ),
        axis=1,
    ).astype(jnp.int32)
    heads = ()
    for pair in range(pairs // 2):
        heads = attention(order, projected, live.turning, pair, heads)
    live.projected, live.order, live.heads = projected, order, heads
    tick(live)
    live.up = square_second(live.up)
    live.down = spread_first(live.down)
    heads = live.heads
    for pair in range(pairs // 2, pairs):
        heads = attention(live.order, live.projected, live.turning, pair, heads)
    live.heads = heads
    attended, *head_grads = live.heads
    head_products = ((live.normed, head_grads), (live.grads, [attended]))
    live.head_parts = [first_grad(width, *head_products, mebibytes=60)]
    tick(live)
    live.down = spread_second(live.down)
    live.head_sum = reduce_first(live.head_parts)
    attended, *head_grads = live.heads
    head_products = ((live.normed, head_grads), (live.grads, [attended]))
    live.up = in_square(live.up, place)
    own_bias = lax.dynamic_slice_in_dim(up_bias, part * units, units, 0).astype(jnp.float32)
    live.activated, live.slope = row_call(
        "hidden",
        hidden_kernel,
        [live.normed],
        [live.up, own_bias[None]],
        [(units, jnp.bfloat16), (units, jnp.bfloat16)],
    )
    live.head_parts = live.head_parts + later_grads(width, *head_products)
    tick(live)
    live.down = spread_third(live.down)
    live.head_sum = reduce_second([(live.head_parts, live.head_sum)], place)
    down_products = (live.grads, [live.activated])
    live.down_parts = [first_grad(units, down_products)] + later_grads(units, down_products)
    columns = [(0, slice(which * width, (which + 1) * width)) for which in range(4)]
    live.normed_part, live.qkv_sums = back(
        list(live.heads[1:]), columns[:3], [live.attention], summing=True
    )
    tick(live)
    live.head_sum, _ = reduce_third(live.head_parts, live.head_sum, place)
    live.down_sum = reduce_first(live.down_parts)
    live.down = in_line(live.down)
    live.hidden_grad, live.up_sums = row_call(
        "hidden_grad",
        hidden_grad_kernel,
        [live.grads, live.slope],
        [live.down],
        [(units, jnp.bfloat16), (1, units, jnp.float32, None)],
    )
    everything = (0, slice(0, units))
    live.branch = back(
        [live.activated, live.heads[0]],
        [everything, (1, columns[3][1])],
        [live.down, live.attention],
        halves=True,
    )
    tick(live)
    live.down_sum = reduce_second([(live.down_parts, live.down_sum)], place)
    up_products = (live.normed, [live.hidden_grad])
    live.up_parts = [first_grad(units, up_products)]
    live.up_sum = reduce_first(live.up_parts)
    far, near = live.branch
    got = hold(scatter_first(near, far), live.up_parts[0])
    (live.branch,) = scatter_third(*scatter_second(got))
    live.up_parts = live.up_parts + later_grads(units, up_products)
    live.normed_part = back(
        [live.hidden_grad], [everything], [live.up], live.normed_part, halves=True
    )
    tick(live)
    live.down_sum, sent = reduce_third(
        live.down_parts, live.down_sum, place, (live.up_parts, live.up_sum)
    )
    live.head_sum = reduce_last(live.head_parts, hold(live.head_sum, sent))
    far, near = live.normed_part
    (live.normed_part,) = scatter_third(*scatter_second(scatter_first(near, far)))
    live.sums = jnp.concatenate(
        [
            lax.dynamic_update_slice_in_dim(
                jnp.zeros(qkv_bias.shape, jnp.float32),
                live.qkv_sums[:, :width],
                part * width,
                1,
            ).reshape(-1),
            lax.dynamic_update_slice_in_dim(
                jnp.zeros(up_bias.shape, jnp.float32), live.up_sums[0], part * units, 0
            ),
        ]
    )
    tick(live)
    second = [(item, live.up_parts[0].shape[0], 1) for item in live.down_sum]
    live.up_sum, sent = reduce_third(live.up_parts, second, place)
    live.both = trade(last_beside(live.head_sum, live.down_parts, hold(live.down_sum, sent)))
    live.tokens_grad, norm_sums = pointwise(
        "tokens_grad",
        tokens_grad_of,
        [],
        [live.tokens, live.cotangent, norm_gain[None]] + addends(live.normed_part, 0),
        [(tokens.shape[1:], jnp.float32), ((3, D), jnp.float32)],
    )
    (live.layer_output,) = pointwise(
        "layer_output",
        lambda tokens, *refs: [sum_of(tokens, *refs)],
        [],
        [live.tokens, out_bias[None], down_bias[None]] + addends(live.branch, 0),
        [(tokens.shape[1:], jnp.bfloat16)],
    )
    norm_sums = total(norm_sums.reshape(-1), TP)
    live.sums = jnp.concatenate([live.sums, norm_sums])
    tick(live)
    up_sum = trade_back(reduce_last(live.up_parts, live.up_sum))
    (down_weight_grad,) = finish(live.both, "down", 1, 2)
    qkv_weight_grad, out_weight_grad = finish(live.both, "attention", 0, 2)
    sums = total(
        live.sums, FSDP, down_weight_grad, (qkv_weight_grad, out_weight_grad)
    )
    sums = total(sums, CTX)
    (up_weight_grad,) = finish(up_sum, "up")
    bias_sums = sums[: -3 * D]
    norm_sums = sums[-3 * D :].reshape(3, D)
    tokens_grad, layer_output = live.tokens_grad, live.layer_output

    return (
        layer_output[None],
        tokens_grad[None],
        norm_sums[0],
        norm_sums[1],
        jnp.swapaxes(qkv_weight_grad, 0, 1),
        bias_sums[: qkv_bias.size].reshape(qkv_bias.shape),
        out_weight_grad,
        norm_sums[2],
        up_weight_grad,
        bias_sums[qkv_bias.size :],
        down_weight_grad,
        norm_sums[2],
    )


def solution(mesh):
    rows = P(FSDP, (CTX, TP), None)
    placed = (
        rows,
        P(),
        rows,
        P(),
        P(),
        P((FSDP, CTX), None, TP),
        P(None, TP),
        P(TP, (FSDP, CTX)),
        P(),
        P((FSDP, CTX), TP),
        P(TP),
        P(TP, (FSDP, CTX)),
        P(),
    )
    return jax.shard_map(
        on_device,
        mesh=mesh,
        in_specs=placed,
        out_specs=(
            rows,
            rows,
            P(),
            P(),
            P((FSDP, CTX), None, TP),
            P(None, TP),
            P(TP, (FSDP, CTX)),
            P(),
            P((FSDP, CTX), TP),
            P(TP),
            P(TP, (FSDP, CTX)),
            P(),
        ),
        check_vma=False,
    )
```
